32 devices in a mesh: grp: 4 (over y, x), pen: 8 (over z, core).
Axes of the slice: x: 2, y: 2, z: 4, core: 2. Of those that a mesh axis runs over, the one named last changes fastest.
Arguments:
- flow_fields: float32 [4, 4, 1536, 1536], P(None, 'grp', 'pen'), may hold values from -6 to 6
- marker_cells: int32 [4, 8, 1024, 8], P('grp', 'pen'), may hold values from 0 to 294911
- marker_weights: float32 [4, 8, 1024, 8], P('grp', 'pen'), may hold values from 0.05 to 0.3
- solid_blocks: int32 [4, 1536, 12], P('grp', 'pen'), may hold values 0 or 1
Outputs:
- velocity_next: float32 [3, 4, 1536, 1536], P(None, 'grp', 'pen')
- poisson_source: float32 [4, 1536, 1536], P(None, 'pen', 'grp')
The draws below stay inside these ranges and needn't reach their ends.
Inputs may be any that keep to these rules, and one draw needn't show every extreme that they name: `marker_cells`: each entry numbers a cell of the device's own home block of 294912 cells, first dimension slowest, third fastest.
All inputs are finite; a program needn't handle non-finite values. No bound on the sum of `solid_blocks` on one device may be relied on, other than what follows from the above.
Results may differ from the reference program's by a relative error of at most 0.0003.
Values sent between devices are 32-bit elements; how exact they have to be, the bound alone decides.
No kernel may reach another device: no remote copies, remote signals or barrier semaphores. Data moves between devices by JAX's collectives and lax.ppermute only.
A program may use at most 128 MiB of HBM per device.

```python
import math
import jax
import jax.numpy as jnp
from jax import lax

NY = 1536
NZ = 1536
CX = 1
MK = 1024
STEN = 8
ZB = 128
NX = 4
CELLS = 294912
N_GRP = 4
N_PEN = 8


def plant(entries, rng, smallest, top_value):
    longest = entries.shape.index(max(entries.shape))
    spots = []
    for shift in (0, 1):
        where = [jax.random.randint(jax.random.fold_in(rng, axis), (), 0, length) for axis, length in enumerate(entries.shape)]
        where[longest] = (where[longest] + shift) % entries.shape[longest]
        spots.append(tuple(where))
    return entries.at[spots[0]].set(smallest).at[spots[1]].set(top_value)


def block_scale(own_key, shape, split, least, largest):
    level, own = 1.0, jax.random.fold_in(own_key, 6)
    for position, shards_of in split:
        steps = jnp.exp(jax.random.uniform(jax.random.fold_in(own, position), (shards_of,), jnp.float32, least / len(split), largest / len(split)))
        level = level * jnp.repeat(steps, shape[position] // shards_of).reshape([-1 if axis == position else 1 for axis in range(len(shape))])
    return level


def bell_draw(rng, extent, scale, limit, split=(), kind=jnp.bfloat16):
    result = scale * jax.random.normal(rng, extent, jnp.float32)
    if split:
        result = result * block_scale(rng, extent, split, -0.22, 0.18)
    return jnp.clip(result, -limit, limit).astype(kind)


def setup_inputs(seed: int = 0) -> dict:
    key_of = jax.random.split(jax.random.key(seed), 5)
    return {
        "flow_fields": bell_draw(key_of[0], (4, NX, NY, NZ), 1.0, 6.0, ((1, 4), (2, 8)), jnp.float32),
        "marker_cells": plant(jax.random.randint(key_of[1], (N_GRP, N_PEN, MK, STEN), 0, CELLS), jax.random.fold_in(key_of[1], 1), 0, CELLS - 1).astype(jnp.int32),
        "marker_weights": jnp.clip(0.05 + 0.25 * jax.random.uniform(key_of[2], (N_GRP, N_PEN, MK, STEN), jnp.float32) ** block_scale(key_of[2], (N_GRP, N_PEN, MK, STEN), ((0, 4), (1, 8)), -0.2, 0.2), 0.05, 0.3),
        "solid_blocks": plant((jax.random.randint(key_of[3], (NX, NY, NZ // ZB), 0, 8) < 1).astype(jnp.int32), jax.random.fold_in(key_of[3], 1), 0, 1),
    }


def compact(line_data):
    length = line_data.shape[0]
    padded = jnp.pad(line_data, ((2, 2), (0, 0)))
    source = 14.0 / 9.0 * 0.5 * (padded[3:-1] - padded[1:-3]) + 1.0 / 9.0 * 0.25 * (padded[4:] - padded[:-4])
    lower_band = jnp.full((length,), 1.0 / 3.0, dtype=line_data.dtype).at[0].set(0.0)
    upper_band = jnp.full((length,), 1.0 / 3.0, dtype=line_data.dtype).at[length - 1].set(0.0)
    middle_band = jnp.ones((length,), dtype=line_data.dtype)
    return lax.linalg.tridiagonal_solve(lower_band, middle_band, upper_band, source)

def spectral(field, axis):
    length = field.shape[axis]
    spectrum = jnp.fft.rfft(field, axis=axis)
    mode_index = jnp.arange(length // 2 + 1).astype(field.dtype)
    wavenumber = jnp.where(mode_index < length // 2, 2.0 * math.pi / length * mode_index, 0.0).astype(field.dtype)
    shape_list = [1] * field.ndim
    shape_list[axis] = length // 2 + 1
    factor = wavenumber.reshape(shape_list)
    derived = jnp.fft.irfft(spectrum * (1j * factor), n=length, axis=axis)
    return derived.astype(field.dtype)

def along_axis(field, axis):
    if axis == 0:
        shaped = field.shape
        return compact(field.reshape(shaped[0], -1)).reshape(shaped)
    return spectral(field, axis)

def reference(flow_fields, marker_cells, marker_weights, solid_blocks):
    velocity = flow_fields[:3]
    pressure = flow_fields[3]
    tendency = [jnp.zeros_like(pressure) for _ in range(3)]
    divergence = jnp.zeros_like(pressure)
    for direction in range(3):
        for component in range(3):
            slope = along_axis(velocity[component], direction)
            tendency[component] = tendency[component] - velocity[direction] * slope
            if component == direction:
                divergence = divergence + slope
        tendency[direction] = tendency[direction] - along_axis(pressure, direction)
    provisional = velocity + 0.1 * jnp.stack(tendency)
    cyl = NY // N_PEN
    blocks = N_GRP * N_PEN
    blocked = provisional.reshape(3, N_GRP, CX, N_PEN, cyl, NZ).transpose(0, 1, 3, 2, 4, 5).reshape(3, blocks, CELLS)
    cells_index = marker_cells.reshape(blocks, MK * STEN).astype(jnp.int32)
    weights = marker_weights.reshape(blocks, MK, STEN)
    gathered = jnp.take_along_axis(blocked, cells_index[None], axis=2).reshape(3, blocks, MK, STEN)
    sampled = jnp.sum(gathered * weights[None], axis=3)
    spread = (sampled[..., None] * weights[None]).reshape(3, blocks * MK * STEN)
    offsets = (jnp.arange(blocks, dtype=jnp.int32) * CELLS)[:, None]
    global_index = (cells_index + offsets).reshape(-1)
    correction = jnp.zeros((3, blocks * CELLS), provisional.dtype).at[:, global_index].add(spread)
    correction = correction.reshape(3, N_GRP, N_PEN, CX, cyl, NZ).transpose(0, 1, 3, 2, 4, 5).reshape(3, NX, NY, NZ)
    solid = jnp.repeat(solid_blocks, ZB, axis=2).astype(provisional.dtype)
    velocity_next = (1.0 - solid)[None] * (provisional - correction)
    return (velocity_next, divergence)
```

```python
import functools
import math

import jax
import jax.numpy as jnp
import ml_dtypes
import numpy as np
from jax import lax
from jax.experimental import pallas as pl
from jax.experimental.pallas import tpu as pltpu
from jax.sharding import PartitionSpec as P

LANES = 128
CHUNK = 256
FIELD_ORDER = (1, 3, 0, 2)
ANY = pl.BlockSpec(memory_space=pl.ANY)
SMEM = pl.BlockSpec(memory_space=pltpu.SMEM)
VMEM = pl.BlockSpec(memory_space=pltpu.VMEM)
BF = jnp.bfloat16
F32 = jnp.float32


def split_table(length):
    half = length // 2
    lag = np.arange(length)
    row = np.zeros(length)
    row[1:] = math.pi / length * (1 - 2 * (lag[1:] % 2)) / np.tan(math.pi * lag[1:] / length)
    row[half] = 0.0
    offset = np.arange(half)[:, None] - np.arange(half)[None, :]
    same, other = row[offset % length], row[(offset + half) % length]
    table = np.stack([(same + other) / 2, (same - other) / 2])
    high = table.astype(ml_dtypes.bfloat16)
    low = (table - high.astype(np.float64)).astype(ml_dtypes.bfloat16)
    return high, low


def compact_matrix(length):
    eye = np.eye(length)
    off = lambda k: np.eye(length, k=k)
    left = eye + (off(1) + off(-1)) / 3
    right = 7 / 9 * (off(1) - off(-1)) + 1 / 36 * (off(2) - off(-2))
    return np.linalg.solve(left, right).astype(np.float32)


def two_terms(value):
    high = value.astype(BF)
    return high, (value - high.astype(F32)).astype(BF)


def dot(a, b):
    return jnp.dot(a, b, preferred_element_type=F32)


def dot_t(a, b):
    return lax.dot_general(a, b, (((1,), (1,)), ((), ())), preferred_element_type=F32)


def params(mib, **more):
    return pltpu.CompilerParams(vmem_limit_bytes=mib * 2**20, **more)


def cost(flops, moved):
    return pl.CostEstimate(flops=int(flops), bytes_accessed=int(moved), transcendentals=0)


class Plan:
    def __init__(self, pens, rows, depth):
        self.pens, self.rows, self.depth = pens, rows, depth
        self.tiles = depth // LANES
        self.pairs = len(FIELD_ORDER) * self.tiles
        self.rounds = -(-self.pairs // pens)
        first = min(-(-2 * self.tiles // pens), self.rounds)
        self.stages = [list(range(first))]
        if first < self.rounds:
            self.stages.append(list(range(first, self.rounds)))

    def place(self, round_, pen):
        pair = jnp.minimum(round_ * self.pens + pen, self.pairs - 1)
        slot, tile = pair // self.tiles, pair % self.tiles
        field = jnp.int32(FIELD_ORDER[0])
        for i, f in enumerate(FIELD_ORDER[1:], 1):
            field = jnp.where(slot == i, f, field)
        return field, pl.multiple_of(tile * LANES, LANES)


def run_copies(copies):
    for c in copies:
        c.start()
    for c in copies:
        c.wait()


def pack_lines(plan, rounds, me, flow):
    n = plan.pens

    def kernel(me_ref, flow_ref, *rest):
        outs, sems = rest[:-1], rest[-1]
        copies = []
        for s in range(1, n):
            pen = lax.rem(me_ref[0] + s, n)
            for k, r in enumerate(rounds):
                field, z = plan.place(r, pen)
                copies.append(pltpu.make_async_copy(
                    flow_ref.at[field, 0, :, pl.ds(z, LANES)], outs[s - 1].at[k], sems.at[len(copies)]))
        run_copies(copies)

    shape = jax.ShapeDtypeStruct((len(rounds), plan.rows, LANES), F32)
    size = 4 * len(rounds) * plan.rows * LANES * n
    return pl.pallas_call(
        kernel, out_shape=[shape] * (n - 1), in_specs=[SMEM, ANY], out_specs=[ANY] * (n - 1),
        scratch_shapes=[pltpu.SemaphoreType.DMA(((n - 1) * len(rounds),))],
        compiler_params=params(4), cost_estimate=cost(0, 2 * size), name="pack_lines",
    )(me, flow)


def line_slopes(plan, rounds, groups, me, flow, received, tables):
    n, rows = plan.pens, plan.rows
    length, half, count = n * rows, n * rows // 2, len(rounds)
    wide = count * LANES
    block = math.gcd(half, 256)

    def kernel(me_ref, flow_ref, high_ref, low_ref, *rest):
        ins = rest[: n - 1]
        outs = rest[n - 1 : n - 1 + n * len(groups)]
        lines, result, x_high, x_low, in_sems, out_sems = rest[n - 1 + n * len(groups) :]
        mine = me_ref[0]
        copies = []
        for s in range(1, n):
            pen = lax.rem(mine + n - s, n)
            at = pl.ds(pl.multiple_of(pen * rows, 8), rows)
            copies.append(pltpu.make_async_copy(ins[s - 1], lines.at[:, at, :], in_sems.at[len(copies)]))
        at = pl.ds(pl.multiple_of(mine * rows, 8), rows)
        for k, r in enumerate(rounds):
            field, z = plan.place(r, mine)
            copies.append(pltpu.make_async_copy(
                flow_ref.at[field, 0, :, pl.ds(z, LANES)], lines.at[k, at, :], in_sems.at[len(copies)]))
        run_copies(copies)

        @pl.loop(0, half // block)
        def _(b):
            upper = pl.ds(pl.multiple_of(b * block, block), block)
            lower = pl.ds(pl.multiple_of(b * block + half, block), block)
            for k in range(count):
                to = pl.ds(k * LANES, LANES)
                first, second = lines[k, upper, :], lines[k, lower, :]
                for part, value in enumerate((first + second, first - second)):
                    h, l = two_terms(value)
                    x_high[part, upper, to] = h
                    x_low[part, upper, to] = l

        @pl.loop(0, half // block)
        def _(b):
            upper = pl.ds(pl.multiple_of(b * block, block), block)
            lower = pl.ds(pl.multiple_of(b * block + half, block), block)
            parts = []
            for part in range(2):
                t_high, t_low = high_ref[part, upper, :], low_ref[part, upper, :]
                h, l = x_high[part], x_low[part]
                parts.append(dot(t_high, h) + (dot(t_high, l) + dot(t_low, h)))
            top, bottom = parts[0] + parts[1], parts[0] - parts[1]
            for k in range(count):
                result[k, upper, :] = top[:, k * LANES : (k + 1) * LANES]
                result[k, lower, :] = bottom[:, k * LANES : (k + 1) * LANES]

        copies = []
        for g, group in enumerate(groups):
            at_k = pl.ds(rounds.index(group[0]), len(group))
            for s in range(n):
                pen = lax.rem(mine + s, n)
                at = pl.ds(pl.multiple_of(pen * rows, 8), rows)
                copies.append(pltpu.make_async_copy(
                    result.at[at_k, at, :], outs[g * n + s], out_sems.at[len(copies)]))
        run_copies(copies)

    shapes = [jax.ShapeDtypeStruct((len(g), rows, LANES), F32) for g in groups for _ in range(n)]
    out = pl.pallas_call(
        kernel, out_shape=shapes,
        in_specs=[SMEM, ANY, VMEM, VMEM] + [ANY] * (n - 1), out_specs=[ANY] * len(shapes),
        scratch_shapes=[
            pltpu.VMEM((count, length, LANES), F32), pltpu.VMEM((count, length, LANES), F32),
            pltpu.VMEM((2, half, wide), BF), pltpu.VMEM((2, half, wide), BF),
            pltpu.SemaphoreType.DMA((n - 1 + count,)), pltpu.SemaphoreType.DMA((len(shapes),)),
        ],
        compiler_params=params(32),
        cost_estimate=cost(12 * half * half * wide, 8 * count * length * LANES + 8 * half * half),
        name="line_slopes",
    )(me, flow, *tables, *received)
    return [out[g * n : (g + 1) * n] for g in range(len(groups))]


def depth_terms(flow, tables):
    fields, _, rows, depth = flow.shape
    half = depth // 2
    step = math.gcd(rows, 48)

    def kernel(flow_ref, high_ref, low_ref, base_ref, slope_ref):
        value = flow_ref[:, 0].reshape(fields * step, depth)
        parts = []
        for part, x in enumerate((value[:, :half] + value[:, half:], value[:, :half] - value[:, half:])):
            h, l = two_terms(x)
            parts.append(dot(h, high_ref[part]) + (dot(l, high_ref[part]) + dot(h, low_ref[part])))
        minus = jnp.concatenate([parts[0] + parts[1], parts[0] - parts[1]], axis=1)
        rows_of = lambda f: minus[f * step : (f + 1) * step]
        speed = flow_ref[2, 0]
        for i in range(3):
            term = speed * rows_of(i)
            if i == 2:
                term = term + rows_of(3)
                slope_ref[...] = -rows_of(2)
            base_ref[i] = flow_ref[i, 0] + 0.1 * term

    whole = pl.BlockSpec((2, half, half), lambda r: (0, 0, 0), pipeline_mode=pl.Buffered(1))
    size = 4 * fields * rows * depth
    return pl.pallas_call(
        kernel, grid=(rows // step,),
        out_shape=[jax.ShapeDtypeStruct((3, rows, depth), F32), jax.ShapeDtypeStruct((rows, depth), F32)],
        in_specs=[pl.BlockSpec((fields, 1, step, depth), lambda r: (0, 0, r, 0)), whole, whole],
        out_specs=[pl.BlockSpec((3, step, depth), lambda r: (0, r, 0)), pl.BlockSpec((step, depth), lambda r: (r, 0))],
        compiler_params=params(40), cost_estimate=cost(12 * fields * rows * half * half, 2 * size + 8 * half * half),
        name="depth_terms",
    )(flow, *tables)


def slab_terms(coefficients, planes):
    n = len(planes)
    fields, rows, width = planes[0].shape
    step = math.gcd(rows, 48)

    def kernel(c_ref, *refs):
        ins, outs, slopes = refs[:n], refs[n : 2 * n], refs[2 * n]
        for to in range(n):
            speed = ins[(n - to) % n][0]
            for f in range(fields):
                slope = c_ref[to, 0] * ins[0][f]
                for s in range(1, n):
                    slope = slope + c_ref[to, s] * ins[s][f]
                if f == 0:
                    slopes[to] = slope
                if f < 3:
                    outs[to][f] = speed * slope
                else:
                    outs[to][0] += slope

    size = 4 * n * fields * rows * width
    out = pl.pallas_call(
        kernel, grid=(rows // step,),
        out_shape=[jax.ShapeDtypeStruct((3, rows, width), F32)] * n + [jax.ShapeDtypeStruct((n, rows, width), F32)],
        in_specs=[SMEM] + [pl.BlockSpec((fields, step, width), lambda r: (0, r, 0))] * n,
        out_specs=[pl.BlockSpec((3, step, width), lambda r: (0, r, 0))] * n
        + [pl.BlockSpec((n, step, width), lambda r: (0, r, 0))],
        compiler_params=params(32), cost_estimate=cost(n * size, 2 * size), name="slab_terms",
    )(coefficients, *planes)
    return out[:n], out[n]


def solve_layout(me, slopes, parts):
    n = len(parts)

    def kernel(me_ref, slopes_ref, *refs):
        out = refs[n]
        for s in range(n):
            out[lax.rem(me_ref[0] + n - s, n)] = refs[s][...] + slopes_ref[(n - s) % n]

    return pl.pallas_call(
        kernel, out_shape=jax.ShapeDtypeStruct(slopes.shape, F32), in_specs=[SMEM] + [VMEM] * (n + 1), out_specs=VMEM,
        compiler_params=params(16), cost_estimate=cost(slopes.size, 12 * slopes.size), name="solve_layout",
    )(me, slopes, *parts)


def marker_order(cells, weights, rows, depth):
    markers, stencil = weights.shape
    tiles, entries = depth // LANES, markers * stencil
    chunks = entries // CHUNK
    marker = lax.iota(jnp.int32, entries) // stencil
    flat = cells.reshape(-1)
    row, z = flat // depth, flat % depth
    place = (z // LANES * rows + row) * LANES + z % LANES
    weight = weights.reshape(-1)
    if rows * depth * markers < 2**31:
        key, weight = lax.sort((place * markers + marker, weight), num_keys=1)
        place, marker = key // markers, key % markers
    else:
        place, marker, weight = lax.sort((place, marker, weight), num_keys=1)
    shape = (chunks, 1, CHUNK)
    tile_row, lane = place // LANES, place % LANES
    tile = (tile_row // rows).reshape(chunks, CHUNK)
    first, last = tile[:, 0], tile[:, -1]
    end = jnp.cumsum(last - first + 1)
    start = end - (last - first + 1)
    pairs = chunks + tiles
    index = lax.iota(jnp.int32, pairs)
    chunk = jnp.minimum(jnp.sum((end[None, :] <= index[:, None]).astype(jnp.int32), axis=1), chunks - 1)
    pick = chunk[:, None] == lax.iota(jnp.int32, chunks)[None, :]
    at = jnp.sum(jnp.where(pick, (first - start)[None, :], 0), axis=1) + index
    at = jnp.where(index < end[-1], at, tiles)
    return chunk, at, tile_row.reshape(shape), lane.reshape(shape), marker.reshape(shape), weight.reshape(shape)


def home_step(plan, component, me, flow, base, across, slope_z, groups, order, solid, out):
    n, rows, depth, tiles = plan.pens, plan.rows, plan.depth, plan.tiles
    wanted = (1, 3) if component == 1 else (component,)
    slots = [FIELD_ORDER.index(f) for f in wanted]
    used = {r for slot in slots for r in range(slot * tiles // n, ((slot + 1) * tiles - 1) // n + 1)}
    low, span = min(used), max(used) - min(used) + 1
    sources = [(group, k, r, s) for group, _ in groups for k, r in enumerate(group) if r in used for s in range(n)]
    buffers = [b for group, bs in groups if used & set(group) for b in bs]
    starts, total = {}, 0
    for group, bs in groups:
        if used & set(group):
            starts[tuple(group)] = total
            total += n
    chunk_of, tile_of, *entries = order
    pairs = chunk_of.shape[0]
    chunks = entries[0].shape[0]
    markers = chunks * CHUNK // 8
    with_div = component == 1
    marker_rows = plan.marker_rows

    def kernel(me_ref, chunk_ref, tile_ref, flow_ref, base_ref, across_ref, slope_ref, row_ref, lane_ref, marker_ref,
               weight_ref, solid_ref, *rest):
        bufs = rest[:total]
        rest = rest[total:]
        if out is not None:
            rest = rest[1:]
        out_ref, rest = rest[0], rest[1:]
        if with_div:
            div_ref, rest = rest[0], rest[1:]
        slopes, speed, value, cross, third, prov, terms, sems = rest
        mine = me_ref[0]
        copies = []

        def copy(src, dst):
            copies.append(pltpu.make_async_copy(src, dst, sems.at[len(copies)]))

        copy(flow_ref.at[1, 0], speed)
        copy(base_ref.at[component], value)
        copy(across_ref.at[component], cross)
        if with_div:
            copy(slope_ref, third)
        for group, k, r, s in sources:
            pen = lax.rem(mine + n - s, n)
            copy(bufs[starts[tuple(group)] + s].at[k], slopes.at[(r - low) * n + pen])
        run_copies(copies)
        for t in range(tiles):
            z = slice(t * LANES, (t + 1) * LANES)
            own = slopes[slots[0] * tiles - low * n + t]
            term = cross[:, z] + speed[:, z] * own
            if with_div:
                term = term + slopes[slots[1] * tiles - low * n + t]
                third[:, z] = third[:, z] + own
            result = value[:, z] - 0.1 * term
            prov[t] = result
            h, l = two_terms(result)
            terms[t, :, :LANES] = h
            terms[t, :, LANES:] = l
        if with_div:
            divergence = pltpu.make_async_copy(third, div_ref, sems.at[0])
            divergence.start()

        row_at = lax.broadcasted_iota(jnp.int32, (rows, CHUNK), 0)
        lane_at = lax.broadcasted_iota(jnp.int32, (LANES, CHUNK), 0)
        marker_at = lax.broadcasted_iota(jnp.int32, (marker_rows, CHUNK), 0)
        one, zero = jnp.ones((), BF), jnp.zeros((), BF)

        def entry(i):
            c, t = chunk_ref[i], tile_ref[i]
            row = row_ref[c] - t * rows
            m = marker_ref[c]
            lanes = jnp.where(lane_at == lane_ref[c], 1.0, 0.0).astype(BF)
            low_part = jnp.where(lane_at == m % LANES, 1.0, 0.0).astype(BF)
            return c, jnp.minimum(t, tiles - 1), row_at == row, lanes, marker_at == m // LANES, low_part

        def gather(i, total):
            c, t, rows_hit, lanes, marker_hit, low_part = entry(i)
            both = dot(terms[t], jnp.concatenate([lanes, lanes], axis=0))
            found = jnp.sum(jnp.where(rows_hit, both, 0.0), axis=0, keepdims=True) * weight_ref[c]
            h, l = two_terms(jnp.where(marker_hit, found, 0.0))
            return total + (dot_t(h, low_part) + dot_t(l, low_part))

        sampled = lax.fori_loop(0, pairs, gather, jnp.zeros((marker_rows, LANES), F32), unroll=2)
        s_high, s_low = two_terms(sampled)

        def scatter(i, carry):
            c, t, rows_hit, lanes, marker_hit, low_part = entry(i)
            spread = dot(s_high, low_part) + dot(s_low, low_part)
            spread = jnp.sum(jnp.where(marker_hit, spread, 0.0), axis=0, keepdims=True) * weight_ref[c]
            h, l = two_terms(jnp.where(rows_hit, spread, 0.0))
            prov[t] -= dot_t(h, lanes) + dot_t(l, lanes)
            return carry

        lax.fori_loop(0, pairs, scatter, 0, unroll=2)
        fluid = 1.0 - solid_ref[...].astype(F32)
        for t in range(tiles):
            z = slice(t * LANES, (t + 1) * LANES)
            b = t * LANES // (depth // solid.shape[1])
            value[:, z] = fluid[:, b : b + 1] * prov[t]
        if with_div:
            divergence.wait()
        last = pltpu.make_async_copy(value, out_ref.at[component, 0], sems.at[1])
        last.start()
        last.wait()

    shapes = [jax.ShapeDtypeStruct((3, 1, rows, depth), F32)]
    if with_div:
        shapes.append(jax.ShapeDtypeStruct((rows, depth), F32))
    operands = [me, chunk_of, tile_of, flow, base, across, slope_z, *entries, solid, *buffers]
    specs = [SMEM] * 3 + [ANY] * 4 + [VMEM] * (len(entries) + 1) + [ANY] * total
    aliases = {}
    if out is not None:
        aliases = {len(operands): 0}
        operands.append(out)
        specs.append(ANY)
    block = pltpu.VMEM((rows, depth), F32)
    result = pl.pallas_call(
        kernel, out_shape=shapes, in_specs=specs, out_specs=[ANY] * len(shapes), input_output_aliases=aliases,
        scratch_shapes=[
            pltpu.VMEM((span * n, rows, LANES), F32), block, block, block, block,
            pltpu.VMEM((tiles, rows, LANES), F32), pltpu.VMEM((tiles, rows, 2 * LANES), BF),
            pltpu.SemaphoreType.DMA((4 + len(sources),)),
        ],
        compiler_params=params(32),
        cost_estimate=cost(pairs * 16 * rows * CHUNK * LANES, 20 * rows * depth), name="home_step",
    )(*operands)
    return result


def body(flow, marker_cells, marker_weights, solid_blocks, *, pens, grps):
    _, planes, rows, depth = flow.shape
    assert planes == 1 and depth % LANES == 0 and rows % 8 == 0
    width = depth // grps
    plan = Plan(pens, rows, depth)
    plan.marker_rows = -(-marker_weights.shape[2] // LANES // 8) * 8
    pen, grp = lax.axis_index("pen"), lax.axis_index("grp")
    pen_at, grp_at = jnp.full((1,), pen, jnp.int32), jnp.full((1,), grp, jnp.int32)
    tables = [jnp.asarray(t) for t in split_table(pens * rows)]
    tables_z = tables if depth == pens * rows else [jnp.asarray(t) for t in split_table(depth)]

    shifts = sorted(range(1, pens), key=lambda s: abs(2 * s - pens))

    def around(axis, n, s, value):
        return lax.ppermute(value, axis, [(i, (i + s) % n) for i in range(n)])

    def send_lines(blocks):
        got = {s: around("pen", pens, s, blocks[s - 1]) for s in shifts}
        return [got[s] for s in range(1, pens)]

    arrived = [send_lines(pack_lines(plan, rounds, pen_at, flow)) for rounds in plan.stages]
    fields = flow[:, 0]
    lines_x = [lax.dynamic_slice_in_dim(fields, lax.rem(grp + s, grps) * width, width, 2) for s in range(grps)]
    lines_x = [lines_x[0]] + [around("grp", grps, s, lines_x[s]) for s in range(1, grps)]
    base, slope_z = depth_terms(flow, tables_z)
    order = marker_order(marker_cells[0, 0], marker_weights[0, 0], rows, depth)
    matrix = jnp.asarray(compact_matrix(grps))
    at = lax.iota(jnp.int32, grps)
    relative = matrix[(grp + at) % grps][:, (grp - at) % grps]
    terms_x, slopes_x = slab_terms(relative, lines_x)
    across = jnp.zeros((3, rows, depth), F32)
    for s in range(grps):
        block = terms_x[s] if s == 0 else around("grp", grps, s, terms_x[s])
        across = lax.dynamic_update_slice_in_dim(across, block, lax.rem(grp + grps - s, grps) * width, 2)
    groups = []
    for number, rounds in enumerate(plan.stages):
        cut = [rounds] if number == 0 or len(rounds) == 1 else [rounds[:-1], rounds[-1:]]
        slopes = line_slopes(plan, rounds, cut, pen_at, flow, arrived[number], tables)
        for group, blocks in zip(cut, slopes):
            groups.append((group, [blocks[0]] + send_lines(blocks[1:])))

    step = functools.partial(home_step, plan, me=pen_at, flow=flow, base=base, across=across, slope_z=slope_z,
                             groups=groups, order=order, solid=solid_blocks[0])
    out, divergence = step(1, out=None)
    parts = [lax.dynamic_slice_in_dim(divergence, lax.rem(grp + s, grps) * width, width, 1) for s in range(grps)]
    parts = [parts[0]] + [around("grp", grps, s, parts[s]) for s in range(1, grps)]
    (out,) = step(0, out=out)
    poisson = solve_layout(grp_at, slopes_x, parts)
    (out,) = step(2, out=out)
    return out, poisson


def solution(mesh):
    return jax.shard_map(
        functools.partial(body, pens=mesh.shape["pen"], grps=mesh.shape["grp"]),
        mesh=mesh,
        in_specs=(
            P(None, "grp", "pen", None),
            P("grp", "pen", None, None),
            P("grp", "pen", None, None),
            P("grp", "pen", None),
        ),
        out_specs=(P(None, "grp", "pen", None), P(None, "pen", "grp")),
        check_vma=False,
    )
```

```python
import functools
import math

import jax
import jax.numpy as jnp
import ml_dtypes
import numpy as np
from jax import lax
from jax.experimental import pallas as pl
from jax.experimental.pallas import tpu as pltpu
from jax.sharding import PartitionSpec as P

LANES = 128
CHUNK = 256
CORES = 2
UNROLL = 11
FIELD_ORDER = (1, 3, 0, 2)
ANY = pl.BlockSpec(memory_space=pl.ANY)
HBM = pl.BlockSpec(memory_space=pltpu.HBM)
SMEM = pl.BlockSpec(memory_space=pltpu.SMEM)
VMEM = pl.BlockSpec(memory_space=pltpu.VMEM)
BF = jnp.bfloat16
F32 = jnp.float32


def split_table(length):
    half = length // 2
    lag = np.arange(length)
    row = np.zeros(length)
    row[1:] = math.pi / length * (1 - 2 * (lag[1:] % 2)) / np.tan(math.pi * lag[1:] / length)
    row[half] = 0.0
    offset = np.arange(half)[:, None] - np.arange(half)[None, :]
    same, other = row[offset % length], row[(offset + half) % length]
    table = np.stack([(same + other) / 2, (same - other) / 2])
    high = table.astype(ml_dtypes.bfloat16)
    low = (table - high.astype(np.float64)).astype(ml_dtypes.bfloat16)
    return high, low


def compact_matrix(length):
    eye = np.eye(length)
    off = lambda k: np.eye(length, k=k)
    left = eye + (off(1) + off(-1)) / 3
    right = 7 / 9 * (off(1) - off(-1)) + 1 / 36 * (off(2) - off(-2))
    return np.linalg.solve(left, right).astype(np.float32)


def two_terms(value):
    high = value.astype(BF)
    return high, (value - high.astype(F32)).astype(BF)


def dot(a, b):
    return jnp.dot(a, b, preferred_element_type=F32)


def dot_t(a, b):
    return lax.dot_general(a, b, (((1,), (1,)), ((), ())), preferred_element_type=F32)


def params():
    return pltpu.CompilerParams(vmem_limit_bytes=60 * 2**20)


def cost(flops, moved):
    return pl.CostEstimate(flops=int(flops) // 100, bytes_accessed=int(moved) // 100, transcendentals=0)


class Plan:
    def __init__(self, pens, rows, depth):
        self.pens, self.chips, self.rows, self.depth = pens, pens // CORES, rows, depth
        self.tiles = depth // LANES
        self.pairs = len(FIELD_ORDER) * self.tiles
        self.rounds = -(-self.pairs // self.chips)
        first = min(-(-2 * self.tiles // self.chips), self.rounds)
        self.stages = [list(range(first))]
        if first < self.rounds:
            self.stages.append(list(range(first, self.rounds)))

    def place(self, round_, chip):
        pair = jnp.minimum(round_ * self.chips + chip, self.pairs - 1)
        slot, tile = pair // self.tiles, pair % self.tiles
        field = jnp.int32(FIELD_ORDER[0])
        for i, f in enumerate(FIELD_ORDER[1:], 1):
            field = jnp.where(slot == i, f, field)
        return field, pl.multiple_of(tile * LANES, LANES)


def run_copies(copies):
    for c in copies:
        c.start()
    for c in copies:
        c.wait()


def pack_lines(plan, me, flow):
    n, stages = plan.chips, plan.stages
    fields, _, rows, depth = flow.shape

    def kernel(me_ref, flow_ref, *rest):
        outs, (held, in_sems, out_sems) = rest[:-3], rest[-3:]
        loads = [pltpu.make_async_copy(flow_ref.at[f, 0], held.at[f], in_sems.at[f]) for f in FIELD_ORDER]
        for c in loads:
            c.start()
        copies = []
        for i, rounds in enumerate(stages):
            last = min((rounds[-1] * n + n - 1) // plan.tiles, fields - 1)
            while len(loads) > fields - 1 - last:
                loads.pop(0).wait()
            for s in range(n):
                chip = lax.rem(me_ref[0] // CORES + s, n)
                for k, r in enumerate(rounds):
                    field, z = plan.place(r, chip)
                    c = pltpu.make_async_copy(held.at[field, :, pl.ds(z, LANES)], outs[i * n + s].at[k], out_sems.at[len(copies)])
                    c.start()
                    copies.append(c)
        for c in copies:
            c.wait()

    shapes = [jax.ShapeDtypeStruct((len(rounds), rows, LANES), F32) for rounds in stages for _ in range(n)]
    out = pl.pallas_call(
        kernel, out_shape=shapes, in_specs=[SMEM, HBM], out_specs=[HBM] * len(shapes),
        scratch_shapes=[pltpu.VMEM((fields, rows, depth), F32), pltpu.SemaphoreType.DMA((fields,)),
                        pltpu.SemaphoreType.DMA((n * plan.rounds,))],
        compiler_params=params(), cost_estimate=cost(0, 2 * flow.size), name="pack_lines",
    )(me, flow)
    return [out[i * n : (i + 1) * n] for i in range(len(stages))]


def line_slopes(plan, rounds, groups, me, received, other, tables):
    n, rows = plan.chips, plan.rows
    length, half, count = plan.pens * rows, plan.pens * rows // 2, len(rounds)
    wide = count * LANES
    block = math.gcd(half, 256)

    def kernel(me_ref, high_ref, low_ref, *rest):
        ins, others = rest[:n], rest[n : 2 * n]
        outs = rest[2 * n : 2 * n + n * len(groups)]
        lines, result, x_high, x_low, in_sems, out_sems = rest[2 * n + n * len(groups) :]
        chip, core = me_ref[0] // CORES, me_ref[0] % CORES
        copies = []
        for refs, c in ((ins, core), (others, 1 - core)):
            for s in range(n):
                pen = lax.rem(chip + n - s, n) * CORES + c
                at = pl.ds(pl.multiple_of(pen * rows, 8), rows)
                copies.append(pltpu.make_async_copy(refs[s], lines.at[:, at, :], in_sems.at[len(copies)]))
        run_copies(copies)

        @pl.loop(0, half // block)
        def _(b):
            upper = pl.ds(pl.multiple_of(b * block, block), block)
            lower = pl.ds(pl.multiple_of(b * block + half, block), block)
            for k in range(count):
                to = pl.ds(k * LANES, LANES)
                first, second = lines[k, upper, :], lines[k, lower, :]
                for part, value in enumerate((first + second, first - second)):
                    h, l = two_terms(value)
                    x_high[part, upper, to] = h
                    x_low[part, upper, to] = l

        for home in range(n // 2):
            at = pl.ds(pl.multiple_of((home * CORES + core) * rows, 16), rows)
            parts = []
            for part in range(2):
                t_high, t_low = high_ref[part, at, :], low_ref[part, at, :]
                h, l = x_high[part], x_low[part]
                parts.append(dot(t_high, h) + (dot(t_high, l) + dot(t_low, h)))
            top, bottom = parts[0] + parts[1], parts[0] - parts[1]
            for k in range(count):
                result[home, k] = top[:, k * LANES : (k + 1) * LANES]
                result[home + n // 2, k] = bottom[:, k * LANES : (k + 1) * LANES]

        copies = []
        for g, group in enumerate(groups):
            at_k = pl.ds(rounds.index(group[0]), len(group))
            for s in range(n):
                home = lax.rem(chip + s, n)
                copies.append(pltpu.make_async_copy(result.at[home, at_k], outs[g * n + s], out_sems.at[len(copies)]))
        run_copies(copies)

    shapes = [jax.ShapeDtypeStruct((len(g), rows, LANES), F32) for g in groups for _ in range(n)]
    out = pl.pallas_call(
        kernel, out_shape=shapes,
        in_specs=[SMEM, VMEM, VMEM] + [HBM] * (2 * n), out_specs=[ANY] * len(shapes),
        scratch_shapes=[
            pltpu.VMEM((count, length, LANES), F32), pltpu.VMEM((n, count, rows, LANES), F32),
            pltpu.VMEM((2, half, wide), BF), pltpu.VMEM((2, half, wide), BF),
            pltpu.SemaphoreType.DMA((2 * n,)), pltpu.SemaphoreType.DMA((len(shapes),)),
        ],
        compiler_params=params(),
        cost_estimate=cost(6 * half * half * wide, 6 * count * length * LANES + 8 * half * half),
        name="line_slopes",
    )(me, *tables, *received, *other)
    return [out[g * n : (g + 1) * n] for g in range(len(groups))]


def depth_terms(flow, tables):
    fields, _, rows, depth = flow.shape
    half = depth // 2
    step = math.gcd(rows, 48)

    def kernel(flow_ref, high_ref, low_ref, base_ref, slope_ref):
        value = flow_ref[:, 0].reshape(fields * step, depth)
        parts = []
        for part, x in enumerate((value[:, :half] + value[:, half:], value[:, :half] - value[:, half:])):
            h, l = two_terms(x)
            parts.append(dot(h, high_ref[part]) + (dot(l, high_ref[part]) + dot(h, low_ref[part])))
        minus = jnp.concatenate([parts[0] + parts[1], parts[0] - parts[1]], axis=1)
        rows_of = lambda f: minus[f * step : (f + 1) * step]
        speed = flow_ref[2, 0]
        for i in range(3):
            term = speed * rows_of(i)
            if i == 2:
                term = term + rows_of(3)
                slope_ref[...] = -rows_of(2)
            base_ref[i] = flow_ref[i, 0] + 0.1 * term

    whole = pl.BlockSpec((2, half, half), lambda r: (0, 0, 0), pipeline_mode=pl.Buffered(1))
    size = 4 * fields * rows * depth
    return pl.pallas_call(
        kernel, grid=(rows // step,),
        out_shape=[jax.ShapeDtypeStruct((3, rows, depth), F32), jax.ShapeDtypeStruct((rows, depth), F32)],
        in_specs=[pl.BlockSpec((fields, 1, step, depth), lambda r: (0, 0, r, 0)), whole, whole],
        out_specs=[pl.BlockSpec((3, step, depth), lambda r: (0, r, 0)), pl.BlockSpec((step, depth), lambda r: (r, 0))],
        compiler_params=params(), cost_estimate=cost(12 * fields * rows * half * half, 2 * size + 8 * half * half),
        name="depth_terms",
    )(flow, *tables)


def slab_terms(coefficients, planes):
    n, fields, rows, width = planes.shape
    step = math.gcd(rows, 48)

    def kernel(in_ref, out_ref, slope_ref):
        for i in range(n):
            for f in range(fields):
                slope = sum(float(coefficients[i, j]) * in_ref[j, f] for j in range(n))
                if f == 0:
                    slope_ref[i] = slope
                if f < 3:
                    out_ref[i, f] = in_ref[i, 0] * slope
                else:
                    out_ref[i, 0] += slope

    size = 4 * n * fields * rows * width
    block = lambda *lead: pl.BlockSpec((*lead, step, width), lambda r: (0,) * len(lead) + (r, 0))
    return pl.pallas_call(
        kernel, grid=(rows // step,),
        out_shape=[jax.ShapeDtypeStruct((n, 3, rows, width), F32), jax.ShapeDtypeStruct((n, rows, width), F32)],
        in_specs=[block(n, fields)], out_specs=[block(n, 3), block(n)],
        compiler_params=params(), cost_estimate=cost(n * size, 2 * size), name="slab_terms",
    )(planes)


def marker_order(cells, weights, rows, depth):
    markers, stencil = weights.shape
    tiles, entries = depth // LANES, markers * stencil
    chunks = entries // CHUNK
    marker = lax.iota(jnp.int32, entries) // stencil
    flat = cells.reshape(-1)
    row, z = flat // depth, flat % depth
    place = (z // LANES * rows + row) * LANES + z % LANES
    weight = weights.reshape(-1)
    if rows * depth * markers < 2**31:
        key, weight = lax.sort((place * markers + marker, weight), num_keys=1)
        place, marker = key // markers, key % markers
    else:
        place, marker, weight = lax.sort((place, marker, weight), num_keys=1)
    shape = (chunks, 1, CHUNK)
    tile_row, lane = place // LANES, place % LANES
    tile = (tile_row // rows).reshape(chunks, CHUNK)
    first, last = tile[:, 0], tile[:, -1]
    end = jnp.cumsum(last - first + 1)
    start = end - (last - first + 1)
    pairs = chunks + tiles
    index = lax.iota(jnp.int32, pairs)
    chunk = jnp.minimum(jnp.sum((end[None, :] <= index[:, None]).astype(jnp.int32), axis=1), chunks - 1)
    pick = chunk[:, None] == lax.iota(jnp.int32, chunks)[None, :]
    at = jnp.sum(jnp.where(pick, (first - start)[None, :], 0), axis=1) + index
    at = jnp.where(index < end[-1], at, tiles)
    return chunk, at, tile_row.reshape(shape), lane.reshape(shape), marker.reshape(shape), weight.reshape(shape)


def home_slopes(plan, slot, groups):
    n, tiles = plan.chips, plan.tiles
    low, high = slot * tiles // n, ((slot + 1) * tiles - 1) // n
    wanted, buffers = [], []
    for group, blocks in groups:
        if any(low <= r <= high for r in group):
            wanted += [(len(buffers) + s, k, r, s) for k, r in enumerate(group) if low <= r <= high for s in range(n)]
            buffers += blocks

    def copies(me, refs, slopes, sems, first):
        return [pltpu.make_async_copy(
            refs[b].at[k], slopes.at[(r - low) * n + lax.rem(me // CORES + n - s, n)], sems.at[first + i])
            for i, (b, k, r, s) in enumerate(wanted)]

    return buffers, (high - low + 1) * n, len(wanted), slot * tiles - low * n, copies


def home_divergence(plan, parts, me, slope_z, groups):
    rows, depth, tiles = plan.rows, plan.depth, plan.tiles
    buffers, span, count, skip, copies_of = home_slopes(plan, FIELD_ORDER.index(1), groups)

    def kernel(me_ref, slope_ref, *rest):
        refs, (out_ref, slopes, third, sems) = rest[: len(buffers)], rest[len(buffers) :]
        copies = copies_of(me_ref[0], refs, slopes, sems, 1)
        run_copies([pltpu.make_async_copy(slope_ref, third, sems.at[0])] + copies)
        for t in range(tiles):
            z = slice(t * LANES, (t + 1) * LANES)
            third[:, z] = third[:, z] + slopes[skip + t]
        width = depth // parts
        for g in range(parts):
            out_ref[g] = third[:, g * width : (g + 1) * width]

    return pl.pallas_call(
        kernel, out_shape=jax.ShapeDtypeStruct((parts, rows, depth // parts), F32),
        in_specs=[SMEM] + [HBM] * (1 + len(buffers)), out_specs=VMEM,
        scratch_shapes=[pltpu.VMEM((span, rows, LANES), F32), pltpu.VMEM((rows, depth), F32),
                        pltpu.SemaphoreType.DMA((1 + count,))],
        compiler_params=params(), cost_estimate=cost(0, 12 * rows * depth), name="home_divergence",
    )(me, slope_z, *buffers)


def home_step(plan, component, me, flow, base, across, groups, order, solid, out):
    rows, depth, tiles = plan.rows, plan.depth, plan.tiles
    wanted = (1, 3) if component == 1 else (component,)
    sources = [home_slopes(plan, FIELD_ORDER.index(f), groups) for f in wanted]
    buffers = [b for source in sources for b in source[0]]
    total = len(buffers)
    chunk_of, tile_of, *entries = order
    pairs = chunk_of.shape[0]
    chunks = entries[0].shape[0]
    marker_rows = plan.marker_rows

    def kernel(me_ref, chunk_ref, tile_ref, flow_ref, base_ref, across_ref, row_ref, lane_ref, marker_ref,
               weight_ref, solid_ref, *rest):
        bufs = rest[:total]
        rest = rest[total:]
        if out is not None:
            rest = rest[1:]
        out_ref, speed, value, cross, prov, terms, sems, *slopes = rest
        copies = [
            pltpu.make_async_copy(flow_ref.at[1, 0], speed, sems.at[0]),
            pltpu.make_async_copy(base_ref.at[component], value, sems.at[1]),
            pltpu.make_async_copy(across_ref.at[component], cross, sems.at[2]),
        ]
        used = 0
        for (held, _, count, _, copies_of), ref in zip(sources, slopes):
            copies += copies_of(me_ref[0], bufs[used : used + len(held)], ref, sems, len(copies))
            used += len(held)
        run_copies(copies)
        for t in range(tiles):
            z = slice(t * LANES, (t + 1) * LANES)
            term = cross[:, z] + speed[:, z] * slopes[0][sources[0][3] + t]
            if component == 1:
                term = term + slopes[1][sources[1][3] + t]
            result = value[:, z] - 0.1 * term
            prov[t] = result
            h, l = two_terms(result)
            terms[t, :, :LANES] = h
            terms[t, :, LANES:] = l

        row_at = lax.broadcasted_iota(jnp.int32, (rows, CHUNK), 0)
        lane_at = lax.broadcasted_iota(jnp.int32, (LANES, CHUNK), 0)
        marker_at = lax.broadcasted_iota(jnp.int32, (marker_rows, CHUNK), 0)
        one, zero = jnp.ones((), BF), jnp.zeros((), BF)

        def entry(i):
            c, t = chunk_ref[i], tile_ref[i]
            m = marker_ref[c]
            low_part = jnp.where(lane_at == m % LANES, 1.0, 0.0).astype(BF)
            return c, jnp.minimum(t, tiles - 1), row_at == row_ref[c] - t * rows, lane_at == lane_ref[c], marker_at == m // LANES, low_part

        def gather(i, total):
            c, t, rows_hit, lanes_hit, marker_hit, low_part = entry(i)
            lanes = jnp.where(lanes_hit, 1.0, 0.0).astype(BF)
            both = dot(terms[t], jnp.concatenate([lanes, lanes], axis=0))
            found = jnp.sum(jnp.where(rows_hit, both, 0.0), axis=0, keepdims=True) * weight_ref[c]
            h, l = two_terms(jnp.where(marker_hit, found, 0.0))
            return total + dot_t(jnp.concatenate([h, l], axis=0), low_part)

        sampled = lax.fori_loop(0, pairs, gather, jnp.zeros((2 * marker_rows, LANES), F32), unroll=UNROLL)
        sampled = jnp.concatenate(two_terms(sampled[:marker_rows] + sampled[marker_rows:]), axis=0)

        def scatter(i, carry):
            c, t, rows_hit, lanes_hit, marker_hit, low_part = entry(i)
            spread = dot(sampled, low_part)
            spread = spread[:marker_rows] + spread[marker_rows:]
            spread = jnp.sum(jnp.where(marker_hit, spread, 0.0), axis=0, keepdims=True) * weight_ref[c]
            h, l = two_terms(spread)
            value = [jnp.where(lanes_hit, x.astype(F32), 0.0).astype(BF) for x in (h, l)]
            both = dot_t(jnp.where(rows_hit, 1.0, 0.0).astype(BF), jnp.concatenate(value, axis=0))
            prov[t] -= both[:, :LANES] + both[:, LANES:]
            return carry

        lax.fori_loop(0, pairs, scatter, 0, unroll=UNROLL)
        fluid = 1.0 - solid_ref[...].astype(F32)
        for t in range(tiles):
            z = slice(t * LANES, (t + 1) * LANES)
            b = t * LANES // (depth // solid.shape[1])
            value[:, z] = fluid[:, b : b + 1] * prov[t]
        last = pltpu.make_async_copy(value, out_ref.at[component, 0], sems.at[0])
        last.start()
        last.wait()

    operands = [me, chunk_of, tile_of, flow, base, across, *entries, solid, *buffers]
    specs = [SMEM] * 3 + [HBM] * 3 + [VMEM] * (len(entries) + 1) + [HBM] * total
    aliases = {}
    if out is not None:
        aliases = {len(operands): 0}
        operands.append(out)
        specs.append(HBM)
    block = pltpu.VMEM((rows, depth), F32)
    return pl.pallas_call(
        kernel, out_shape=jax.ShapeDtypeStruct((3, 1, rows, depth), F32), in_specs=specs, out_specs=HBM,
        input_output_aliases=aliases,
        scratch_shapes=[
            block, block, block, pltpu.VMEM((tiles, rows, LANES), F32), pltpu.VMEM((tiles, rows, 2 * LANES), BF),
            pltpu.SemaphoreType.DMA((3 + sum(source[2] for source in sources),)),
            *[pltpu.VMEM((source[1], rows, LANES), F32) for source in sources],
        ],
        compiler_params=params(),
        cost_estimate=cost(pairs * 16 * rows * CHUNK * LANES, 20 * rows * depth), name="home_step",
    )(*operands)


def body(flow, marker_cells, marker_weights, solid_blocks, *, pens, grps):
    _, planes, rows, depth = flow.shape
    assert planes == 1 and depth % LANES == 0 and rows % 8 == 0
    width = depth // grps
    plan = Plan(pens, rows, depth)
    plan.marker_rows = -(-marker_weights.shape[2] // LANES // 8) * 8
    pen_at = jnp.full((1,), lax.axis_index("pen"), jnp.int32)
    tables = [jnp.asarray(t) for t in split_table(pens * rows)]
    tables_z = tables if depth == pens * rows else [jnp.asarray(t) for t in split_table(depth)]

    def after(value, *others):
        return lax.optimization_barrier((value, others))[0]

    chips = plan.chips
    shifts = sorted(range(1, chips), key=lambda s: abs(2 * s - chips))

    def send_lines(blocks):
        got = {0: blocks[0]}
        for s in shifts:
            got[s] = lax.ppermute(blocks[s], "pen", [(i, (i + CORES * s) % pens) for i in range(pens)])
        return [got[s] for s in range(chips)]

    def swap(blocks):
        def other(value):
            return lax.ppermute(value, "pen", [(i, i ^ 1) for i in range(pens)])

        joined = other(jnp.concatenate(blocks[1:], axis=0))
        return [other(blocks[0])] + jnp.split(joined, chips - 1, axis=0)

    def cut_depth(value):
        return jnp.moveaxis(value.reshape(*value.shape[:-1], grps, width), -2, 0)

    def exchange(value):
        return lax.all_to_all(value, "grp", 0, 0, tiled=True)

    def slopes_of(rounds, cut, lines):
        return line_slopes(plan, rounds, cut, pen_at, lines, swap(lines), tables)

    first, second = plan.stages
    middle = -(-len(second) // 2)
    cut = [second[:middle], second[middle:]] if len(second) > 1 else [second]
    together = lax.optimization_barrier

    packed = pack_lines(plan, pen_at, flow)
    lines = send_lines(packed[0])
    lines_x = exchange(cut_depth(after(flow, packed)[:, 0]))
    order = marker_order(*after((marker_cells[0, 0], marker_weights[0, 0]), packed), rows, depth)
    lines, order, packed = together((lines, order, packed))
    lines_2 = send_lines(packed[1])
    (slopes,) = slopes_of(first, [first], lines)
    terms_x, slopes_x = slab_terms(compact_matrix(grps), after(lines_x, slopes))
    across = exchange(terms_x)
    lines_2, slopes, slopes_x = together((lines_2, slopes, slopes_x))
    back = send_lines(slopes)
    slopes = slopes_of(second, cut, lines_2)
    base, slope_z = depth_terms(after(flow, slopes), tables_z)
    across = jnp.moveaxis(after(across, base), 0, 2).reshape(3, rows, depth)
    back, slopes, across, base, slope_z = together((back, slopes, across, base, slope_z))
    groups = [(first, back)]
    step = functools.partial(home_step, plan, me=pen_at, flow=flow, base=base, across=across, order=order, solid=solid_blocks[0])
    back = send_lines(slopes[0])
    poisson = exchange(home_divergence(plan, grps, pen_at, slope_z, groups))
    out = step(1, groups=groups, out=None)
    slopes, back, out, poisson = together((slopes, back, out, poisson))
    groups = groups + [(cut[0], back)]
    if len(cut) > 1:
        back = send_lines(slopes[1])
    out = step(0, groups=groups, out=out)
    if len(cut) > 1:
        back, out = together((back, out))
        groups = groups + [(cut[1], back)]
    out = step(2, groups=groups, out=out)
    return out, poisson + slopes_x


def solution(mesh):
    return jax.shard_map(
        functools.partial(body, pens=mesh.shape["pen"], grps=mesh.shape["grp"]),
        mesh=mesh,
        in_specs=(
            P(None, "grp", "pen", None),
            P("grp", "pen", None, None),
            P("grp", "pen", None, None),
            P("grp", "pen", None),
        ),
        out_specs=(P(None, "grp", "pen", None), P(None, "pen", "grp")),
        check_vma=False,
    )
```

```python
import functools
import math

import jax
import jax.numpy as jnp
import ml_dtypes
import numpy as np
from jax import lax
from jax.experimental import pallas as pl
from jax.experimental.pallas import tpu as pltpu
from jax.sharding import PartitionSpec as P

LANES = 128
CHUNK = 256
CORES = 2
UNROLL = 11
FIELD_ORDER = (1, 3, 0, 2)
ANY = pl.BlockSpec(memory_space=pl.ANY)
HBM = pl.BlockSpec(memory_space=pltpu.HBM)
SMEM = pl.BlockSpec(memory_space=pltpu.SMEM)
VMEM = pl.BlockSpec(memory_space=pltpu.VMEM)
BF = jnp.bfloat16
F32 = jnp.float32


def split_table(length):
    half = length // 2
    lag = np.arange(length)
    row = np.zeros(length)
    row[1:] = math.pi / length * (1 - 2 * (lag[1:] % 2)) / np.tan(math.pi * lag[1:] / length)
    row[half] = 0.0
    offset = np.arange(half)[:, None] - np.arange(half)[None, :]
    same, other = row[offset % length], row[(offset + half) % length]
    table = np.stack([(same + other) / 2, (same - other) / 2])
    high = table.astype(ml_dtypes.bfloat16)
    low = (table - high.astype(np.float64)).astype(ml_dtypes.bfloat16)
    return high, low


def compact_matrix(length):
    eye = np.eye(length)
    off = lambda k: np.eye(length, k=k)
    left = eye + (off(1) + off(-1)) / 3
    right = 7 / 9 * (off(1) - off(-1)) + 1 / 36 * (off(2) - off(-2))
    return np.linalg.solve(left, right).astype(np.float32)


def two_terms(value):
    high = value.astype(BF)
    return high, (value - high.astype(F32)).astype(BF)


def dot(a, b):
    return jnp.dot(a, b, preferred_element_type=F32)


def dot_t(a, b):
    return lax.dot_general(a, b, (((1,), (1,)), ((), ())), preferred_element_type=F32)


def params():
    return pltpu.CompilerParams(vmem_limit_bytes=60 * 2**20)


def cost(flops, moved, share=0.01):
    return pl.CostEstimate(flops=int(flops * share), bytes_accessed=int(moved * share), transcendentals=0)


class Plan:
    def __init__(self, pens, rows, depth):
        self.pens, self.chips, self.rows, self.depth = pens, pens // CORES, rows, depth
        self.tiles = depth // LANES
        self.pairs = len(FIELD_ORDER) * self.tiles
        self.rounds = -(-self.pairs // self.chips)
        first = min(-(-2 * self.tiles // self.chips), self.rounds)
        self.stages = [list(range(first))]
        if first < self.rounds:
            self.stages.append(list(range(first, self.rounds)))

    def place(self, round_, chip):
        pair = jnp.minimum(round_ * self.chips + chip, self.pairs - 1)
        slot, tile = pair // self.tiles, pair % self.tiles
        field = jnp.int32(FIELD_ORDER[0])
        for i, f in enumerate(FIELD_ORDER[1:], 1):
            field = jnp.where(slot == i, f, field)
        return field, pl.multiple_of(tile * LANES, LANES)


def run_copies(copies):
    for c in copies:
        c.start()
    for c in copies:
        c.wait()


def pack_lines(plan, rounds, me, flow):
    n = plan.chips
    fields, _, rows, depth = flow.shape
    used = FIELD_ORDER[rounds[0] * n // plan.tiles : min((rounds[-1] * n + n - 1) // plan.tiles, fields - 1) + 1]

    def kernel(me_ref, flow_ref, *rest):
        outs, (held, in_sems, out_sems) = rest[:-3], rest[-3:]
        run_copies([pltpu.make_async_copy(flow_ref.at[f, 0], held.at[f], in_sems.at[f]) for f in used])
        copies = []
        for s in range(n):
            chip = lax.rem(me_ref[0] // CORES + s, n)
            for k, r in enumerate(rounds):
                field, z = plan.place(r, chip)
                copies.append(pltpu.make_async_copy(
                    held.at[field, :, pl.ds(z, LANES)], outs[s].at[k], out_sems.at[len(copies)]))
        run_copies(copies)

    shape = jax.ShapeDtypeStruct((len(rounds), rows, LANES), F32)
    return pl.pallas_call(
        kernel, out_shape=[shape] * n, in_specs=[SMEM, HBM], out_specs=[HBM] * n,
        scratch_shapes=[pltpu.VMEM((fields, rows, depth), F32), pltpu.SemaphoreType.DMA((fields,)),
                        pltpu.SemaphoreType.DMA((n * len(rounds),))],
        compiler_params=params(), cost_estimate=cost(0, 2 * flow.size), name="pack_lines",
    )(me, flow)


def line_slopes(plan, rounds, groups, me, received, other, tables):
    n, rows = plan.chips, plan.rows
    length, half, count = plan.pens * rows, plan.pens * rows // 2, len(rounds)
    wide = count * LANES
    block = math.gcd(half, 256)

    def kernel(me_ref, high_ref, low_ref, *rest):
        ins, others = rest[:n], rest[n : 2 * n]
        outs = rest[2 * n : 2 * n + n * len(groups)]
        lines, result, x_high, x_low, in_sems, out_sems = rest[2 * n + n * len(groups) :]
        chip, core = me_ref[0] // CORES, me_ref[0] % CORES
        copies = []
        for refs, c in ((ins, core), (others, 1 - core)):
            for s in range(n):
                pen = lax.rem(chip + n - s, n) * CORES + c
                at = pl.ds(pl.multiple_of(pen * rows, 8), rows)
                copies.append(pltpu.make_async_copy(refs[s], lines.at[:, at, :], in_sems.at[len(copies)]))
        run_copies(copies)

        @pl.loop(0, half // block)
        def _(b):
            upper = pl.ds(pl.multiple_of(b * block, block), block)
            lower = pl.ds(pl.multiple_of(b * block + half, block), block)
            for k in range(count):
                to = pl.ds(k * LANES, LANES)
                first, second = lines[k, upper, :], lines[k, lower, :]
                for part, value in enumerate((first + second, first - second)):
                    h, l = two_terms(value)
                    x_high[part, upper, to] = h
                    x_low[part, upper, to] = l

        for home in range(n // 2):
            at = pl.ds(pl.multiple_of((home * CORES + core) * rows, 16), rows)
            parts = []
            for part in range(2):
                t_high, t_low = high_ref[part, at, :], low_ref[part, at, :]
                h, l = x_high[part], x_low[part]
                parts.append(dot(t_high, h) + (dot(t_high, l) + dot(t_low, h)))
            top, bottom = parts[0] + parts[1], parts[0] - parts[1]
            for k in range(count):
                result[home, k] = top[:, k * LANES : (k + 1) * LANES]
                result[home + n // 2, k] = bottom[:, k * LANES : (k + 1) * LANES]

        copies = []
        for g, group in enumerate(groups):
            at_k = pl.ds(rounds.index(group[0]), len(group))
            for s in range(n):
                home = lax.rem(chip + s, n)
                copies.append(pltpu.make_async_copy(result.at[home, at_k], outs[g * n + s], out_sems.at[len(copies)]))
        run_copies(copies)

    shapes = [jax.ShapeDtypeStruct((len(g), rows, LANES), F32) for g in groups for _ in range(n)]
    out = pl.pallas_call(
        kernel, out_shape=shapes,
        in_specs=[SMEM, VMEM, VMEM] + [HBM] * (2 * n), out_specs=[ANY] * len(shapes),
        scratch_shapes=[
            pltpu.VMEM((count, length, LANES), F32), pltpu.VMEM((n, count, rows, LANES), F32),
            pltpu.VMEM((2, half, wide), BF), pltpu.VMEM((2, half, wide), BF),
            pltpu.SemaphoreType.DMA((2 * n,)), pltpu.SemaphoreType.DMA((len(shapes),)),
        ],
        compiler_params=params(),
        cost_estimate=cost(6 * half * half * wide, 6 * count * length * LANES + 8 * half * half),
        name="line_slopes",
    )(me, *tables, *received, *other)
    return [out[g * n : (g + 1) * n] for g in range(len(groups))]


def depth_terms(flow, tables):
    fields, _, rows, depth = flow.shape
    half = depth // 2
    step = math.gcd(rows, 48)

    def kernel(flow_ref, high_ref, low_ref, base_ref, slope_ref):
        value = flow_ref[:, 0].reshape(fields * step, depth)
        parts = []
        for part, x in enumerate((value[:, :half] + value[:, half:], value[:, :half] - value[:, half:])):
            h, l = two_terms(x)
            parts.append(dot(h, high_ref[part]) + (dot(l, high_ref[part]) + dot(h, low_ref[part])))
        minus = jnp.concatenate([parts[0] + parts[1], parts[0] - parts[1]], axis=1)
        rows_of = lambda f: minus[f * step : (f + 1) * step]
        speed = flow_ref[2, 0]
        for i in range(3):
            term = speed * rows_of(i)
            if i == 2:
                term = term + rows_of(3)
                slope_ref[...] = -rows_of(2)
            base_ref[i] = flow_ref[i, 0] + 0.1 * term

    whole = pl.BlockSpec((2, half, half), lambda r: (0, 0, 0), pipeline_mode=pl.Buffered(1))
    size = 4 * fields * rows * depth
    return pl.pallas_call(
        kernel, grid=(rows // step,),
        out_shape=[jax.ShapeDtypeStruct((3, rows, depth), F32), jax.ShapeDtypeStruct((rows, depth), F32)],
        in_specs=[pl.BlockSpec((fields, 1, step, depth), lambda r: (0, 0, r, 0)), whole, whole],
        out_specs=[pl.BlockSpec((3, step, depth), lambda r: (0, r, 0)), pl.BlockSpec((step, depth), lambda r: (r, 0))],
        compiler_params=params(), cost_estimate=cost(12 * fields * rows * half * half, 2 * size + 8 * half * half),
        name="depth_terms",
    )(flow, *tables)


def slab_terms(coefficients, planes):
    n, fields, rows, width = planes.shape
    step = math.gcd(rows, 48)

    def kernel(in_ref, out_ref, slope_ref):
        for i in range(n):
            for f in range(fields):
                slope = sum(float(coefficients[i, j]) * in_ref[j, f] for j in range(n))
                if f == 0:
                    slope_ref[i] = slope
                if f < 3:
                    out_ref[i, f] = in_ref[i, 0] * slope
                else:
                    out_ref[i, 0] += slope

    size = 4 * n * fields * rows * width
    block = lambda *lead: pl.BlockSpec((*lead, step, width), lambda r: (0,) * len(lead) + (r, 0))
    return pl.pallas_call(
        kernel, grid=(rows // step,),
        out_shape=[jax.ShapeDtypeStruct((n, 3, rows, width), F32), jax.ShapeDtypeStruct((n, rows, width), F32)],
        in_specs=[block(n, fields)], out_specs=[block(n, 3), block(n)],
        compiler_params=params(), cost_estimate=cost(n * size, 2 * size), name="slab_terms",
    )(planes)


def marker_order(cells, weights, rows, depth):
    markers, stencil = weights.shape
    tiles, entries = depth // LANES, markers * stencil
    chunks = entries // CHUNK
    marker = lax.iota(jnp.int32, entries) // stencil
    flat = cells.reshape(-1)
    row, z = flat // depth, flat % depth
    place = (z // LANES * rows + row) * LANES + z % LANES
    weight = weights.reshape(-1)
    if rows * depth * markers < 2**31:
        key, weight = lax.sort((place * markers + marker, weight), num_keys=1)
        place, marker = key // markers, key % markers
    else:
        place, marker, weight = lax.sort((place, marker, weight), num_keys=1)
    shape = (chunks, 1, CHUNK)
    tile_row, lane = place // LANES, place % LANES
    tile = (tile_row // rows).reshape(chunks, CHUNK)
    first, last = tile[:, 0], tile[:, -1]
    end = jnp.cumsum(last - first + 1)
    start = end - (last - first + 1)
    pairs = chunks + tiles
    index = lax.iota(jnp.int32, pairs)
    chunk = jnp.minimum(jnp.sum((end[None, :] <= index[:, None]).astype(jnp.int32), axis=1), chunks - 1)
    pick = chunk[:, None] == lax.iota(jnp.int32, chunks)[None, :]
    at = jnp.sum(jnp.where(pick, (first - start)[None, :], 0), axis=1) + index
    at = jnp.where(index < end[-1], at, tiles)
    return chunk, at, tile_row.reshape(shape), lane.reshape(shape), marker.reshape(shape), weight.reshape(shape)


def home_slopes(plan, slot, groups):
    n, tiles = plan.chips, plan.tiles
    low, high = slot * tiles // n, ((slot + 1) * tiles - 1) // n
    wanted, buffers = [], []
    for group, blocks in groups:
        if any(low <= r <= high for r in group):
            wanted += [(len(buffers) + s, k, r, s) for k, r in enumerate(group) if low <= r <= high for s in range(n)]
            buffers += blocks

    def copies(me, refs, slopes, sems, first):
        return [pltpu.make_async_copy(
            refs[b].at[k], slopes.at[(r - low) * n + lax.rem(me // CORES + n - s, n)], sems.at[first + i])
            for i, (b, k, r, s) in enumerate(wanted)]

    return buffers, (high - low + 1) * n, len(wanted), slot * tiles - low * n, copies


def home_divergence(plan, parts, me, slope_z, groups):
    rows, depth, tiles = plan.rows, plan.depth, plan.tiles
    buffers, span, count, skip, copies_of = home_slopes(plan, FIELD_ORDER.index(1), groups)

    def kernel(me_ref, slope_ref, *rest):
        refs, (out_ref, slopes, third, sems) = rest[: len(buffers)], rest[len(buffers) :]
        copies = copies_of(me_ref[0], refs, slopes, sems, 1)
        run_copies([pltpu.make_async_copy(slope_ref, third, sems.at[0])] + copies)
        for t in range(tiles):
            z = slice(t * LANES, (t + 1) * LANES)
            third[:, z] = third[:, z] + slopes[skip + t]
        width = depth // parts
        for g in range(parts):
            out_ref[g] = third[:, g * width : (g + 1) * width]

    return pl.pallas_call(
        kernel, out_shape=jax.ShapeDtypeStruct((parts, rows, depth // parts), F32),
        in_specs=[SMEM] + [HBM] * (1 + len(buffers)), out_specs=VMEM,
        scratch_shapes=[pltpu.VMEM((span, rows, LANES), F32), pltpu.VMEM((rows, depth), F32),
                        pltpu.SemaphoreType.DMA((1 + count,))],
        compiler_params=params(), cost_estimate=cost(0, 12 * rows * depth), name="home_divergence",
    )(me, slope_z, *buffers)


def home_step(plan, component, me, flow, base, groups, order, solid, out, share=0.01):
    rows, depth, tiles = plan.rows, plan.depth, plan.tiles
    wanted = (1, 3) if component == 1 else (component,)
    sources = [home_slopes(plan, FIELD_ORDER.index(f), groups) for f in wanted]
    buffers = [b for source in sources for b in source[0]]
    total = len(buffers)
    chunk_of, tile_of, *entries = order
    pairs = chunk_of.shape[0]
    chunks = entries[0].shape[0]
    marker_rows = plan.marker_rows

    def kernel(me_ref, chunk_ref, tile_ref, flow_ref, base_ref, row_ref, lane_ref, marker_ref,
               weight_ref, solid_ref, *rest):
        bufs = rest[:total]
        rest = rest[total:]
        if out is not None:
            rest = rest[1:]
        out_ref, speed, value, prov, terms, found, sems, *slopes = rest
        copies = [
            pltpu.make_async_copy(flow_ref.at[1, 0], speed, sems.at[0]),
            pltpu.make_async_copy(base_ref.at[component], value, sems.at[1]),
        ]
        used = 0
        for (held, _, count, _, copies_of), ref in zip(sources, slopes):
            copies += copies_of(me_ref[0], bufs[used : used + len(held)], ref, sems, len(copies))
            used += len(held)
        run_copies(copies)
        for t in range(tiles):
            z = slice(t * LANES, (t + 1) * LANES)
            term = speed[:, z] * slopes[0][sources[0][3] + t]
            if component == 1:
                term = term + slopes[1][sources[1][3] + t]
            result = value[:, z] - 0.1 * term
            prov[t] = result
            h, l = two_terms(result)
            terms[t, :, :LANES] = h
            terms[t, :, LANES:] = l

        row_at = lax.broadcasted_iota(jnp.int32, (rows, CHUNK), 0)
        lane_at = lax.broadcasted_iota(jnp.int32, (LANES, CHUNK), 0)
        marker_at = lax.broadcasted_iota(jnp.int32, (marker_rows, CHUNK), 0)
        one, zero = jnp.ones((), BF), jnp.zeros((), BF)

        def one_hot(hit):
            return jnp.where(hit, 1.0, 0.0).astype(BF)

        def pair(i):
            c, t = chunk_ref[i], tile_ref[i]
            return c, jnp.minimum(t, tiles - 1), row_at == row_ref[c] - t * rows, lane_at == lane_ref[c]

        found[...] = jnp.zeros_like(found)

        def gather(i, carry):
            c, t, rows_hit, lanes_hit = pair(i)
            lanes = one_hot(lanes_hit)
            both = dot(terms[t], jnp.concatenate([lanes, lanes], axis=0))
            found[c] += jnp.sum(jnp.where(rows_hit, both, 0.0), axis=0, keepdims=True)
            return carry

        lax.fori_loop(0, pairs, gather, 0, unroll=UNROLL)

        def add_up(c, total):
            m = marker_ref[c]
            share = jnp.where(marker_at == m // LANES, found[c] * weight_ref[c], 0.0)
            return total + dot_t(jnp.concatenate(two_terms(share), axis=0), one_hot(lane_at == m % LANES))

        sampled = lax.fori_loop(0, chunks, add_up, jnp.zeros((2 * marker_rows, LANES), F32), unroll=8)
        sampled = jnp.concatenate(two_terms(sampled[:marker_rows] + sampled[marker_rows:]), axis=0)

        def spread(c, carry):
            m = marker_ref[c]
            both = dot(sampled, one_hot(lane_at == m % LANES))
            both = jnp.where(marker_at == m // LANES, both[:marker_rows] + both[marker_rows:], 0.0)
            found[c] = jnp.sum(both, axis=0, keepdims=True) * weight_ref[c]
            return carry

        lax.fori_loop(0, chunks, spread, 0, unroll=8)

        def scatter(i, carry):
            c, t, rows_hit, lanes_hit = pair(i)
            value = [jnp.where(lanes_hit, x.astype(F32), 0.0).astype(BF) for x in two_terms(found[c])]
            both = dot_t(one_hot(rows_hit), jnp.concatenate(value, axis=0))
            prov[t] -= both[:, :LANES] + both[:, LANES:]
            return carry

        lax.fori_loop(0, pairs, scatter, 0, unroll=UNROLL)
        fluid = 1.0 - solid_ref[...].astype(F32)
        for t in range(tiles):
            z = slice(t * LANES, (t + 1) * LANES)
            b = t * LANES // (depth // solid.shape[1])
            value[:, z] = fluid[:, b : b + 1] * prov[t]
        last = pltpu.make_async_copy(value, out_ref.at[component, 0], sems.at[0])
        last.start()
        last.wait()

    operands = [me, chunk_of, tile_of, flow, base, *entries, solid, *buffers]
    specs = [SMEM] * 3 + [HBM] * 2 + [VMEM] * (len(entries) + 1) + [HBM] * total
    aliases = {}
    if out is not None:
        aliases = {len(operands): 0}
        operands.append(out)
        specs.append(HBM)
    block = pltpu.VMEM((rows, depth), F32)
    return pl.pallas_call(
        kernel, out_shape=jax.ShapeDtypeStruct((3, 1, rows, depth), F32), in_specs=specs, out_specs=HBM,
        input_output_aliases=aliases,
        scratch_shapes=[
            block, block, pltpu.VMEM((tiles, rows, LANES), F32), pltpu.VMEM((tiles, rows, 2 * LANES), BF),
            pltpu.VMEM((chunks, 1, CHUNK), F32),
            pltpu.SemaphoreType.DMA((2 + sum(source[2] for source in sources),)),
            *[pltpu.VMEM((source[1], rows, LANES), F32) for source in sources],
        ],
        compiler_params=params(),
        cost_estimate=cost(pairs * 16 * rows * CHUNK * LANES, 20 * rows * depth, share), name="home_step",
    )(*operands)


def body(flow, marker_cells, marker_weights, solid_blocks, *, pens, grps):
    _, planes, rows, depth = flow.shape
    assert planes == 1 and depth % LANES == 0 and rows % 8 == 0
    width = depth // grps
    plan = Plan(pens, rows, depth)
    plan.marker_rows = -(-marker_weights.shape[2] // LANES // 8) * 8
    pen_at = jnp.full((1,), lax.axis_index("pen"), jnp.int32)
    tables = [jnp.asarray(t) for t in split_table(pens * rows)]
    tables_z = tables if depth == pens * rows else [jnp.asarray(t) for t in split_table(depth)]

    def after(value, *others):
        return lax.optimization_barrier((value, others))[0]

    chips = plan.chips
    shifts = sorted(range(1, chips), key=lambda s: abs(2 * s - chips))

    def send_lines(blocks):
        got = {0: blocks[0]}
        for s in shifts:
            got[s] = lax.ppermute(blocks[s], "pen", [(i, (i + CORES * s) % pens) for i in range(pens)])
        return [got[s] for s in range(chips)]

    def swap(blocks):
        def other(value):
            return lax.ppermute(value, "pen", [(i, i ^ 1) for i in range(pens)])

        joined = other(jnp.concatenate(blocks[1:], axis=0))
        return [other(blocks[0])] + jnp.split(joined, chips - 1, axis=0)

    def cut_depth(value):
        return jnp.moveaxis(value.reshape(*value.shape[:-1], grps, width), -2, 0)

    def exchange(value):
        return lax.all_to_all(value, "grp", 0, 0, tiled=True)

    def slopes_of(rounds, cut, lines):
        return line_slopes(plan, rounds, cut, pen_at, lines, swap(lines), tables)

    first, second = plan.stages
    middle = -(-len(second) // 2)
    cut = [second[:middle], second[middle:]] if len(second) > 1 else [second]
    together = lax.optimization_barrier

    packed = pack_lines(plan, first, pen_at, flow)
    lines = send_lines(packed)
    lines_x = exchange(cut_depth(after(flow, packed)[:, 0]))
    order = marker_order(*after((marker_cells[0, 0], marker_weights[0, 0]), packed), rows, depth)
    packed = pack_lines(plan, second, pen_at, after(flow, order))
    lines, order, packed = together((lines, order, packed))
    lines_2 = send_lines(packed)
    (slopes,) = slopes_of(first, [first], lines)
    terms_x, slopes_x = slab_terms(compact_matrix(grps), after(lines_x, slopes))
    across = exchange(terms_x)
    lines_2, slopes, slopes_x = together((lines_2, slopes, slopes_x))
    back = send_lines(slopes)
    slopes = slopes_of(second, cut, lines_2)
    base, slope_z = depth_terms(after(flow, slopes), tables_z)
    base = base - 0.1 * jnp.moveaxis(after(across, base), 0, 2).reshape(3, rows, depth)
    back, slopes, base, slope_z = together((back, slopes, base, slope_z))
    groups = [(first, back)]
    step = functools.partial(home_step, plan, me=pen_at, flow=flow, base=base, order=order, solid=solid_blocks[0])
    back = send_lines(slopes[0])
    out = step(1, groups=groups, out=None)
    slopes, back, out = together((slopes, back, out))
    groups = groups + [(cut[0], back)]
    if len(cut) > 1:
        back = send_lines(slopes[1])
    out = step(0, groups=groups, out=out)
    divergence = home_divergence(plan, grps, pen_at, after(slope_z, out), groups)
    poisson = exchange(divergence)
    if len(cut) > 1:
        back, out = together((back, out))
        groups = groups + [(cut[1], back)]
    out = step(2, groups=groups, out=out, share=10.0)
    return out, poisson + slopes_x


def solution(mesh):
    return jax.shard_map(
        functools.partial(body, pens=mesh.shape["pen"], grps=mesh.shape["grp"]),
        mesh=mesh,
        in_specs=(
            P(None, "grp", "pen", None),
            P("grp", "pen", None, None),
            P("grp", "pen", None, None),
            P("grp", "pen", None),
        ),
        out_specs=(P(None, "grp", "pen", None), P(None, "pen", "grp")),
        check_vma=False,
    )
```

```python
import functools
import math

import jax
import jax.numpy as jnp
import ml_dtypes
import numpy as np
from jax import lax
from jax.experimental import pallas as pl
from jax.experimental.pallas import tpu as pltpu
from jax.sharding import PartitionSpec as P

LANES = 128
CHUNK = 256
CORES = 2
UNROLL = 22
FIELD_ORDER = (1, 3, 0, 2)
ANY = pl.BlockSpec(memory_space=pl.ANY)
HBM = pl.BlockSpec(memory_space=pltpu.HBM)
SMEM = pl.BlockSpec(memory_space=pltpu.SMEM)
VMEM = pl.BlockSpec(memory_space=pltpu.VMEM)
BF = jnp.bfloat16
F32 = jnp.float32


def split_table(length):
    half = length // 2
    lag = np.arange(length)
    row = np.zeros(length)
    row[1:] = math.pi / length * (1 - 2 * (lag[1:] % 2)) / np.tan(math.pi * lag[1:] / length)
    row[half] = 0.0
    offset = np.arange(half)[:, None] - np.arange(half)[None, :]
    same, other = row[offset % length], row[(offset + half) % length]
    table = np.stack([(same + other) / 2, (same - other) / 2])
    high = table.astype(ml_dtypes.bfloat16)
    low = (table - high.astype(np.float64)).astype(ml_dtypes.bfloat16)
    return high, low


def compact_matrix(length):
    eye = np.eye(length)
    off = lambda k: np.eye(length, k=k)
    left = eye + (off(1) + off(-1)) / 3
    right = 7 / 9 * (off(1) - off(-1)) + 1 / 36 * (off(2) - off(-2))
    return np.linalg.solve(left, right).astype(np.float32)


def two_terms(value):
    high = value.astype(BF)
    return high, (value - high.astype(F32)).astype(BF)


def dot(a, b):
    return jnp.dot(a, b, preferred_element_type=F32)


def dot_t(a, b):
    return lax.dot_general(a, b, (((1,), (1,)), ((), ())), preferred_element_type=F32)


def params():
    return pltpu.CompilerParams(vmem_limit_bytes=60 * 2**20)


def cost(flops, moved, share=0.01):
    return pl.CostEstimate(flops=int(flops * share), bytes_accessed=int(moved * share), transcendentals=0)


class Plan:
    def __init__(self, pens, rows, depth):
        self.pens, self.chips, self.rows, self.depth = pens, pens // CORES, rows, depth
        self.tiles = depth // LANES
        self.pairs = len(FIELD_ORDER) * self.tiles
        self.rounds = -(-self.pairs // self.chips)
        first = min(-(-2 * self.tiles // self.chips), self.rounds)
        self.stages = [list(range(first))]
        if first < self.rounds:
            self.stages.append(list(range(first, self.rounds)))


def run_copies(copies):
    for c in copies:
        c.start()
    for c in copies:
        c.wait()


def pack_lines(plan, rounds, me, flow):
    n, rows, tiles = plan.chips, plan.rows, plan.tiles
    start, end = rounds[0] * n, min((rounds[-1] + 1) * n, plan.pairs)

    def kernel(me_ref, flow_ref, *rest):
        outs, (held, in_sems, out_sems) = rest[:-3], rest[-3:]
        loads = [pltpu.make_async_copy(
            flow_ref.at[FIELD_ORDER[q // tiles], 0, :, pl.ds(q % tiles * LANES, LANES)], held.at[q - start],
            in_sems.at[q - start]) for q in range(start, end)]
        for c in loads:
            c.start()
        copies = []
        for k in range(len(rounds)):
            for c in loads[k * n : (k + 1) * n]:
                c.wait()
            for s in range(n):
                pair = jnp.minimum(k * n + lax.rem(me_ref[0] // CORES + s, n), end - start - 1)
                copies.append(pltpu.make_async_copy(held.at[pair], outs[s].at[k], out_sems.at[len(copies)]))
                copies[-1].start()
        for c in copies:
            c.wait()

    shape = jax.ShapeDtypeStruct((len(rounds), rows, LANES), F32)
    return pl.pallas_call(
        kernel, out_shape=[shape] * n, in_specs=[SMEM, HBM], out_specs=[HBM] * n,
        scratch_shapes=[pltpu.VMEM((end - start, rows, LANES), F32), pltpu.SemaphoreType.DMA((end - start,)),
                        pltpu.SemaphoreType.DMA((n * len(rounds),))],
        compiler_params=params(), cost_estimate=cost(0, 2 * flow.size), name="pack_lines",
    )(me, flow)


def line_slopes(plan, rounds, groups, me, received, other, tables):
    n, rows = plan.chips, plan.rows
    length, half, count = plan.pens * rows, plan.pens * rows // 2, len(rounds)
    wide = count * LANES
    block = math.gcd(half, 256)

    def kernel(me_ref, high_ref, low_ref, *rest):
        ins, others = rest[:n], rest[n : 2 * n]
        outs = rest[2 * n : 2 * n + n * len(groups)]
        lines, result, x_high, x_low, in_sems, out_sems = rest[2 * n + n * len(groups) :]
        chip, core = me_ref[0] // CORES, me_ref[0] % CORES
        copies = []
        for refs, c in ((ins, core), (others, 1 - core)):
            for s in range(n):
                pen = lax.rem(chip + n - s, n) * CORES + c
                at = pl.ds(pl.multiple_of(pen * rows, 8), rows)
                copies.append(pltpu.make_async_copy(refs[s], lines.at[:, at, :], in_sems.at[len(copies)]))
        run_copies(copies)

        @pl.loop(0, half // block)
        def _(b):
            upper = pl.ds(pl.multiple_of(b * block, block), block)
            lower = pl.ds(pl.multiple_of(b * block + half, block), block)
            for k in range(count):
                to = pl.ds(k * LANES, LANES)
                first, second = lines[k, upper, :], lines[k, lower, :]
                for part, value in enumerate((first + second, first - second)):
                    h, l = two_terms(value)
                    x_high[part, upper, to] = h
                    x_low[part, upper, to] = l

        for home in range(n // 2):
            at = pl.ds(pl.multiple_of((home * CORES + core) * rows, 16), rows)
            parts = []
            for part in range(2):
                t_high, t_low = high_ref[part, at, :], low_ref[part, at, :]
                h, l = x_high[part], x_low[part]
                parts.append(dot(t_high, h) + (dot(t_high, l) + dot(t_low, h)))
            top, bottom = parts[0] + parts[1], parts[0] - parts[1]
            for k in range(count):
                result[home, k] = top[:, k * LANES : (k + 1) * LANES]
                result[home + n // 2, k] = bottom[:, k * LANES : (k + 1) * LANES]

        copies = []
        for g, group in enumerate(groups):
            at_k = pl.ds(rounds.index(group[0]), len(group))
            for s in range(n):
                home = lax.rem(chip + s, n)
                copies.append(pltpu.make_async_copy(result.at[home, at_k], outs[g * n + s], out_sems.at[len(copies)]))
        run_copies(copies)

    shapes = [jax.ShapeDtypeStruct((len(g), rows, LANES), F32) for g in groups for _ in range(n)]
    out = pl.pallas_call(
        kernel, out_shape=shapes,
        in_specs=[SMEM, VMEM, VMEM] + [HBM] * (2 * n), out_specs=[ANY] * len(shapes),
        scratch_shapes=[
            pltpu.VMEM((count, length, LANES), F32), pltpu.VMEM((n, count, rows, LANES), F32),
            pltpu.VMEM((2, half, wide), BF), pltpu.VMEM((2, half, wide), BF),
            pltpu.SemaphoreType.DMA((2 * n,)), pltpu.SemaphoreType.DMA((len(shapes),)),
        ],
        compiler_params=params(),
        cost_estimate=cost(6 * half * half * wide, 6 * count * length * LANES + 8 * half * half),
        name="line_slopes",
    )(me, *tables, *received, *other)
    return [out[g * n : (g + 1) * n] for g in range(len(groups))]


def depth_terms(flow, tables):
    fields, _, rows, depth = flow.shape
    half = depth // 2
    step = math.gcd(rows, 48)

    def kernel(flow_ref, high_ref, low_ref, base_ref, slope_ref):
        value = flow_ref[:, 0].reshape(fields * step, depth)
        parts = []
        for part, x in enumerate((value[:, :half] + value[:, half:], value[:, :half] - value[:, half:])):
            h, l = two_terms(x)
            parts.append(dot(h, high_ref[part]) + (dot(l, high_ref[part]) + dot(h, low_ref[part])))
        minus = jnp.concatenate([parts[0] + parts[1], parts[0] - parts[1]], axis=1)
        rows_of = lambda f: minus[f * step : (f + 1) * step]
        speed = flow_ref[2, 0]
        for i in range(3):
            term = speed * rows_of(i)
            if i == 2:
                term = term + rows_of(3)
                slope_ref[...] = -rows_of(2)
            base_ref[i] = flow_ref[i, 0] + 0.1 * term

    whole = pl.BlockSpec((2, half, half), lambda r: (0, 0, 0), pipeline_mode=pl.Buffered(1))
    size = 4 * fields * rows * depth
    return pl.pallas_call(
        kernel, grid=(rows // step,),
        out_shape=[jax.ShapeDtypeStruct((3, rows, depth), F32), jax.ShapeDtypeStruct((rows, depth), F32)],
        in_specs=[pl.BlockSpec((fields, 1, step, depth), lambda r: (0, 0, r, 0)), whole, whole],
        out_specs=[pl.BlockSpec((3, step, depth), lambda r: (0, r, 0)), pl.BlockSpec((step, depth), lambda r: (r, 0))],
        compiler_params=params(), cost_estimate=cost(12 * fields * rows * half * half, 2 * size + 8 * half * half),
        name="depth_terms",
    )(flow, *tables)


def slab_terms(coefficients, planes):
    n, fields, rows, width = planes.shape
    step = math.gcd(rows, 48)

    def kernel(in_ref, out_ref, slope_ref):
        for i in range(n):
            for f in range(fields):
                slope = sum(float(coefficients[i, j]) * in_ref[j, f] for j in range(n))
                if f == 0:
                    slope_ref[i] = slope
                if f < 3:
                    out_ref[i, f] = in_ref[i, 0] * slope
                else:
                    out_ref[i, 0] += slope

    size = 4 * n * fields * rows * width
    block = lambda *lead: pl.BlockSpec((*lead, step, width), lambda r: (0,) * len(lead) + (r, 0))
    return pl.pallas_call(
        kernel, grid=(rows // step,),
        out_shape=[jax.ShapeDtypeStruct((n, 3, rows, width), F32), jax.ShapeDtypeStruct((n, rows, width), F32)],
        in_specs=[block(n, fields)], out_specs=[block(n, 3), block(n)],
        compiler_params=params(), cost_estimate=cost(n * size, 2 * size), name="slab_terms",
    )(planes)


def marker_order(cells, weights, rows, depth):
    markers, stencil = weights.shape
    tiles, entries = depth // LANES, markers * stencil
    chunks = entries // CHUNK
    marker = lax.iota(jnp.int32, entries) // stencil
    flat = cells.reshape(-1)
    row, z = flat // depth, flat % depth
    place = (z // LANES * rows + row) * LANES + z % LANES
    weight = weights.reshape(-1)
    if rows * depth * markers < 2**31:
        key, weight = lax.sort((place * markers + marker, weight), num_keys=1)
        place, marker = key // markers, key % markers
    else:
        place, marker, weight = lax.sort((place, marker, weight), num_keys=1)
    shape = (chunks, 1, CHUNK)
    tile_row, lane = place // LANES, place % LANES
    tile = (tile_row // rows).reshape(chunks, CHUNK)
    first, last = tile[:, 0], tile[:, -1]
    end = jnp.cumsum(last - first + 1)
    start = end - (last - first + 1)
    pairs = chunks + tiles
    index = lax.iota(jnp.int32, pairs)
    chunk = jnp.minimum(jnp.sum((end[None, :] <= index[:, None]).astype(jnp.int32), axis=1), chunks - 1)
    pick = chunk[:, None] == lax.iota(jnp.int32, chunks)[None, :]
    at = jnp.sum(jnp.where(pick, (first - start)[None, :], 0), axis=1) + index
    at = jnp.where(index < end[-1], at, tiles)
    return chunk, at, tile_row.reshape(shape), lane.reshape(shape), marker.reshape(shape), weight.reshape(shape)


def home_slopes(plan, slot, groups):
    n, tiles = plan.chips, plan.tiles
    low, high = slot * tiles // n, ((slot + 1) * tiles - 1) // n
    wanted, buffers = [], []
    for group, blocks in groups:
        if any(low <= r <= high for r in group):
            wanted += [(len(buffers) + s, k, r, s) for k, r in enumerate(group) if low <= r <= high for s in range(n)]
            buffers += blocks

    def copies(me, refs, slopes, sems, first):
        return [(r, pltpu.make_async_copy(
            refs[b].at[k], slopes.at[(r - low) * n + lax.rem(me // CORES + n - s, n)], sems.at[first + i]))
            for i, (b, k, r, s) in enumerate(wanted)]

    skip = slot * tiles - low * n
    spans = [(r, max(0, (r - low) * n - skip), min(tiles, (r - low + 1) * n - skip)) for r in range(low, high + 1)]
    return buffers, (high - low + 1) * n, len(wanted), skip, copies, spans


def home_divergence(plan, parts, me, slope_z, groups):
    rows, depth, tiles = plan.rows, plan.depth, plan.tiles
    buffers, span, count, skip, copies_of, _ = home_slopes(plan, FIELD_ORDER.index(1), groups)

    def kernel(me_ref, slope_ref, *rest):
        refs, (out_ref, slopes, third, sems) = rest[: len(buffers)], rest[len(buffers) :]
        copies = [c for _, c in copies_of(me_ref[0], refs, slopes, sems, 1)]
        run_copies([pltpu.make_async_copy(slope_ref, third, sems.at[0])] + copies)
        for t in range(tiles):
            z = slice(t * LANES, (t + 1) * LANES)
            third[:, z] = third[:, z] + slopes[skip + t]
        width = depth // parts
        for g in range(parts):
            out_ref[g] = third[:, g * width : (g + 1) * width]

    return pl.pallas_call(
        kernel, out_shape=jax.ShapeDtypeStruct((parts, rows, depth // parts), F32),
        in_specs=[SMEM] + [HBM] * (1 + len(buffers)), out_specs=VMEM,
        scratch_shapes=[pltpu.VMEM((span, rows, LANES), F32), pltpu.VMEM((rows, depth), F32),
                        pltpu.SemaphoreType.DMA((1 + count,))],
        compiler_params=params(), cost_estimate=cost(0, 12 * rows * depth), name="home_divergence",
    )(me, slope_z, *buffers)


def home_step(plan, component, me, flow, base, groups, order, solid, out, share=0.01):
    rows, depth, tiles = plan.rows, plan.depth, plan.tiles
    wanted = (1, 3) if component == 1 else (component,)
    sources = [home_slopes(plan, FIELD_ORDER.index(f), groups) for f in wanted]
    buffers = [b for source in sources for b in source[0]]
    total = len(buffers)
    chunk_of, tile_of, *entries = order
    pairs = chunk_of.shape[0]
    chunks = entries[0].shape[0]
    marker_rows = plan.marker_rows
    assert rows <= 256

    spans = sources[0][5]

    def kernel(me_ref, chunk_ref, tile_ref, flow_ref, base_ref, *rest):
        early, bufs, rest = rest[:5], rest[5 : 5 + total], rest[5 + total :]
        if out is not None:
            rest = rest[1:]
        out_ref, speed, value, prov, terms, found, row_ref, lane_ref, marker_ref, weight_ref, solid_ref, sems, *slopes = rest
        first = {span[0]: [] for span in spans}
        for r, start, end in spans:
            z = pl.ds(start * LANES, (end - start) * LANES)
            for src, dst in ((flow_ref.at[1, 0], speed), (base_ref.at[component], value)):
                at = sum(len(cs) for cs in first.values())
                first[r].append(pltpu.make_async_copy(src.at[:, z], dst.at[:, z], sems.at[at]))
        at, used = 2 * len(spans), 0
        for source, ref in zip(sources, slopes):
            for r, c in source[4](me_ref[0], bufs[used : used + len(source[0])], ref, sems, at):
                first[r if source is sources[0] else spans[0][0]].append(c)
            at += source[2]
            used += len(source[0])
        later = [pltpu.make_async_copy(src, dst, sems.at[at + i]) for i, (src, dst) in enumerate(zip(
            early, (row_ref, lane_ref, marker_ref, weight_ref, solid_ref)))]
        for c in [c for cs in first.values() for c in cs] + later:
            c.start()
        for r, start, end in spans:
            for c in first[r]:
                c.wait()
            for t in range(start, end):
                z = slice(t * LANES, (t + 1) * LANES)
                term = speed[:, z] * slopes[0][sources[0][3] + t]
                if component == 1:
                    term = term + slopes[1][sources[1][3] + t]
                result = value[:, z] - 0.1 * term
                prov[t] = result
                h, l = two_terms(result)
                terms[t, :, :LANES] = h
                terms[t, :, LANES:] = l
        for c in later:
            c.wait()

        row_at = lax.broadcasted_iota(jnp.int32, (rows, CHUNK), 0)
        marker_at = lax.broadcasted_iota(jnp.int32, (marker_rows, CHUNK), 0)
        row_key = row_at.astype(BF)
        lane_key = lax.broadcasted_iota(jnp.int32, (LANES, CHUNK), 0).astype(BF)
        one, zero = jnp.ones((), BF), jnp.zeros((), BF)

        def key(value):
            return value.astype(F32).astype(BF)

        def pair(i):
            c, t = chunk_ref[i], tile_ref[i]
            return c, jnp.minimum(t, tiles - 1), row_ref[c] - t * rows, lane_key == key(lane_ref[c])

        found[...] = jnp.zeros_like(found)

        def gather(i, carry):
            c, t, row, lanes_hit = pair(i)
            lanes = jnp.where(lanes_hit, one, zero)
            both = dot(terms[t], jnp.concatenate([lanes, lanes], axis=0))
            found[c] += jnp.sum(jnp.where(row_at == row, both, 0.0), axis=0, keepdims=True)
            return carry

        lax.fori_loop(0, pairs, gather, 0, unroll=UNROLL)

        def add_up(c, total):
            m = marker_ref[c]
            share = jnp.where(marker_at == m // LANES, found[c] * weight_ref[c], 0.0)
            low_part = jnp.where(lane_key == key(m % LANES), one, zero)
            return total + dot_t(jnp.concatenate(two_terms(share), axis=0), low_part)

        sampled = lax.fori_loop(0, chunks, add_up, jnp.zeros((2 * marker_rows, LANES), F32), unroll=8)
        sampled = jnp.concatenate(two_terms(sampled[:marker_rows] + sampled[marker_rows:]), axis=0)

        def spread(c, carry):
            m = marker_ref[c]
            both = dot(sampled, jnp.where(lane_key == key(m % LANES), one, zero))
            both = jnp.where(marker_at == m // LANES, both[:marker_rows] + both[marker_rows:], 0.0)
            found[c] = jnp.sum(both, axis=0, keepdims=True) * weight_ref[c]
            return carry

        lax.fori_loop(0, chunks, spread, 0, unroll=8)

        def scatter(i, carry):
            c, t, row, lanes_hit = pair(i)
            value = [jnp.where(lanes_hit, x, zero) for x in two_terms(found[c])]
            both = dot_t(jnp.where(row_key == key(row), one, zero), jnp.concatenate(value, axis=0))
            prov[t] -= both[:, :LANES] + both[:, LANES:]
            return carry

        lax.fori_loop(0, pairs, scatter, 0, unroll=UNROLL)
        fluid = 1.0 - solid_ref[...].astype(F32)
        last = []
        for i, (_, start, end) in enumerate(spans):
            for t in range(start, end):
                b = t * LANES // (depth // solid.shape[1])
                value[:, t * LANES : (t + 1) * LANES] = fluid[:, b : b + 1] * prov[t]
            z = pl.ds(start * LANES, (end - start) * LANES)
            last.append(pltpu.make_async_copy(value.at[:, z], out_ref.at[component, 0, :, z], sems.at[i]))
            last[-1].start()
        for c in last:
            c.wait()

    operands = [me, chunk_of, tile_of, flow, base, *entries, solid, *buffers]
    specs = [SMEM] * 3 + [HBM] * (2 + len(entries) + 1 + total)
    aliases = {}
    if out is not None:
        aliases = {len(operands): 0}
        operands.append(out)
        specs.append(HBM)
    block = pltpu.VMEM((rows, depth), F32)
    return pl.pallas_call(
        kernel, out_shape=jax.ShapeDtypeStruct((3, 1, rows, depth), F32), in_specs=specs, out_specs=HBM,
        input_output_aliases=aliases,
        scratch_shapes=[
            block, block, pltpu.VMEM((tiles, rows, LANES), F32), pltpu.VMEM((tiles, rows, 2 * LANES), BF),
            pltpu.VMEM((chunks, 1, CHUNK), F32),
            *[pltpu.VMEM(x.shape, x.dtype) for x in (*entries, solid)],
            pltpu.SemaphoreType.DMA((2 * len(spans) + sum(source[2] for source in sources) + 5,)),
            *[pltpu.VMEM((source[1], rows, LANES), F32) for source in sources],
        ],
        compiler_params=params(),
        cost_estimate=cost(pairs * 16 * rows * CHUNK * LANES, 20 * rows * depth, share), name="home_step",
    )(*operands)


def body(flow, marker_cells, marker_weights, solid_blocks, *, pens, grps):
    _, planes, rows, depth = flow.shape
    assert planes == 1 and depth % LANES == 0 and rows % 8 == 0
    width = depth // grps
    plan = Plan(pens, rows, depth)
    plan.marker_rows = -(-marker_weights.shape[2] // LANES // 8) * 8
    pen_at = jnp.full((1,), lax.axis_index("pen"), jnp.int32)
    tables = [jnp.asarray(t) for t in split_table(pens * rows)]
    tables_z = tables if depth == pens * rows else [jnp.asarray(t) for t in split_table(depth)]

    def after(value, *others):
        return lax.optimization_barrier((value, others))[0]

    chips = plan.chips
    shifts = sorted(range(1, chips), key=lambda s: abs(2 * s - chips))

    def send_lines(blocks):
        got = {0: blocks[0]}
        for s in shifts:
            got[s] = lax.ppermute(blocks[s], "pen", [(i, (i + CORES * s) % pens) for i in range(pens)])
        return [got[s] for s in range(chips)]

    def swap(blocks):
        def other(value):
            return lax.ppermute(value, "pen", [(i, i ^ 1) for i in range(pens)])

        joined = other(jnp.concatenate(blocks[1:], axis=0))
        return [other(blocks[0])] + jnp.split(joined, chips - 1, axis=0)

    def cut_depth(value):
        return jnp.moveaxis(value.reshape(*value.shape[:-1], grps, width), -2, 0)

    def exchange(value):
        return lax.all_to_all(value, "grp", 0, 0, tiled=True)

    def slopes_of(rounds, cut, lines):
        return line_slopes(plan, rounds, cut, pen_at, lines, swap(lines), tables)

    first, second = plan.stages
    middle = -(-len(second) // 2)
    cut = [second[:middle], second[middle:]] if len(second) > 1 else [second]
    together = lax.optimization_barrier

    packed = pack_lines(plan, first, pen_at, flow)
    lines = send_lines(packed)
    lines_x = exchange(cut_depth(after(flow, packed)[:, 0]))
    order = marker_order(*after((marker_cells[0, 0], marker_weights[0, 0]), packed), rows, depth)
    packed = pack_lines(plan, second, pen_at, after(flow, order))
    lines, order, packed = together((lines, order, packed))
    lines_2 = send_lines(packed)
    (slopes,) = slopes_of(first, [first], lines)
    terms_x, slopes_x = slab_terms(compact_matrix(grps), after(lines_x, slopes))
    across = exchange(terms_x)
    lines_2, slopes, slopes_x = together((lines_2, slopes, slopes_x))
    back = send_lines(slopes)
    slopes = slopes_of(second, cut, lines_2)
    base, slope_z = depth_terms(after(flow, slopes), tables_z)
    base = base - 0.1 * jnp.moveaxis(after(across, base), 0, 2).reshape(3, rows, depth)
    back, slopes, base, slope_z = together((back, slopes, base, slope_z))
    groups = [(first, back)]
    step = functools.partial(home_step, plan, me=pen_at, flow=flow, base=base, order=order, solid=solid_blocks[0])
    back = send_lines(slopes[0])
    out = step(1, groups=groups, out=None)
    slopes, back, out = together((slopes, back, out))
    groups = groups + [(cut[0], back)]
    if len(cut) > 1:
        back = send_lines(slopes[1])
    out = step(0, groups=groups, out=out)
    divergence = home_divergence(plan, grps, pen_at, after(slope_z, out), groups)
    poisson = exchange(divergence)
    if len(cut) > 1:
        back, out = together((back, out))
        groups = groups + [(cut[1], back)]
    out = step(2, groups=groups, out=out, share=10.0)
    return out, poisson + slopes_x


def solution(mesh):
    return jax.shard_map(
        functools.partial(body, pens=mesh.shape["pen"], grps=mesh.shape["grp"]),
        mesh=mesh,
        in_specs=(
            P(None, "grp", "pen", None),
            P("grp", "pen", None, None),
            P("grp", "pen", None, None),
            P("grp", "pen", None),
        ),
        out_specs=(P(None, "grp", "pen", None), P(None, "pen", "grp")),
        check_vma=False,
    )
```

```python
import functools
import math

import jax
import jax.numpy as jnp
import ml_dtypes
import numpy as np
from jax import lax
from jax.experimental import pallas as pl
from jax.experimental.pallas import tpu as pltpu
from jax.sharding import PartitionSpec as P

LANES = 128
CHUNK = 256
CORES = 2
UNROLL = 22
FIELD_ORDER = (1, 3, 0, 2)
ANY = pl.BlockSpec(memory_space=pl.ANY)
HBM = pl.BlockSpec(memory_space=pltpu.HBM)
SMEM = pl.BlockSpec(memory_space=pltpu.SMEM)
VMEM = pl.BlockSpec(memory_space=pltpu.VMEM)
BF = jnp.bfloat16
F32 = jnp.float32


def split_table(length):
    half = length // 2
    lag = np.arange(length)
    row = np.zeros(length)
    row[1:] = math.pi / length * (1 - 2 * (lag[1:] % 2)) / np.tan(math.pi * lag[1:] / length)
    row[half] = 0.0
    offset = np.arange(half)[:, None] - np.arange(half)[None, :]
    same, other = row[offset % length], row[(offset + half) % length]
    table = np.stack([(same + other) / 2, (same - other) / 2])
    high = table.astype(ml_dtypes.bfloat16)
    low = (table - high.astype(np.float64)).astype(ml_dtypes.bfloat16)
    return high, low


def compact_matrix(length):
    eye = np.eye(length)
    off = lambda k: np.eye(length, k=k)
    left = eye + (off(1) + off(-1)) / 3
    right = 7 / 9 * (off(1) - off(-1)) + 1 / 36 * (off(2) - off(-2))
    return np.linalg.solve(left, right).astype(np.float32)


def two_terms(value):
    high = value.astype(BF)
    return high, (value - high.astype(F32)).astype(BF)


def dot(a, b):
    return jnp.dot(a, b, preferred_element_type=F32)


def dot_t(a, b):
    return lax.dot_general(a, b, (((1,), (1,)), ((), ())), preferred_element_type=F32)


def params():
    return pltpu.CompilerParams(vmem_limit_bytes=60 * 2**20)


def cost(flops, moved, share=0.01):
    return pl.CostEstimate(flops=int(flops * share), bytes_accessed=int(moved * share), transcendentals=0)


class Plan:
    def __init__(self, pens, rows, depth):
        self.pens, self.chips, self.rows, self.depth = pens, pens // CORES, rows, depth
        self.tiles = depth // LANES
        self.pairs = len(FIELD_ORDER) * self.tiles
        self.rounds = -(-self.pairs // self.chips)
        first = min(-(-2 * self.tiles // self.chips), self.rounds)
        self.stages = [list(range(first))]
        if first < self.rounds:
            self.stages.append(list(range(first, self.rounds)))
        self.paired = self.chips & (self.chips - 1) == 0

    def to(self, chip, s):
        return chip ^ s if self.paired else (chip + s) % self.chips

    def source(self, chip, s):
        return chip ^ s if self.paired else (chip + self.chips - s) % self.chips


def run_copies(copies):
    for c in copies:
        c.start()
    for c in copies:
        c.wait()


def pack_lines(plan, rounds, me, flow):
    n, rows, tiles = plan.chips, plan.rows, plan.tiles
    start, end = rounds[0] * n, min((rounds[-1] + 1) * n, plan.pairs)

    def kernel(me_ref, flow_ref, *rest):
        outs, (held, in_sems, out_sems) = rest[:-3], rest[-3:]
        loads = [pltpu.make_async_copy(
            flow_ref.at[FIELD_ORDER[q // tiles], 0, :, pl.ds(q % tiles * LANES, LANES)], held.at[q - start],
            in_sems.at[q - start]) for q in range(start, end)]
        for c in loads:
            c.start()
        copies = []
        for k in range(len(rounds)):
            for c in loads[k * n : (k + 1) * n]:
                c.wait()
            for s in range(n):
                pair = jnp.minimum(k * n + plan.to(me_ref[0] // CORES, s), end - start - 1)
                copies.append(pltpu.make_async_copy(held.at[pair], outs[s].at[k], out_sems.at[len(copies)]))
                copies[-1].start()
        for c in copies:
            c.wait()

    shape = jax.ShapeDtypeStruct((len(rounds), rows, LANES), F32)
    return pl.pallas_call(
        kernel, out_shape=[shape] * n, in_specs=[SMEM, HBM], out_specs=[HBM] * n,
        scratch_shapes=[pltpu.VMEM((end - start, rows, LANES), F32), pltpu.SemaphoreType.DMA((end - start,)),
                        pltpu.SemaphoreType.DMA((n * len(rounds),))],
        compiler_params=params(), cost_estimate=cost(0, 2 * flow.size), name="pack_lines",
    )(me, flow)


def line_slopes(plan, rounds, groups, me, received, other, tables, share=0.01):
    n, rows = plan.chips, plan.rows
    length, half, count = plan.pens * rows, plan.pens * rows // 2, len(rounds)
    wide = count * LANES
    block = math.gcd(half, 256)

    def kernel(me_ref, high_ref, low_ref, *rest):
        ins, others = rest[:n], rest[n : 2 * n]
        outs = rest[2 * n : 2 * n + n * len(groups)]
        lines, result, x_high, x_low, in_sems, out_sems = rest[2 * n + n * len(groups) :]
        chip, core = me_ref[0] // CORES, me_ref[0] % CORES
        copies = []
        for refs, c in ((ins, core), (others, 1 - core)):
            for s in range(n):
                pen = plan.source(chip, s) * CORES + c
                at = pl.ds(pl.multiple_of(pen * rows, 8), rows)
                copies.append(pltpu.make_async_copy(refs[s], lines.at[:, at, :], in_sems.at[len(copies)]))
        run_copies(copies)

        @pl.loop(0, half // block)
        def _(b):
            upper = pl.ds(pl.multiple_of(b * block, block), block)
            lower = pl.ds(pl.multiple_of(b * block + half, block), block)
            for k in range(count):
                to = pl.ds(k * LANES, LANES)
                first, second = lines[k, upper, :], lines[k, lower, :]
                for part, value in enumerate((first + second, first - second)):
                    h, l = two_terms(value)
                    x_high[part, upper, to] = h
                    x_low[part, upper, to] = l

        for home in range(n // 2):
            at = pl.ds(pl.multiple_of((home * CORES + core) * rows, 16), rows)
            parts = []
            for part in range(2):
                t_high, t_low = high_ref[part, at, :], low_ref[part, at, :]
                h, l = x_high[part], x_low[part]
                parts.append(dot(t_high, h) + (dot(t_high, l) + dot(t_low, h)))
            top, bottom = parts[0] + parts[1], parts[0] - parts[1]
            for k in range(count):
                result[home, k] = top[:, k * LANES : (k + 1) * LANES]
                result[home + n // 2, k] = bottom[:, k * LANES : (k + 1) * LANES]

        copies = []
        for g, group in enumerate(groups):
            at_k = pl.ds(rounds.index(group[0]), len(group))
            for s in range(n):
                home = plan.to(chip, s)
                copies.append(pltpu.make_async_copy(result.at[home, at_k], outs[g * n + s], out_sems.at[len(copies)]))
        run_copies(copies)

    shapes = [jax.ShapeDtypeStruct((len(g), rows, LANES), F32) for g in groups for _ in range(n)]
    out = pl.pallas_call(
        kernel, out_shape=shapes,
        in_specs=[SMEM, VMEM, VMEM] + [HBM] * (2 * n), out_specs=[ANY] * len(shapes),
        scratch_shapes=[
            pltpu.VMEM((count, length, LANES), F32), pltpu.VMEM((n, count, rows, LANES), F32),
            pltpu.VMEM((2, half, wide), BF), pltpu.VMEM((2, half, wide), BF),
            pltpu.SemaphoreType.DMA((2 * n,)), pltpu.SemaphoreType.DMA((len(shapes),)),
        ],
        compiler_params=params(),
        cost_estimate=cost(6 * half * half * wide, 6 * count * length * LANES + 8 * half * half, share),
        name="line_slopes",
    )(me, *tables, *received, *other)
    return [out[g * n : (g + 1) * n] for g in range(len(groups))]


def depth_terms(flow, tables):
    fields, _, rows, depth = flow.shape
    half = depth // 2
    step = math.gcd(rows, 48)

    def kernel(flow_ref, high_ref, low_ref, base_ref, slope_ref):
        value = flow_ref[:, 0].reshape(fields * step, depth)
        parts = []
        for part, x in enumerate((value[:, :half] + value[:, half:], value[:, :half] - value[:, half:])):
            h, l = two_terms(x)
            parts.append(dot(h, high_ref[part]) + (dot(l, high_ref[part]) + dot(h, low_ref[part])))
        minus = jnp.concatenate([parts[0] + parts[1], parts[0] - parts[1]], axis=1)
        rows_of = lambda f: minus[f * step : (f + 1) * step]
        speed = flow_ref[2, 0]
        for i in range(3):
            term = speed * rows_of(i)
            if i == 2:
                term = term + rows_of(3)
                slope_ref[...] = -rows_of(2)
            base_ref[i] = flow_ref[i, 0] + 0.1 * term

    whole = pl.BlockSpec((2, half, half), lambda r: (0, 0, 0), pipeline_mode=pl.Buffered(1))
    size = 4 * fields * rows * depth
    return pl.pallas_call(
        kernel, grid=(rows // step,),
        out_shape=[jax.ShapeDtypeStruct((3, rows, depth), F32), jax.ShapeDtypeStruct((rows, depth), F32)],
        in_specs=[pl.BlockSpec((fields, 1, step, depth), lambda r: (0, 0, r, 0)), whole, whole],
        out_specs=[pl.BlockSpec((3, step, depth), lambda r: (0, r, 0)), pl.BlockSpec((step, depth), lambda r: (r, 0))],
        compiler_params=params(), cost_estimate=cost(12 * fields * rows * half * half, 2 * size + 8 * half * half),
        name="depth_terms",
    )(flow, *tables)


def slab_terms(coefficients, planes):
    n, fields, rows, width = planes.shape
    step = math.gcd(rows, 48)

    def kernel(in_ref, out_ref, slope_ref):
        for i in range(n):
            for f in range(fields):
                slope = sum(float(coefficients[i, j]) * in_ref[j, f] for j in range(n))
                if f == 0:
                    slope_ref[i] = slope
                if f < 3:
                    out_ref[i, f] = in_ref[i, 0] * slope
                else:
                    out_ref[i, 0] += slope

    size = 4 * n * fields * rows * width
    block = lambda *lead: pl.BlockSpec((*lead, step, width), lambda r: (0,) * len(lead) + (r, 0))
    return pl.pallas_call(
        kernel, grid=(rows // step,),
        out_shape=[jax.ShapeDtypeStruct((n, 3, rows, width), F32), jax.ShapeDtypeStruct((n, rows, width), F32)],
        in_specs=[block(n, fields)], out_specs=[block(n, 3), block(n)],
        compiler_params=params(), cost_estimate=cost(n * size, 2 * size), name="slab_terms",
    )(planes)


def marker_order(cells, weights, rows, depth):
    markers, stencil = weights.shape
    tiles, entries = depth // LANES, markers * stencil
    chunks = entries // CHUNK
    marker = lax.iota(jnp.int32, entries) // stencil
    flat = cells.reshape(-1)
    row, z = flat // depth, flat % depth
    place = (z // LANES * rows + row) * LANES + z % LANES
    weight = weights.reshape(-1)
    if rows * depth * markers < 2**31:
        key, weight = lax.sort((place * markers + marker, weight), num_keys=1)
        place, marker = key // markers, key % markers
    else:
        place, marker, weight = lax.sort((place, marker, weight), num_keys=1)
    shape = (chunks, 1, CHUNK)
    tile_row, lane = place // LANES, place % LANES
    tile = (tile_row // rows).reshape(chunks, CHUNK)
    first, last = tile[:, 0], tile[:, -1]
    end = jnp.cumsum(last - first + 1)
    start = end - (last - first + 1)
    pairs = chunks + tiles
    index = lax.iota(jnp.int32, pairs)
    chunk = jnp.minimum(jnp.sum((end[None, :] <= index[:, None]).astype(jnp.int32), axis=1), chunks - 1)
    pick = chunk[:, None] == lax.iota(jnp.int32, chunks)[None, :]
    at = jnp.sum(jnp.where(pick, (first - start)[None, :], 0), axis=1) + index
    at = jnp.where(index < end[-1], at, tiles)
    return chunk, at, tile_row.reshape(shape), lane.reshape(shape), marker.reshape(shape), weight.reshape(shape)


def home_slopes(plan, slot, groups):
    n, tiles = plan.chips, plan.tiles
    low, high = slot * tiles // n, ((slot + 1) * tiles - 1) // n
    wanted, buffers = [], []
    for group, blocks in groups:
        if any(low <= r <= high for r in group):
            wanted += [(len(buffers) + s, k, r, s) for k, r in enumerate(group) if low <= r <= high for s in range(n)]
            buffers += blocks

    def copies(me, refs, slopes, sems, first):
        return [(r, pltpu.make_async_copy(
            refs[b].at[k], slopes.at[(r - low) * n + plan.source(me // CORES, s)], sems.at[first + i]))
            for i, (b, k, r, s) in enumerate(wanted)]

    skip = slot * tiles - low * n
    spans = [(r, max(0, (r - low) * n - skip), min(tiles, (r - low + 1) * n - skip)) for r in range(low, high + 1)]
    return buffers, (high - low + 1) * n, len(wanted), skip, copies, spans


def home_divergence(plan, parts, me, slope_z, groups):
    rows, depth, tiles = plan.rows, plan.depth, plan.tiles
    buffers, span, count, skip, copies_of, _ = home_slopes(plan, FIELD_ORDER.index(1), groups)

    def kernel(me_ref, slope_ref, *rest):
        refs, (out_ref, slopes, third, sems) = rest[: len(buffers)], rest[len(buffers) :]
        copies = [c for _, c in copies_of(me_ref[0], refs, slopes, sems, 1)]
        run_copies([pltpu.make_async_copy(slope_ref, third, sems.at[0])] + copies)
        for t in range(tiles):
            z = slice(t * LANES, (t + 1) * LANES)
            third[:, z] = third[:, z] + slopes[skip + t]
        width = depth // parts
        for g in range(parts):
            out_ref[g] = third[:, g * width : (g + 1) * width]

    return pl.pallas_call(
        kernel, out_shape=jax.ShapeDtypeStruct((parts, rows, depth // parts), F32),
        in_specs=[SMEM] + [HBM] * (1 + len(buffers)), out_specs=VMEM,
        scratch_shapes=[pltpu.VMEM((span, rows, LANES), F32), pltpu.VMEM((rows, depth), F32),
                        pltpu.SemaphoreType.DMA((1 + count,))],
        compiler_params=params(), cost_estimate=cost(0, 12 * rows * depth), name="home_divergence",
    )(me, slope_z, *buffers)


def home_step(plan, component, me, flow, base, groups, order, solid, out, share=0.01):
    rows, depth, tiles = plan.rows, plan.depth, plan.tiles
    wanted = (1, 3) if component == 1 else (component,)
    sources = [home_slopes(plan, FIELD_ORDER.index(f), groups) for f in wanted]
    buffers = [b for source in sources for b in source[0]]
    total = len(buffers)
    chunk_of, tile_of, *entries = order
    pairs = chunk_of.shape[0]
    chunks = entries[0].shape[0]
    marker_rows = plan.marker_rows
    assert rows <= 256

    spans = sources[0][5]

    def kernel(me_ref, chunk_ref, tile_ref, flow_ref, base_ref, *rest):
        early, bufs, rest = rest[:5], rest[5 : 5 + total], rest[5 + total :]
        if out is not None:
            rest = rest[1:]
        out_ref, speed, value, prov, terms, found, row_ref, lane_ref, marker_ref, weight_ref, solid_ref, sems, *slopes = rest
        first = {span[0]: [] for span in spans}
        for r, start, end in spans:
            z = pl.ds(start * LANES, (end - start) * LANES)
            for src, dst in ((flow_ref.at[1, 0], speed), (base_ref.at[component], value)):
                at = sum(len(cs) for cs in first.values())
                first[r].append(pltpu.make_async_copy(src.at[:, z], dst.at[:, z], sems.at[at]))
        at, used = 2 * len(spans), 0
        for source, ref in zip(sources, slopes):
            for r, c in source[4](me_ref[0], bufs[used : used + len(source[0])], ref, sems, at):
                first[r if source is sources[0] else spans[0][0]].append(c)
            at += source[2]
            used += len(source[0])
        later = [pltpu.make_async_copy(src, dst, sems.at[at + i]) for i, (src, dst) in enumerate(zip(
            early, (row_ref, lane_ref, marker_ref, weight_ref, solid_ref)))]
        for c in [c for cs in first.values() for c in cs] + later:
            c.start()
        for r, start, end in spans:
            for c in first[r]:
                c.wait()
            for t in range(start, end):
                z = slice(t * LANES, (t + 1) * LANES)
                term = speed[:, z] * slopes[0][sources[0][3] + t]
                if component == 1:
                    term = term + slopes[1][sources[1][3] + t]
                result = value[:, z] - 0.1 * term
                prov[t] = result
                h, l = two_terms(result)
                terms[t, :, :LANES] = h
                terms[t, :, LANES:] = l
        for c in later:
            c.wait()

        row_at = lax.broadcasted_iota(jnp.int32, (rows, CHUNK), 0)
        marker_at = lax.broadcasted_iota(jnp.int32, (marker_rows, CHUNK), 0)
        row_key = row_at.astype(BF)
        lane_key = lax.broadcasted_iota(jnp.int32, (LANES, CHUNK), 0).astype(BF)
        one, zero = jnp.ones((), BF), jnp.zeros((), BF)

        def key(value):
            return value.astype(F32).astype(BF)

        def pair(i):
            c, t = chunk_ref[i], tile_ref[i]
            return c, jnp.minimum(t, tiles - 1), row_ref[c] - t * rows, lane_key == key(lane_ref[c])

        found[...] = jnp.zeros_like(found)

        def gather(i, carry):
            c, t, row, lanes_hit = pair(i)
            lanes = jnp.where(lanes_hit, one, zero)
            both = dot(terms[t], jnp.concatenate([lanes, lanes], axis=0))
            found[c] += jnp.sum(jnp.where(row_at == row, both, 0.0), axis=0, keepdims=True)
            return carry

        lax.fori_loop(0, pairs, gather, 0, unroll=UNROLL)

        def add_up(c, total):
            m = marker_ref[c]
            share = jnp.where(marker_at == m // LANES, found[c] * weight_ref[c], 0.0)
            low_part = jnp.where(lane_key == key(m % LANES), one, zero)
            return total + dot_t(jnp.concatenate(two_terms(share), axis=0), low_part)

        sampled = lax.fori_loop(0, chunks, add_up, jnp.zeros((2 * marker_rows, LANES), F32), unroll=8)
        sampled = jnp.concatenate(two_terms(sampled[:marker_rows] + sampled[marker_rows:]), axis=0)

        def spread(c, carry):
            m = marker_ref[c]
            both = dot(sampled, jnp.where(lane_key == key(m % LANES), one, zero))
            both = jnp.where(marker_at == m // LANES, both[:marker_rows] + both[marker_rows:], 0.0)
            found[c] = jnp.sum(both, axis=0, keepdims=True) * weight_ref[c]
            return carry

        lax.fori_loop(0, chunks, spread, 0, unroll=8)

        def scatter(i, carry):
            c, t, row, lanes_hit = pair(i)
            value = [jnp.where(lanes_hit, x, zero) for x in two_terms(found[c])]
            both = dot_t(jnp.where(row_key == key(row), one, zero), jnp.concatenate(value, axis=0))
            prov[t] -= both[:, :LANES] + both[:, LANES:]
            return carry

        lax.fori_loop(0, pairs, scatter, 0, unroll=UNROLL)
        fluid = 1.0 - solid_ref[...].astype(F32)
        last = []
        for i, (_, start, end) in enumerate(spans):
            for t in range(start, end):
                b = t * LANES // (depth // solid.shape[1])
                value[:, t * LANES : (t + 1) * LANES] = fluid[:, b : b + 1] * prov[t]
            z = pl.ds(start * LANES, (end - start) * LANES)
            last.append(pltpu.make_async_copy(value.at[:, z], out_ref.at[component, 0, :, z], sems.at[i]))
            last[-1].start()
        for c in last:
            c.wait()

    operands = [me, chunk_of, tile_of, flow, base, *entries, solid, *buffers]
    specs = [SMEM] * 3 + [HBM] * (2 + len(entries) + 1 + total)
    aliases = {}
    if out is not None:
        aliases = {len(operands): 0}
        operands.append(out)
        specs.append(HBM)
    block = pltpu.VMEM((rows, depth), F32)
    return pl.pallas_call(
        kernel, out_shape=jax.ShapeDtypeStruct((3, 1, rows, depth), F32), in_specs=specs, out_specs=HBM,
        input_output_aliases=aliases,
        scratch_shapes=[
            block, block, pltpu.VMEM((tiles, rows, LANES), F32), pltpu.VMEM((tiles, rows, 2 * LANES), BF),
            pltpu.VMEM((chunks, 1, CHUNK), F32),
            *[pltpu.VMEM(x.shape, x.dtype) for x in (*entries, solid)],
            pltpu.SemaphoreType.DMA((2 * len(spans) + sum(source[2] for source in sources) + 5,)),
            *[pltpu.VMEM((source[1], rows, LANES), F32) for source in sources],
        ],
        compiler_params=params(),
        cost_estimate=cost(pairs * 16 * rows * CHUNK * LANES, 20 * rows * depth, share), name="home_step",
    )(*operands)


def body(flow, marker_cells, marker_weights, solid_blocks, *, pens, grps):
    _, planes, rows, depth = flow.shape
    assert planes == 1 and depth % LANES == 0 and rows % 8 == 0
    width = depth // grps
    plan = Plan(pens, rows, depth)
    plan.marker_rows = -(-marker_weights.shape[2] // LANES // 8) * 8
    pen_at = jnp.full((1,), lax.axis_index("pen"), jnp.int32)
    tables = [jnp.asarray(t) for t in split_table(pens * rows)]
    tables_z = tables if depth == pens * rows else [jnp.asarray(t) for t in split_table(depth)]

    def after(value, *others):
        return lax.optimization_barrier((value, others))[0]

    chips = plan.chips
    shifts = [2, 1, 3] if chips == 4 else list(range(1, chips))

    def send_lines(blocks):
        got = {0: blocks[0]}
        for s in shifts:
            got[s] = lax.ppermute(blocks[s], "pen", [(i, plan.to(i // CORES, s) * CORES + i % CORES) for i in range(pens)])
        return [got[s] for s in range(chips)]

    def other(value):
        return lax.ppermute(value, "pen", [(i, i ^ 1) for i in range(pens)])

    def swap(blocks):
        joined = other(jnp.concatenate(blocks[1:], axis=0))
        return [other(blocks[0])] + jnp.split(joined, chips - 1, axis=0)

    def cut_depth(value):
        return jnp.moveaxis(value.reshape(*value.shape[:-1], grps, width), -2, 0)

    def exchange(value):
        return lax.all_to_all(value, "grp", 0, 0, tiled=True)

    def slopes_of(rounds, cut, lines, swapped, share=0.01):
        return line_slopes(plan, rounds, cut, pen_at, lines, swapped, tables, share)

    first, second = plan.stages
    middle = -(-len(second) // 2)
    cut = [second[:middle], second[middle:]] if len(second) > 1 else [second]
    def together(values):
        turn = lambda v, back: [v[0]] + [v[1 + (shifts.index(s) if back else shifts[s - 1] - 1)] for s in range(1, chips)]
        is_lines = lambda v: isinstance(v, list) and len(v) == chips and all(hasattr(x, "shape") for x in v)
        turned = [turn(v, False) if is_lines(v) else v for v in values]
        out = lax.optimization_barrier(tuple(turned))
        return [turn(o, True) if is_lines(v) else o for v, o in zip(values, out)]

    packed = pack_lines(plan, first, pen_at, flow)
    lines = send_lines(packed)
    lines_x = exchange(cut_depth(after(flow, packed)[:, 0]))
    order = marker_order(*after((marker_cells[0, 0], marker_weights[0, 0]), packed), rows, depth)
    packed = pack_lines(plan, second, pen_at, after(flow, order))
    lines, order, packed = together((lines, order, packed))
    lines_2 = send_lines(packed)
    (slopes,) = slopes_of(first, [first], lines, swap(lines))
    own = other(after(packed[0], slopes))
    terms_x, slopes_x = slab_terms(compact_matrix(grps), after(lines_x, slopes))
    across = exchange(terms_x)
    lines_2, slopes, slopes_x, own = together((lines_2, slopes, slopes_x, own))
    back = send_lines(slopes)
    slopes = slopes_of(second, cut, lines_2, [own] + [other(x) for x in lines_2[1:]], 6.5)
    base, slope_z = depth_terms(after(flow, slopes), tables_z)
    base = base - 0.1 * jnp.moveaxis(after(across, base), 0, 2).reshape(3, rows, depth)
    back, slopes, base, slope_z = together((back, slopes, base, slope_z))
    groups = [(first, back)]
    step = functools.partial(home_step, plan, me=pen_at, flow=flow, base=base, order=order, solid=solid_blocks[0])
    back = send_lines(slopes[0])
    out = step(1, groups=groups, out=None)
    slopes, back, out = together((slopes, back, out))
    groups = groups + [(cut[0], back)]
    if len(cut) > 1:
        back = send_lines(slopes[1])
    out = step(0, groups=groups, out=out)
    divergence = home_divergence(plan, grps, pen_at, after(slope_z, out), groups)
    poisson = exchange(divergence)
    if len(cut) > 1:
        back, out = together((back, out))
        groups = groups + [(cut[1], back)]
    out = step(2, groups=groups, out=out, share=10.0)
    return out, poisson + slopes_x


def solution(mesh):
    return jax.shard_map(
        functools.partial(body, pens=mesh.shape["pen"], grps=mesh.shape["grp"]),
        mesh=mesh,
        in_specs=(
            P(None, "grp", "pen", None),
            P("grp", "pen", None, None),
            P("grp", "pen", None, None),
            P("grp", "pen", None),
        ),
        out_specs=(P(None, "grp", "pen", None), P(None, "pen", "grp")),
        check_vma=False,
    )
```

```python
import functools
import math

import jax
import jax.numpy as jnp
import ml_dtypes
import numpy as np
from jax import lax
from jax.experimental import pallas as pl
from jax.experimental.pallas import tpu as pltpu
from jax.sharding import PartitionSpec as P

LANES = 128
CHUNK = 256
CORES = 2
UNROLL = 22
FIELD_ORDER = (1, 3, 0, 2)
ANY = pl.BlockSpec(memory_space=pl.ANY)
HBM = pl.BlockSpec(memory_space=pltpu.HBM)
SMEM = pl.BlockSpec(memory_space=pltpu.SMEM)
VMEM = pl.BlockSpec(memory_space=pltpu.VMEM)
BF = jnp.bfloat16
F32 = jnp.float32


def split_table(length):
    half = length // 2
    lag = np.arange(length)
    row = np.zeros(length)
    row[1:] = math.pi / length * (1 - 2 * (lag[1:] % 2)) / np.tan(math.pi * lag[1:] / length)
    row[half] = 0.0
    offset = np.arange(half)[:, None] - np.arange(half)[None, :]
    same, other = row[offset % length], row[(offset + half) % length]
    table = np.stack([(same + other) / 2, (same - other) / 2])
    high = table.astype(ml_dtypes.bfloat16)
    low = (table - high.astype(np.float64)).astype(ml_dtypes.bfloat16)
    return high, low


def compact_matrix(length):
    eye = np.eye(length)
    off = lambda k: np.eye(length, k=k)
    left = eye + (off(1) + off(-1)) / 3
    right = 7 / 9 * (off(1) - off(-1)) + 1 / 36 * (off(2) - off(-2))
    return np.linalg.solve(left, right).astype(np.float32)


def two_terms(value):
    high = value.astype(BF)
    return high, (value - high.astype(F32)).astype(BF)


def dot(a, b):
    return jnp.dot(a, b, preferred_element_type=F32)


def dot_t(a, b):
    return lax.dot_general(a, b, (((1,), (1,)), ((), ())), preferred_element_type=F32)


def params():
    return pltpu.CompilerParams(vmem_limit_bytes=60 * 2**20)


def cost(flops, moved, share=0.01):
    return pl.CostEstimate(flops=int(flops * share), bytes_accessed=int(moved * share), transcendentals=0)


class Plan:
    def __init__(self, pens, rows, depth):
        self.pens, self.chips, self.rows, self.depth = pens, pens // CORES, rows, depth
        self.tiles = depth // LANES
        self.pairs = len(FIELD_ORDER) * self.tiles
        self.rounds = -(-self.pairs // self.chips)
        first = min(-(-2 * self.tiles // self.chips), self.rounds)
        self.stages = [list(range(first))]
        if first < self.rounds:
            self.stages.append(list(range(first, self.rounds)))
        self.paired = self.chips & (self.chips - 1) == 0

    def to(self, chip, s):
        return chip ^ s if self.paired else (chip + s) % self.chips

    def source(self, chip, s):
        return chip ^ s if self.paired else (chip + self.chips - s) % self.chips


def run_copies(copies):
    for c in copies:
        c.start()
    for c in copies:
        c.wait()


def pack_lines(plan, rounds, me, flow):
    n, rows, tiles = plan.chips, plan.rows, plan.tiles
    start, end = rounds[0] * n, min((rounds[-1] + 1) * n, plan.pairs)

    def kernel(me_ref, flow_ref, *rest):
        outs, (held, in_sems, out_sems) = rest[:-3], rest[-3:]
        loads = [pltpu.make_async_copy(
            flow_ref.at[FIELD_ORDER[q // tiles], 0, :, pl.ds(q % tiles * LANES, LANES)], held.at[q - start],
            in_sems.at[q - start]) for q in range(start, end)]
        for c in loads:
            c.start()
        copies = []
        for k in range(len(rounds)):
            for c in loads[k * n : (k + 1) * n]:
                c.wait()
            for s in range(n):
                pair = jnp.minimum(k * n + plan.to(me_ref[0] // CORES, s), end - start - 1)
                copies.append(pltpu.make_async_copy(held.at[pair], outs[s].at[k], out_sems.at[len(copies)]))
                copies[-1].start()
        for c in copies:
            c.wait()

    shape = jax.ShapeDtypeStruct((len(rounds), rows, LANES), F32)
    return pl.pallas_call(
        kernel, out_shape=[shape] * n, in_specs=[SMEM, HBM], out_specs=[HBM] * n,
        scratch_shapes=[pltpu.VMEM((end - start, rows, LANES), F32), pltpu.SemaphoreType.DMA((end - start,)),
                        pltpu.SemaphoreType.DMA((n * len(rounds),))],
        compiler_params=params(), cost_estimate=cost(0, 2 * flow.size), name="pack_lines",
    )(me, flow)


def line_slopes(plan, rounds, groups, me, received, other, tables, share=0.01):
    n, rows = plan.chips, plan.rows
    length, half, count = plan.pens * rows, plan.pens * rows // 2, len(rounds)
    wide = count * LANES
    block = math.gcd(half, 256)

    def kernel(me_ref, high_ref, low_ref, *rest):
        ins, others = rest[:n], rest[n : 2 * n]
        outs = rest[2 * n : 2 * n + n * len(groups)]
        lines, result, x_high, x_low, in_sems, out_sems = rest[2 * n + n * len(groups) :]
        chip, core = me_ref[0] // CORES, me_ref[0] % CORES
        copies = []
        for refs, c in ((ins, core), (others, 1 - core)):
            for s in range(n):
                pen = plan.source(chip, s) * CORES + c
                at = pl.ds(pl.multiple_of(pen * rows, 8), rows)
                copies.append(pltpu.make_async_copy(refs[s], lines.at[:, at, :], in_sems.at[len(copies)]))
        run_copies(copies)

        @pl.loop(0, half // block)
        def _(b):
            upper = pl.ds(pl.multiple_of(b * block, block), block)
            lower = pl.ds(pl.multiple_of(b * block + half, block), block)
            for k in range(count):
                to = pl.ds(k * LANES, LANES)
                first, second = lines[k, upper, :], lines[k, lower, :]
                for part, value in enumerate((first + second, first - second)):
                    h, l = two_terms(value)
                    x_high[part, upper, to] = h
                    x_low[part, upper, to] = l

        for home in range(n // 2):
            at = pl.ds(pl.multiple_of((home * CORES + core) * rows, 16), rows)
            parts = []
            for part in range(2):
                t_high, t_low = high_ref[part, at, :], low_ref[part, at, :]
                h, l = x_high[part], x_low[part]
                parts.append(dot(t_high, h) + (dot(t_high, l) + dot(t_low, h)))
            top, bottom = parts[0] + parts[1], parts[0] - parts[1]
            for k in range(count):
                result[home, k] = top[:, k * LANES : (k + 1) * LANES]
                result[home + n // 2, k] = bottom[:, k * LANES : (k + 1) * LANES]

        copies = []
        for g, group in enumerate(groups):
            at_k = pl.ds(rounds.index(group[0]), len(group))
            for s in range(n):
                home = plan.to(chip, s)
                copies.append(pltpu.make_async_copy(result.at[home, at_k], outs[g * n + s], out_sems.at[len(copies)]))
        run_copies(copies)

    shapes = [jax.ShapeDtypeStruct((len(g), rows, LANES), F32) for g in groups for _ in range(n)]
    out = pl.pallas_call(
        kernel, out_shape=shapes,
        in_specs=[SMEM, VMEM, VMEM] + [HBM] * (2 * n), out_specs=[ANY] * len(shapes),
        scratch_shapes=[
            pltpu.VMEM((count, length, LANES), F32), pltpu.VMEM((n, count, rows, LANES), F32),
            pltpu.VMEM((2, half, wide), BF), pltpu.VMEM((2, half, wide), BF),
            pltpu.SemaphoreType.DMA((2 * n,)), pltpu.SemaphoreType.DMA((len(shapes),)),
        ],
        compiler_params=params(),
        cost_estimate=cost(6 * half * half * wide, 6 * count * length * LANES + 8 * half * half, share),
        name="line_slopes",
    )(me, *tables, *received, *other)
    return [out[g * n : (g + 1) * n] for g in range(len(groups))]


def depth_terms(flow, tables):
    fields, _, rows, depth = flow.shape
    half = depth // 2
    step = math.gcd(rows, 48)

    def kernel(flow_ref, high_ref, low_ref, base_ref, slope_ref):
        value = flow_ref[:, 0].reshape(fields * step, depth)
        parts = []
        for part, x in enumerate((value[:, :half] + value[:, half:], value[:, :half] - value[:, half:])):
            h, l = two_terms(x)
            parts.append(dot(h, high_ref[part]) + (dot(l, high_ref[part]) + dot(h, low_ref[part])))
        minus = jnp.concatenate([parts[0] + parts[1], parts[0] - parts[1]], axis=1)
        rows_of = lambda f: minus[f * step : (f + 1) * step]
        speed = flow_ref[2, 0]
        for i in range(3):
            term = speed * rows_of(i)
            if i == 2:
                term = term + rows_of(3)
                slope_ref[...] = -rows_of(2)
            base_ref[i] = flow_ref[i, 0] + 0.1 * term

    whole = pl.BlockSpec((2, half, half), lambda r: (0, 0, 0), pipeline_mode=pl.Buffered(1))
    size = 4 * fields * rows * depth
    return pl.pallas_call(
        kernel, grid=(rows // step,),
        out_shape=[jax.ShapeDtypeStruct((3, rows, depth), F32), jax.ShapeDtypeStruct((rows, depth), F32)],
        in_specs=[pl.BlockSpec((fields, 1, step, depth), lambda r: (0, 0, r, 0)), whole, whole],
        out_specs=[pl.BlockSpec((3, step, depth), lambda r: (0, r, 0)), pl.BlockSpec((step, depth), lambda r: (r, 0))],
        compiler_params=params(), cost_estimate=cost(12 * fields * rows * half * half, 2 * size + 8 * half * half),
        name="depth_terms",
    )(flow, *tables)


def slab_terms(coefficients, planes):
    n, fields, rows, width = planes.shape
    step = math.gcd(rows, 48)

    def kernel(in_ref, out_ref, slope_ref):
        for i in range(n):
            for f in range(fields):
                slope = sum(float(coefficients[i, j]) * in_ref[j, f] for j in range(n))
                if f == 0:
                    slope_ref[i] = slope
                if f < 3:
                    out_ref[i, f] = in_ref[i, 0] * slope
                else:
                    out_ref[i, 0] += slope

    size = 4 * n * fields * rows * width
    block = lambda *lead: pl.BlockSpec((*lead, step, width), lambda r: (0,) * len(lead) + (r, 0))
    return pl.pallas_call(
        kernel, grid=(rows // step,),
        out_shape=[jax.ShapeDtypeStruct((n, 3, rows, width), F32), jax.ShapeDtypeStruct((n, rows, width), F32)],
        in_specs=[block(n, fields)], out_specs=[block(n, 3), block(n)],
        compiler_params=params(), cost_estimate=cost(n * size, 2 * size), name="slab_terms",
    )(planes)


def marker_order(cells, weights, rows, depth):
    markers, stencil = weights.shape
    tiles, entries = depth // LANES, markers * stencil
    chunks = entries // CHUNK
    marker = lax.iota(jnp.int32, entries) // stencil
    flat = cells.reshape(-1)
    row, z = flat // depth, flat % depth
    place = (z // LANES * rows + row) * LANES + z % LANES
    weight = weights.reshape(-1)
    if rows * depth * markers < 2**31:
        key, weight = lax.sort((place * markers + marker, weight), num_keys=1)
        place, marker = key // markers, key % markers
    else:
        place, marker, weight = lax.sort((place, marker, weight), num_keys=1)
    shape = (chunks, 1, CHUNK)
    tile_row, lane = place // LANES, place % LANES
    tile = (tile_row // rows).reshape(chunks, CHUNK)
    first, last = tile[:, 0], tile[:, -1]
    end = jnp.cumsum(last - first + 1)
    start = end - (last - first + 1)
    pairs = chunks + tiles
    index = lax.iota(jnp.int32, pairs)
    chunk = jnp.minimum(jnp.sum((end[None, :] <= index[:, None]).astype(jnp.int32), axis=1), chunks - 1)
    pick = chunk[:, None] == lax.iota(jnp.int32, chunks)[None, :]
    at = jnp.sum(jnp.where(pick, (first - start)[None, :], 0), axis=1) + index
    at = jnp.where(index < end[-1], at, tiles)
    return chunk, at, tile_row.reshape(shape), lane.reshape(shape), marker.reshape(shape), weight.reshape(shape)


def home_slopes(plan, slot, groups):
    n, tiles = plan.chips, plan.tiles
    low, high = slot * tiles // n, ((slot + 1) * tiles - 1) // n
    wanted, buffers = [], []
    for group, blocks in groups:
        if any(low <= r <= high for r in group):
            wanted += [(len(buffers) + s, k, r, s) for k, r in enumerate(group) if low <= r <= high for s in range(n)]
            buffers += blocks

    def copies(me, refs, slopes, sems, first):
        return [(r, pltpu.make_async_copy(
            refs[b].at[k], slopes.at[(r - low) * n + plan.source(me // CORES, s)], sems.at[first + i]))
            for i, (b, k, r, s) in enumerate(wanted)]

    skip = slot * tiles - low * n
    spans = [(r, max(0, (r - low) * n - skip), min(tiles, (r - low + 1) * n - skip)) for r in range(low, high + 1)]
    return buffers, (high - low + 1) * n, len(wanted), skip, copies, spans


def home_divergence(plan, parts, me, slope_z, groups):
    rows, depth, tiles = plan.rows, plan.depth, plan.tiles
    buffers, span, count, skip, copies_of, _ = home_slopes(plan, FIELD_ORDER.index(1), groups)

    def kernel(me_ref, slope_ref, *rest):
        refs, (out_ref, slopes, third, sems) = rest[: len(buffers)], rest[len(buffers) :]
        copies = [c for _, c in copies_of(me_ref[0], refs, slopes, sems, 1)]
        run_copies([pltpu.make_async_copy(slope_ref, third, sems.at[0])] + copies)
        for t in range(tiles):
            z = slice(t * LANES, (t + 1) * LANES)
            third[:, z] = third[:, z] + slopes[skip + t]
        width = depth // parts
        for g in range(parts):
            out_ref[g] = third[:, g * width : (g + 1) * width]

    return pl.pallas_call(
        kernel, out_shape=jax.ShapeDtypeStruct((parts, rows, depth // parts), F32),
        in_specs=[SMEM] + [HBM] * (1 + len(buffers)), out_specs=VMEM,
        scratch_shapes=[pltpu.VMEM((span, rows, LANES), F32), pltpu.VMEM((rows, depth), F32),
                        pltpu.SemaphoreType.DMA((1 + count,))],
        compiler_params=params(), cost_estimate=cost(0, 12 * rows * depth), name="home_divergence",
    )(me, slope_z, *buffers)


def home_step(plan, component, me, flow, base, groups, order, solid, out, share=0.01):
    rows, depth, tiles = plan.rows, plan.depth, plan.tiles
    wanted = (1, 3) if component == 1 else (component,)
    sources = [home_slopes(plan, FIELD_ORDER.index(f), groups) for f in wanted]
    buffers = [b for source in sources for b in source[0]]
    total = len(buffers)
    chunk_of, tile_of, *entries = order
    pairs = chunk_of.shape[0]
    chunks = entries[0].shape[0]
    marker_rows = plan.marker_rows
    assert rows <= 256

    spans = sources[0][5]

    def kernel(me_ref, chunk_ref, tile_ref, flow_ref, base_ref, *rest):
        early, bufs, rest = rest[:5], rest[5 : 5 + total], rest[5 + total :]
        if out is not None:
            rest = rest[1:]
        out_ref, speed, value, prov, terms, found, row_ref, lane_ref, marker_ref, weight_ref, solid_ref, sems, *slopes = rest
        first = {span[0]: [] for span in spans}
        for r, start, end in spans:
            z = pl.ds(start * LANES, (end - start) * LANES)
            for src, dst in ((flow_ref.at[1, 0], speed), (base_ref.at[component], value)):
                at = sum(len(cs) for cs in first.values())
                first[r].append(pltpu.make_async_copy(src.at[:, z], dst.at[:, z], sems.at[at]))
        at, used = 2 * len(spans), 0
        for source, ref in zip(sources, slopes):
            for r, c in source[4](me_ref[0], bufs[used : used + len(source[0])], ref, sems, at):
                first[r if source is sources[0] else spans[0][0]].append(c)
            at += source[2]
            used += len(source[0])
        later = [pltpu.make_async_copy(src, dst, sems.at[at + i]) for i, (src, dst) in enumerate(zip(
            early, (row_ref, lane_ref, marker_ref, weight_ref, solid_ref)))]
        for c in [c for cs in first.values() for c in cs] + later:
            c.start()
        for r, start, end in spans:
            for c in first[r]:
                c.wait()
            for t in range(start, end):
                z = slice(t * LANES, (t + 1) * LANES)
                term = speed[:, z] * slopes[0][sources[0][3] + t]
                if component == 1:
                    term = term + slopes[1][sources[1][3] + t]
                result = value[:, z] - 0.1 * term
                prov[t] = result
                h, l = two_terms(result)
                terms[t, :, :LANES] = h
                terms[t, :, LANES:] = l
        for c in later:
            c.wait()

        row_at = lax.broadcasted_iota(jnp.int32, (rows, CHUNK), 0)
        marker_at = lax.broadcasted_iota(jnp.int32, (marker_rows, CHUNK), 0)
        row_key = row_at.astype(BF)
        lane_key = lax.broadcasted_iota(jnp.int32, (LANES, CHUNK), 0).astype(BF)
        one, zero = jnp.ones((), BF), jnp.zeros((), BF)

        def key(value):
            return value.astype(F32).astype(BF)

        def pair(i):
            c, t = chunk_ref[i], tile_ref[i]
            return c, jnp.minimum(t, tiles - 1), row_ref[c] - t * rows, lane_key == key(lane_ref[c])

        found[...] = jnp.zeros_like(found)

        def gather(i, carry):
            c, t, row, lanes_hit = pair(i)
            lanes = jnp.where(lanes_hit, one, zero)
            both = dot(terms[t], jnp.concatenate([lanes, lanes], axis=0))
            found[c] += jnp.sum(jnp.where(row_at == row, both, 0.0), axis=0, keepdims=True)
            return carry

        lax.fori_loop(0, pairs, gather, 0, unroll=UNROLL)

        def add_up(c, total):
            m = marker_ref[c]
            share = jnp.where(marker_at == m // LANES, found[c] * weight_ref[c], 0.0)
            low_part = jnp.where(lane_key == key(m % LANES), one, zero)
            return total + dot_t(jnp.concatenate(two_terms(share), axis=0), low_part)

        sampled = lax.fori_loop(0, chunks, add_up, jnp.zeros((2 * marker_rows, LANES), F32), unroll=16)
        sampled = jnp.concatenate(two_terms(sampled[:marker_rows] + sampled[marker_rows:]), axis=0)

        def spread(c, carry):
            m = marker_ref[c]
            both = dot(sampled, jnp.where(lane_key == key(m % LANES), one, zero))
            both = jnp.where(marker_at == m // LANES, both[:marker_rows] + both[marker_rows:], 0.0)
            found[c] = jnp.sum(both, axis=0, keepdims=True) * weight_ref[c]
            return carry

        lax.fori_loop(0, chunks, spread, 0, unroll=16)

        def scatter(i, carry):
            c, t, row, lanes_hit = pair(i)
            value = [jnp.where(lanes_hit, x, zero) for x in two_terms(found[c])]
            both = dot_t(jnp.where(row_key == key(row), one, zero), jnp.concatenate(value, axis=0))
            prov[t] -= both[:, :LANES] + both[:, LANES:]
            return carry

        lax.fori_loop(0, pairs, scatter, 0, unroll=UNROLL)
        fluid = 1.0 - solid_ref[...].astype(F32)
        last = []
        for i, (_, start, end) in enumerate(spans):
            for t in range(start, end):
                b = t * LANES // (depth // solid.shape[1])
                value[:, t * LANES : (t + 1) * LANES] = fluid[:, b : b + 1] * prov[t]
            z = pl.ds(start * LANES, (end - start) * LANES)
            last.append(pltpu.make_async_copy(value.at[:, z], out_ref.at[component, 0, :, z], sems.at[i]))
            last[-1].start()
        for c in last:
            c.wait()

    operands = [me, chunk_of, tile_of, flow, base, *entries, solid, *buffers]
    specs = [SMEM] * 3 + [HBM] * (2 + len(entries) + 1 + total)
    aliases = {}
    if out is not None:
        aliases = {len(operands): 0}
        operands.append(out)
        specs.append(HBM)
    block = pltpu.VMEM((rows, depth), F32)
    return pl.pallas_call(
        kernel, out_shape=jax.ShapeDtypeStruct((3, 1, rows, depth), F32), in_specs=specs, out_specs=HBM,
        input_output_aliases=aliases,
        scratch_shapes=[
            block, block, pltpu.VMEM((tiles, rows, LANES), F32), pltpu.VMEM((tiles, rows, 2 * LANES), BF),
            pltpu.VMEM((chunks, 1, CHUNK), F32),
            *[pltpu.VMEM(x.shape, x.dtype) for x in (*entries, solid)],
            pltpu.SemaphoreType.DMA((2 * len(spans) + sum(source[2] for source in sources) + 5,)),
            *[pltpu.VMEM((source[1], rows, LANES), F32) for source in sources],
        ],
        compiler_params=params(),
        cost_estimate=cost(pairs * 16 * rows * CHUNK * LANES, 20 * rows * depth, share), name="home_step",
    )(*operands)


def body(flow, marker_cells, marker_weights, solid_blocks, *, pens, grps):
    _, planes, rows, depth = flow.shape
    assert planes == 1 and depth % LANES == 0 and rows % 8 == 0
    width = depth // grps
    plan = Plan(pens, rows, depth)
    plan.marker_rows = -(-marker_weights.shape[2] // LANES // 8) * 8
    pen_at = jnp.full((1,), lax.axis_index("pen"), jnp.int32)
    tables = [jnp.asarray(t) for t in split_table(pens * rows)]
    tables_z = tables if depth == pens * rows else [jnp.asarray(t) for t in split_table(depth)]

    def after(value, *others):
        return lax.optimization_barrier((value, others))[0]

    chips = plan.chips
    shifts = [2, 1, 3] if chips == 4 else list(range(1, chips))

    def send_lines(blocks):
        got = {0: blocks[0]}
        for s in shifts:
            got[s] = lax.ppermute(blocks[s], "pen", [(i, plan.to(i // CORES, s) * CORES + i % CORES) for i in range(pens)])
        return [got[s] for s in range(chips)]

    def other(value):
        return lax.ppermute(value, "pen", [(i, i ^ 1) for i in range(pens)])

    def swap(blocks):
        joined = other(jnp.concatenate(blocks[1:], axis=0))
        return [other(blocks[0])] + jnp.split(joined, chips - 1, axis=0)

    def cut_depth(value):
        return jnp.moveaxis(value.reshape(*value.shape[:-1], grps, width), -2, 0)

    def exchange(value):
        return lax.all_to_all(value, "grp", 0, 0, tiled=True)

    def slopes_of(rounds, cut, lines, swapped, share=0.01):
        return line_slopes(plan, rounds, cut, pen_at, lines, swapped, tables, share)

    first, second = plan.stages
    middle = -(-len(second) // 2)
    cut = [second[:middle], second[middle:]] if len(second) > 1 else [second]
    def together(values):
        turn = lambda v, back: [v[0]] + [v[1 + (shifts.index(s) if back else shifts[s - 1] - 1)] for s in range(1, chips)]
        is_lines = lambda v: isinstance(v, list) and len(v) == chips and all(hasattr(x, "shape") for x in v)
        turned = [turn(v, False) if is_lines(v) else v for v in values]
        out = lax.optimization_barrier(tuple(turned))
        return [turn(o, True) if is_lines(v) else o for v, o in zip(values, out)]

    packed = pack_lines(plan, first, pen_at, flow)
    lines = send_lines(packed)
    lines_x = exchange(cut_depth(after(flow, packed)[:, 0]))
    order = marker_order(*after((marker_cells[0, 0], marker_weights[0, 0]), packed), rows, depth)
    packed = pack_lines(plan, second, pen_at, after(flow, order))
    lines, order, packed = together((lines, order, packed))
    lines_2 = send_lines(packed)
    (slopes,) = slopes_of(first, [first], lines, swap(lines))
    own = other(after(packed[0], slopes))
    terms_x, slopes_x = slab_terms(compact_matrix(grps), after(lines_x, slopes))
    across = exchange(terms_x)
    lines_2, slopes, slopes_x, own = together((lines_2, slopes, slopes_x, own))
    back = send_lines(slopes)
    slopes = slopes_of(second, cut, lines_2, [own] + [other(x) for x in lines_2[1:]], 6.5)
    base, slope_z = depth_terms(after(flow, slopes), tables_z)
    base = base - 0.1 * jnp.moveaxis(after(across, base), 0, 2).reshape(3, rows, depth)
    back, slopes, base, slope_z = together((back, slopes, base, slope_z))
    groups = [(first, back)]
    step = functools.partial(home_step, plan, me=pen_at, flow=flow, base=base, order=order, solid=solid_blocks[0])
    back = send_lines(slopes[0])
    out = step(1, groups=groups, out=None)
    back, slopes, out = together((back, slopes, out))
    groups = groups + [(cut[0], back)]
    if len(cut) > 1:
        back = send_lines(slopes[1])
    out = step(0, groups=groups, out=out)
    divergence = home_divergence(plan, grps, pen_at, after(slope_z, out), groups)
    poisson = exchange(divergence)
    if len(cut) > 1:
        back, out = together((back, out))
        groups = groups + [(cut[1], back)]
    out = step(2, groups=groups, out=out, share=10.0)
    return out, poisson + slopes_x


def solution(mesh):
    return jax.shard_map(
        functools.partial(body, pens=mesh.shape["pen"], grps=mesh.shape["grp"]),
        mesh=mesh,
        in_specs=(
            P(None, "grp", "pen", None),
            P("grp", "pen", None, None),
            P("grp", "pen", None, None),
            P("grp", "pen", None),
        ),
        out_specs=(P(None, "grp", "pen", None), P(None, "pen", "grp")),
        check_vma=False,
    )
```

```python
import functools
import math

import jax
import jax.numpy as jnp
import ml_dtypes
import numpy as np
from jax import lax
from jax.experimental import pallas as pl
from jax.experimental.pallas import tpu as pltpu
from jax.sharding import PartitionSpec as P

LANES = 128
CHUNK = 256
CORES = 2
UNROLL = 44
FIELD_ORDER = (1, 3, 0, 2)
ANY = pl.BlockSpec(memory_space=pl.ANY)
HBM = pl.BlockSpec(memory_space=pltpu.HBM)
SMEM = pl.BlockSpec(memory_space=pltpu.SMEM)
VMEM = pl.BlockSpec(memory_space=pltpu.VMEM)
BF = jnp.bfloat16
F32 = jnp.float32


def split_table(length):
    half = length // 2
    lag = np.arange(length)
    row = np.zeros(length)
    row[1:] = math.pi / length * (1 - 2 * (lag[1:] % 2)) / np.tan(math.pi * lag[1:] / length)
    row[half] = 0.0
    offset = np.arange(half)[:, None] - np.arange(half)[None, :]
    same, other = row[offset % length], row[(offset + half) % length]
    table = np.stack([(same + other) / 2, (same - other) / 2])
    high = table.astype(ml_dtypes.bfloat16)
    low = (table - high.astype(np.float64)).astype(ml_dtypes.bfloat16)
    return high, low


def compact_matrix(length):
    eye = np.eye(length)
    off = lambda k: np.eye(length, k=k)
    left = eye + (off(1) + off(-1)) / 3
    right = 7 / 9 * (off(1) - off(-1)) + 1 / 36 * (off(2) - off(-2))
    return np.linalg.solve(left, right).astype(np.float32)


def two_terms(value):
    high = value.astype(BF)
    return high, (value - high.astype(F32)).astype(BF)


def dot(a, b):
    return jnp.dot(a, b, preferred_element_type=F32)


def dot_t(a, b):
    return lax.dot_general(a, b, (((1,), (1,)), ((), ())), preferred_element_type=F32)


def params():
    return pltpu.CompilerParams(vmem_limit_bytes=60 * 2**20)


def cost(flops, moved, share=0.01):
    return pl.CostEstimate(flops=int(flops * share), bytes_accessed=int(moved * share), transcendentals=0)


class Plan:
    def __init__(self, pens, rows, depth):
        self.pens, self.chips, self.rows, self.depth = pens, pens // CORES, rows, depth
        self.tiles = depth // LANES
        self.pairs = len(FIELD_ORDER) * self.tiles
        self.rounds = -(-self.pairs // self.chips)
        first = min(-(-2 * self.tiles // self.chips), self.rounds)
        self.stages = [list(range(first))]
        if first < self.rounds:
            self.stages.append(list(range(first, self.rounds)))
        self.paired = self.chips & (self.chips - 1) == 0

    def to(self, chip, s):
        return chip ^ s if self.paired else (chip + s) % self.chips

    def source(self, chip, s):
        return chip ^ s if self.paired else (chip + self.chips - s) % self.chips


def run_copies(copies):
    for c in copies:
        c.start()
    for c in copies:
        c.wait()


def pack_lines(plan, rounds, me, flow, messages):
    n, rows, tiles = plan.chips, plan.rows, plan.tiles
    start, end = rounds[0] * n, min((rounds[-1] + 1) * n, plan.pairs)

    def kernel(me_ref, flow_ref, *rest):
        outs, (held, in_sems, out_sems) = rest[:-3], rest[-3:]
        chip = me_ref[0] // CORES
        copies = []
        if len(messages) == 1:
            loads = []
            for k, r in enumerate(rounds):
                pair = jnp.minimum(r * n + plan.to(chip, messages[0]), plan.pairs - 1)
                slot, z = pair // tiles, pl.multiple_of(pair % tiles * LANES, LANES)
                field = jnp.int32(FIELD_ORDER[0])
                for i, f in enumerate(FIELD_ORDER[1:], 1):
                    field = jnp.where(slot == i, f, field)
                loads.append(pltpu.make_async_copy(flow_ref.at[field, 0, :, pl.ds(z, LANES)], held.at[k], in_sems.at[k]))
                copies.append(pltpu.make_async_copy(held.at[k], outs[0].at[k], out_sems.at[k]))
            for c in loads:
                c.start()
            for load, store in zip(loads, copies):
                load.wait()
                store.start()
        else:
            loads = [pltpu.make_async_copy(
                flow_ref.at[FIELD_ORDER[q // tiles], 0, :, pl.ds(q % tiles * LANES, LANES)], held.at[q - start],
                in_sems.at[q - start]) for q in range(start, end)]
            for c in loads:
                c.start()
            for k in range(len(rounds)):
                for c in loads[k * n : (k + 1) * n]:
                    c.wait()
                for i, s in enumerate(messages):
                    pair = jnp.minimum(k * n + plan.to(chip, s), end - start - 1)
                    copies.append(pltpu.make_async_copy(held.at[pair], outs[i].at[k], out_sems.at[len(copies)]))
                    copies[-1].start()
        for c in copies:
            c.wait()

    shape = jax.ShapeDtypeStruct((len(rounds), rows, LANES), F32)
    return pl.pallas_call(
        kernel, out_shape=[shape] * len(messages), in_specs=[SMEM, HBM], out_specs=[HBM] * len(messages),
        scratch_shapes=[pltpu.VMEM((end - start, rows, LANES), F32), pltpu.SemaphoreType.DMA((end - start,)),
                        pltpu.SemaphoreType.DMA((len(messages) * len(rounds),))],
        compiler_params=params(), cost_estimate=cost(0, 2 * flow.size), name="pack_lines",
    )(me, flow)


def line_slopes(plan, rounds, groups, me, received, other, tables, share=0.01):
    n, rows = plan.chips, plan.rows
    length, half, count = plan.pens * rows, plan.pens * rows // 2, len(rounds)
    wide = count * LANES
    block = math.gcd(half, 256)

    def kernel(me_ref, high_ref, low_ref, *rest):
        ins, others = rest[:n], rest[n : 2 * n]
        outs = rest[2 * n : 2 * n + n * len(groups)]
        lines, result, x_high, x_low, in_sems, out_sems = rest[2 * n + n * len(groups) :]
        chip, core = me_ref[0] // CORES, me_ref[0] % CORES
        copies = []
        for refs, c in ((ins, core), (others, 1 - core)):
            for s in range(n):
                pen = plan.source(chip, s) * CORES + c
                at = pl.ds(pl.multiple_of(pen * rows, 8), rows)
                copies.append(pltpu.make_async_copy(refs[s], lines.at[:, at, :], in_sems.at[len(copies)]))
        run_copies(copies)

        @pl.loop(0, half // block)
        def _(b):
            upper = pl.ds(pl.multiple_of(b * block, block), block)
            lower = pl.ds(pl.multiple_of(b * block + half, block), block)
            for k in range(count):
                to = pl.ds(k * LANES, LANES)
                first, second = lines[k, upper, :], lines[k, lower, :]
                for part, value in enumerate((first + second, first - second)):
                    h, l = two_terms(value)
                    x_high[part, upper, to] = h
                    x_low[part, upper, to] = l

        for home in range(n // 2):
            at = pl.ds(pl.multiple_of((home * CORES + core) * rows, 16), rows)
            parts = []
            for part in range(2):
                t_high, t_low = high_ref[part, at, :], low_ref[part, at, :]
                h, l = x_high[part], x_low[part]
                parts.append(dot(t_high, h) + (dot(t_high, l) + dot(t_low, h)))
            top, bottom = parts[0] + parts[1], parts[0] - parts[1]
            for k in range(count):
                result[home, k] = top[:, k * LANES : (k + 1) * LANES]
                result[home + n // 2, k] = bottom[:, k * LANES : (k + 1) * LANES]

        copies = []
        for g, group in enumerate(groups):
            at_k = pl.ds(rounds.index(group[0]), len(group))
            for s in range(n):
                home = plan.to(chip, s)
                copies.append(pltpu.make_async_copy(result.at[home, at_k], outs[g * n + s], out_sems.at[len(copies)]))
        run_copies(copies)

    shapes = [jax.ShapeDtypeStruct((len(g), rows, LANES), F32) for g in groups for _ in range(n)]
    out = pl.pallas_call(
        kernel, out_shape=shapes,
        in_specs=[SMEM, VMEM, VMEM] + [HBM] * (2 * n), out_specs=[ANY] * len(shapes),
        scratch_shapes=[
            pltpu.VMEM((count, length, LANES), F32), pltpu.VMEM((n, count, rows, LANES), F32),
            pltpu.VMEM((2, half, wide), BF), pltpu.VMEM((2, half, wide), BF),
            pltpu.SemaphoreType.DMA((2 * n,)), pltpu.SemaphoreType.DMA((len(shapes),)),
        ],
        compiler_params=params(),
        cost_estimate=cost(6 * half * half * wide, 6 * count * length * LANES + 8 * half * half, share),
        name="line_slopes",
    )(me, *tables, *received, *other)
    return [out[g * n : (g + 1) * n] for g in range(len(groups))]


def depth_terms(flow, tables):
    fields, _, rows, depth = flow.shape
    half = depth // 2
    step = math.gcd(rows, 48)

    def kernel(flow_ref, high_ref, low_ref, base_ref, slope_ref):
        value = flow_ref[:, 0].reshape(fields * step, depth)
        parts = []
        for part, x in enumerate((value[:, :half] + value[:, half:], value[:, :half] - value[:, half:])):
            h, l = two_terms(x)
            parts.append(dot(h, high_ref[part]) + (dot(l, high_ref[part]) + dot(h, low_ref[part])))
        minus = jnp.concatenate([parts[0] + parts[1], parts[0] - parts[1]], axis=1)
        rows_of = lambda f: minus[f * step : (f + 1) * step]
        speed = flow_ref[2, 0]
        for i in range(3):
            term = speed * rows_of(i)
            if i == 2:
                term = term + rows_of(3)
                slope_ref[...] = -rows_of(2)
            base_ref[i] = flow_ref[i, 0] + 0.1 * term

    whole = pl.BlockSpec((2, half, half), lambda r: (0, 0, 0), pipeline_mode=pl.Buffered(1))
    size = 4 * fields * rows * depth
    return pl.pallas_call(
        kernel, grid=(rows // step,),
        out_shape=[jax.ShapeDtypeStruct((3, rows, depth), F32), jax.ShapeDtypeStruct((rows, depth), F32)],
        in_specs=[pl.BlockSpec((fields, 1, step, depth), lambda r: (0, 0, r, 0)), whole, whole],
        out_specs=[pl.BlockSpec((3, step, depth), lambda r: (0, r, 0)), pl.BlockSpec((step, depth), lambda r: (r, 0))],
        compiler_params=params(), cost_estimate=cost(12 * fields * rows * half * half, 2 * size + 8 * half * half),
        name="depth_terms",
    )(flow, *tables)


def slab_terms(coefficients, planes):
    n, fields, rows, width = planes.shape
    step = math.gcd(rows, 48)

    def kernel(in_ref, out_ref, slope_ref):
        for i in range(n):
            for f in range(fields):
                slope = sum(float(coefficients[i, j]) * in_ref[j, f] for j in range(n))
                if f == 0:
                    slope_ref[i] = slope
                if f < 3:
                    out_ref[i, f] = in_ref[i, 0] * slope
                else:
                    out_ref[i, 0] += slope

    size = 4 * n * fields * rows * width
    block = lambda *lead: pl.BlockSpec((*lead, step, width), lambda r: (0,) * len(lead) + (r, 0))
    return pl.pallas_call(
        kernel, grid=(rows // step,),
        out_shape=[jax.ShapeDtypeStruct((n, 3, rows, width), F32), jax.ShapeDtypeStruct((n, rows, width), F32)],
        in_specs=[block(n, fields)], out_specs=[block(n, 3), block(n)],
        compiler_params=params(), cost_estimate=cost(n * size, 2 * size), name="slab_terms",
    )(planes)


def marker_order(cells, weights, rows, depth):
    markers, stencil = weights.shape
    tiles, entries = depth // LANES, markers * stencil
    chunks = entries // CHUNK
    marker = lax.iota(jnp.int32, entries) // stencil
    flat = cells.reshape(-1)
    row, z = flat // depth, flat % depth
    place = (z // LANES * rows + row) * LANES + z % LANES
    weight = weights.reshape(-1)
    if rows * depth * markers < 2**31:
        key, weight = lax.sort((place * markers + marker, weight), num_keys=1)
        place, marker = key // markers, key % markers
    else:
        place, marker, weight = lax.sort((place, marker, weight), num_keys=1)
    shape = (chunks, 1, CHUNK)
    tile_row, lane = place // LANES, place % LANES
    tile = (tile_row // rows).reshape(chunks, CHUNK)
    first, last = tile[:, 0], tile[:, -1]
    end = jnp.cumsum(last - first + 1)
    start = end - (last - first + 1)
    pairs = chunks + tiles
    index = lax.iota(jnp.int32, pairs)
    chunk = jnp.minimum(jnp.sum((end[None, :] <= index[:, None]).astype(jnp.int32), axis=1), chunks - 1)
    pick = chunk[:, None] == lax.iota(jnp.int32, chunks)[None, :]
    at = jnp.sum(jnp.where(pick, (first - start)[None, :], 0), axis=1) + index
    at = jnp.where(index < end[-1], at, tiles)
    return chunk, at, tile_row.reshape(shape), lane.reshape(shape), marker.reshape(shape), weight.reshape(shape)


def home_slopes(plan, slot, groups):
    n, tiles = plan.chips, plan.tiles
    low, high = slot * tiles // n, ((slot + 1) * tiles - 1) // n
    wanted, buffers = [], []
    for group, blocks in groups:
        if any(low <= r <= high for r in group):
            wanted += [(len(buffers) + s, k, r, s) for k, r in enumerate(group) if low <= r <= high for s in range(n)]
            buffers += blocks

    def copies(me, refs, slopes, sems, first):
        return [(r, pltpu.make_async_copy(
            refs[b].at[k], slopes.at[(r - low) * n + plan.source(me // CORES, s)], sems.at[first + i]))
            for i, (b, k, r, s) in enumerate(wanted)]

    skip = slot * tiles - low * n
    spans = [(r, max(0, (r - low) * n - skip), min(tiles, (r - low + 1) * n - skip)) for r in range(low, high + 1)]
    return buffers, (high - low + 1) * n, len(wanted), skip, copies, spans


def home_divergence(plan, parts, me, slope_z, groups):
    rows, depth, tiles = plan.rows, plan.depth, plan.tiles
    buffers, span, count, skip, copies_of, _ = home_slopes(plan, FIELD_ORDER.index(1), groups)

    def kernel(me_ref, slope_ref, *rest):
        refs, (out_ref, slopes, third, sems) = rest[: len(buffers)], rest[len(buffers) :]
        copies = [c for _, c in copies_of(me_ref[0], refs, slopes, sems, 1)]
        run_copies([pltpu.make_async_copy(slope_ref, third, sems.at[0])] + copies)
        for t in range(tiles):
            z = slice(t * LANES, (t + 1) * LANES)
            third[:, z] = third[:, z] + slopes[skip + t]
        width = depth // parts
        for g in range(parts):
            out_ref[g] = third[:, g * width : (g + 1) * width]

    return pl.pallas_call(
        kernel, out_shape=jax.ShapeDtypeStruct((parts, rows, depth // parts), F32),
        in_specs=[SMEM] + [HBM] * (1 + len(buffers)), out_specs=VMEM,
        scratch_shapes=[pltpu.VMEM((span, rows, LANES), F32), pltpu.VMEM((rows, depth), F32),
                        pltpu.SemaphoreType.DMA((1 + count,))],
        compiler_params=params(), cost_estimate=cost(0, 12 * rows * depth), name="home_divergence",
    )(me, slope_z, *buffers)


def home_step(plan, component, me, flow, base, groups, order, solid, out, share=0.01):
    rows, depth, tiles = plan.rows, plan.depth, plan.tiles
    wanted = (1, 3) if component == 1 else (component,)
    sources = [home_slopes(plan, FIELD_ORDER.index(f), groups) for f in wanted]
    buffers = [b for source in sources for b in source[0]]
    total = len(buffers)
    chunk_of, tile_of, *entries = order
    pairs = chunk_of.shape[0]
    chunks = entries[0].shape[0]
    marker_rows = plan.marker_rows
    assert rows <= 256

    spans = sources[0][5]

    def kernel(me_ref, chunk_ref, tile_ref, flow_ref, base_ref, *rest):
        early, bufs, rest = rest[:5], rest[5 : 5 + total], rest[5 + total :]
        if out is not None:
            rest = rest[1:]
        out_ref, speed, value, prov, terms, found, row_ref, lane_ref, marker_ref, weight_ref, solid_ref, sems, *slopes = rest
        first = {span[0]: [] for span in spans}
        for r, start, end in spans:
            z = pl.ds(start * LANES, (end - start) * LANES)
            for src, dst in ((flow_ref.at[1, 0], speed), (base_ref.at[component], value)):
                at = sum(len(cs) for cs in first.values())
                first[r].append(pltpu.make_async_copy(src.at[:, z], dst.at[:, z], sems.at[at]))
        at, used = 2 * len(spans), 0
        for source, ref in zip(sources, slopes):
            for r, c in source[4](me_ref[0], bufs[used : used + len(source[0])], ref, sems, at):
                first[r if source is sources[0] else spans[0][0]].append(c)
            at += source[2]
            used += len(source[0])
        later = [pltpu.make_async_copy(src, dst, sems.at[at + i]) for i, (src, dst) in enumerate(zip(
            early, (row_ref, lane_ref, marker_ref, weight_ref, solid_ref)))]
        for c in [c for cs in first.values() for c in cs] + later:
            c.start()
        for r, start, end in spans:
            for c in first[r]:
                c.wait()
            for t in range(start, end):
                z = slice(t * LANES, (t + 1) * LANES)
                term = speed[:, z] * slopes[0][sources[0][3] + t]
                if component == 1:
                    term = term + slopes[1][sources[1][3] + t]
                result = value[:, z] - 0.1 * term
                prov[t] = result
                h, l = two_terms(result)
                terms[t, :, :LANES] = h
                terms[t, :, LANES:] = l
        for c in later:
            c.wait()

        row_at = lax.broadcasted_iota(jnp.int32, (rows, CHUNK), 0)
        marker_at = lax.broadcasted_iota(jnp.int32, (marker_rows, CHUNK), 0)
        row_key = row_at.astype(BF)
        lane_key = lax.broadcasted_iota(jnp.int32, (LANES, CHUNK), 0).astype(BF)
        one, zero = jnp.ones((), BF), jnp.zeros((), BF)

        def key(value):
            return value.astype(F32).astype(BF)

        def pair(i):
            c, t = chunk_ref[i], tile_ref[i]
            return c, jnp.minimum(t, tiles - 1), row_ref[c] - t * rows, lane_key == key(lane_ref[c])

        found[...] = jnp.zeros_like(found)

        def gather(i, carry):
            c, t, row, lanes_hit = pair(i)
            lanes = jnp.where(lanes_hit, one, zero)
            both = dot(terms[t], jnp.concatenate([lanes, lanes], axis=0))
            found[c] += jnp.sum(jnp.where(row_at == row, both, 0.0), axis=0, keepdims=True)
            return carry

        lax.fori_loop(0, pairs, gather, 0, unroll=UNROLL)

        def add_up(c, total):
            m = marker_ref[c]
            share = jnp.where(marker_at == m // LANES, found[c] * weight_ref[c], 0.0)
            low_part = jnp.where(lane_key == key(m % LANES), one, zero)
            return total + dot_t(jnp.concatenate(two_terms(share), axis=0), low_part)

        sampled = lax.fori_loop(0, chunks, add_up, jnp.zeros((2 * marker_rows, LANES), F32), unroll=16)
        sampled = jnp.concatenate(two_terms(sampled[:marker_rows] + sampled[marker_rows:]), axis=0)

        def spread(c, carry):
            m = marker_ref[c]
            both = dot(sampled, jnp.where(lane_key == key(m % LANES), one, zero))
            both = jnp.where(marker_at == m // LANES, both[:marker_rows] + both[marker_rows:], 0.0)
            found[c] = jnp.sum(both, axis=0, keepdims=True) * weight_ref[c]
            return carry

        lax.fori_loop(0, chunks, spread, 0, unroll=16)

        def scatter(i, carry):
            c, t, row, lanes_hit = pair(i)
            value = [jnp.where(lanes_hit, x, zero) for x in two_terms(found[c])]
            both = dot_t(jnp.where(row_key == key(row), one, zero), jnp.concatenate(value, axis=0))
            prov[t] -= both[:, :LANES] + both[:, LANES:]
            return carry

        lax.fori_loop(0, pairs, scatter, 0, unroll=UNROLL)
        fluid = 1.0 - solid_ref[...].astype(F32)
        last = []
        for i, (_, start, end) in enumerate(spans):
            for t in range(start, end):
                b = t * LANES // (depth // solid.shape[1])
                value[:, t * LANES : (t + 1) * LANES] = fluid[:, b : b + 1] * prov[t]
            z = pl.ds(start * LANES, (end - start) * LANES)
            last.append(pltpu.make_async_copy(value.at[:, z], out_ref.at[component, 0, :, z], sems.at[i]))
            last[-1].start()
        for c in last:
            c.wait()

    operands = [me, chunk_of, tile_of, flow, base, *entries, solid, *buffers]
    specs = [SMEM] * 3 + [HBM] * (2 + len(entries) + 1 + total)
    aliases = {}
    if out is not None:
        aliases = {len(operands): 0}
        operands.append(out)
        specs.append(HBM)
    block = pltpu.VMEM((rows, depth), F32)
    return pl.pallas_call(
        kernel, out_shape=jax.ShapeDtypeStruct((3, 1, rows, depth), F32), in_specs=specs, out_specs=HBM,
        input_output_aliases=aliases,
        scratch_shapes=[
            block, block, pltpu.VMEM((tiles, rows, LANES), F32), pltpu.VMEM((tiles, rows, 2 * LANES), BF),
            pltpu.VMEM((chunks, 1, CHUNK), F32),
            *[pltpu.VMEM(x.shape, x.dtype) for x in (*entries, solid)],
            pltpu.SemaphoreType.DMA((2 * len(spans) + sum(source[2] for source in sources) + 5,)),
            *[pltpu.VMEM((source[1], rows, LANES), F32) for source in sources],
        ],
        compiler_params=params(),
        cost_estimate=cost(pairs * 16 * rows * CHUNK * LANES, 20 * rows * depth, share), name="home_step",
    )(*operands)


def body(flow, marker_cells, marker_weights, solid_blocks, *, pens, grps):
    _, planes, rows, depth = flow.shape
    assert planes == 1 and depth % LANES == 0 and rows % 8 == 0
    width = depth // grps
    plan = Plan(pens, rows, depth)
    plan.marker_rows = -(-marker_weights.shape[2] // LANES // 8) * 8
    pen_at = jnp.full((1,), lax.axis_index("pen"), jnp.int32)
    tables = [jnp.asarray(t) for t in split_table(pens * rows)]
    tables_z = tables if depth == pens * rows else [jnp.asarray(t) for t in split_table(depth)]

    def after(value, *others):
        return lax.optimization_barrier((value, others))[0]

    chips = plan.chips
    shifts = [2, 1, 3] if chips == 4 else list(range(1, chips))

    def send_lines(blocks):
        got = {0: blocks[0]}
        for s in shifts:
            got[s] = lax.ppermute(blocks[s], "pen", [(i, plan.to(i // CORES, s) * CORES + i % CORES) for i in range(pens)])
        return [got[s] for s in range(chips)]

    def other(value):
        return lax.ppermute(value, "pen", [(i, i ^ 1) for i in range(pens)])

    def swap(blocks):
        joined = other(jnp.concatenate(blocks[1:], axis=0))
        return [other(blocks[0])] + jnp.split(joined, chips - 1, axis=0)

    def cut_depth(value):
        return jnp.moveaxis(value.reshape(*value.shape[:-1], grps, width), -2, 0)

    def exchange(value):
        return lax.all_to_all(value, "grp", 0, 0, tiled=True)

    def slopes_of(rounds, cut, lines, swapped, share=0.01):
        return line_slopes(plan, rounds, cut, pen_at, lines, swapped, tables, share)

    first, second = plan.stages
    middle = -(-len(second) // 2)
    cut = [second[:middle], second[middle:]] if len(second) > 1 else [second]
    def together(values):
        turn = lambda v, back: [v[0]] + [v[1 + (shifts.index(s) if back else shifts[s - 1] - 1)] for s in range(1, chips)]
        is_lines = lambda v: isinstance(v, list) and len(v) == chips and all(hasattr(x, "shape") for x in v)
        turned = [turn(v, False) if is_lines(v) else v for v in values]
        out = lax.optimization_barrier(tuple(turned))
        return [turn(o, True) if is_lines(v) else o for v, o in zip(values, out)]

    heavy, everything = shifts[0], list(range(chips))
    light = [s for s in everything if s != heavy]
    (packed_heavy,) = pack_lines(plan, first, pen_at, flow, [heavy])
    packed = list(pack_lines(plan, first, pen_at, after(flow, packed_heavy), light))
    packed.insert(heavy, packed_heavy)
    lines = send_lines(packed)
    lines_x = exchange(cut_depth(after(flow, packed)[:, 0]))
    order = marker_order(*after((marker_cells[0, 0], marker_weights[0, 0]), packed), rows, depth)
    packed = pack_lines(plan, second, pen_at, after(flow, order), everything)
    lines, order, packed = together((lines, order, packed))
    lines_2 = send_lines(packed)
    (slopes,) = slopes_of(first, [first], lines, swap(lines))
    own = other(after(packed[0], slopes))
    terms_x, slopes_x = slab_terms(compact_matrix(grps), after(lines_x, slopes))
    across = exchange(terms_x)
    lines_2, slopes, slopes_x, own = together((lines_2, slopes, slopes_x, own))
    back = send_lines(slopes)
    slopes = slopes_of(second, cut, lines_2, [own] + [other(x) for x in lines_2[1:]], 6.5)
    base, slope_z = depth_terms(after(flow, slopes), tables_z)
    base = base - 0.1 * jnp.moveaxis(after(across, base), 0, 2).reshape(3, rows, depth)
    back, slopes, base, slope_z = together((back, slopes, base, slope_z))
    groups = [(first, back)]
    step = functools.partial(home_step, plan, me=pen_at, flow=flow, base=base, order=order, solid=solid_blocks[0])
    back = send_lines(slopes[0])
    out = step(1, groups=groups, out=None)
    back, slopes, out = together((back, slopes, out))
    groups = groups + [(cut[0], back)]
    if len(cut) > 1:
        back = send_lines(slopes[1])
    out = step(0, groups=groups, out=out)
    divergence = home_divergence(plan, grps, pen_at, after(slope_z, out), groups)
    poisson = exchange(divergence)
    if len(cut) > 1:
        back, out = together((back, out))
        groups = groups + [(cut[1], back)]
    out = step(2, groups=groups, out=out, share=10.0)
    return out, poisson + slopes_x


def solution(mesh):
    return jax.shard_map(
        functools.partial(body, pens=mesh.shape["pen"], grps=mesh.shape["grp"]),
        mesh=mesh,
        in_specs=(
            P(None, "grp", "pen", None),
            P("grp", "pen", None, None),
            P("grp", "pen", None, None),
            P("grp", "pen", None),
        ),
        out_specs=(P(None, "grp", "pen", None), P(None, "pen", "grp")),
        check_vma=False,
    )
```

```python
import functools
import math

import jax
import jax.numpy as jnp
import ml_dtypes
import numpy as np
from jax import lax
from jax.experimental import pallas as pl
from jax.experimental.pallas import tpu as pltpu
from jax.sharding import PartitionSpec as P

LANES = 128
CHUNK = 256
CORES = 2
UNROLL = 44
FIELD_ORDER = (1, 3, 0, 2)
ANY = pl.BlockSpec(memory_space=pl.ANY)
HBM = pl.BlockSpec(memory_space=pltpu.HBM)
SMEM = pl.BlockSpec(memory_space=pltpu.SMEM)
VMEM = pl.BlockSpec(memory_space=pltpu.VMEM)
BF = jnp.bfloat16
F32 = jnp.float32


def split_table(length):
    half = length // 2
    lag = np.arange(length)
    row = np.zeros(length)
    row[1:] = math.pi / length * (1 - 2 * (lag[1:] % 2)) / np.tan(math.pi * lag[1:] / length)
    row[half] = 0.0
    offset = np.arange(half)[:, None] - np.arange(half)[None, :]
    same, other = row[offset % length], row[(offset + half) % length]
    table = np.stack([(same + other) / 2, (same - other) / 2])
    high = table.astype(ml_dtypes.bfloat16)
    low = (table - high.astype(np.float64)).astype(ml_dtypes.bfloat16)
    return high, low


def compact_matrix(length):
    eye = np.eye(length)
    off = lambda k: np.eye(length, k=k)
    left = eye + (off(1) + off(-1)) / 3
    right = 7 / 9 * (off(1) - off(-1)) + 1 / 36 * (off(2) - off(-2))
    return np.linalg.solve(left, right).astype(np.float32)


def two_terms(value):
    high = value.astype(BF)
    return high, (value - high.astype(F32)).astype(BF)


def dot(a, b):
    return jnp.dot(a, b, preferred_element_type=F32)


def dot_t(a, b):
    return lax.dot_general(a, b, (((1,), (1,)), ((), ())), preferred_element_type=F32)


def params():
    return pltpu.CompilerParams(vmem_limit_bytes=60 * 2**20)


def cost(flops, moved, share=0.01):
    return pl.CostEstimate(flops=int(flops * share), bytes_accessed=int(moved * share), transcendentals=0)


class Plan:
    def __init__(self, pens, rows, depth):
        self.pens, self.chips, self.rows, self.depth = pens, pens // CORES, rows, depth
        self.tiles = depth // LANES
        self.pairs = len(FIELD_ORDER) * self.tiles
        self.rounds = -(-self.pairs // self.chips)
        first = min(-(-2 * self.tiles // self.chips), self.rounds)
        self.stages = [list(range(first))]
        if first < self.rounds:
            self.stages.append(list(range(first, self.rounds)))
        self.paired = self.chips & (self.chips - 1) == 0

    def to(self, chip, s):
        return chip ^ s if self.paired else (chip + s) % self.chips

    def source(self, chip, s):
        return chip ^ s if self.paired else (chip + self.chips - s) % self.chips


def run_copies(copies):
    for c in copies:
        c.start()
    for c in copies:
        c.wait()


def pack_lines(plan, rounds, me, flow, messages):
    n, rows, tiles = plan.chips, plan.rows, plan.tiles
    start, end = rounds[0] * n, min((rounds[-1] + 1) * n, plan.pairs)

    def kernel(me_ref, flow_ref, *rest):
        outs, (held, in_sems, out_sems) = rest[:-3], rest[-3:]
        chip = me_ref[0] // CORES
        copies = []
        if len(messages) == 1:
            loads = []
            for k, r in enumerate(rounds):
                pair = jnp.minimum(r * n + plan.to(chip, messages[0]), plan.pairs - 1)
                slot, z = pair // tiles, pl.multiple_of(pair % tiles * LANES, LANES)
                field = jnp.int32(FIELD_ORDER[0])
                for i, f in enumerate(FIELD_ORDER[1:], 1):
                    field = jnp.where(slot == i, f, field)
                loads.append(pltpu.make_async_copy(flow_ref.at[field, 0, :, pl.ds(z, LANES)], held.at[k], in_sems.at[k]))
                copies.append(pltpu.make_async_copy(held.at[k], outs[0].at[k], out_sems.at[k]))
            for c in loads:
                c.start()
            for load, store in zip(loads, copies):
                load.wait()
                store.start()
        else:
            loads = [pltpu.make_async_copy(
                flow_ref.at[FIELD_ORDER[q // tiles], 0, :, pl.ds(q % tiles * LANES, LANES)], held.at[q - start],
                in_sems.at[q - start]) for q in range(start, end)]
            for c in loads:
                c.start()
            for k in range(len(rounds)):
                for c in loads[k * n : (k + 1) * n]:
                    c.wait()
                for i, s in enumerate(messages):
                    pair = jnp.minimum(k * n + plan.to(chip, s), end - start - 1)
                    copies.append(pltpu.make_async_copy(held.at[pair], outs[i].at[k], out_sems.at[len(copies)]))
                    copies[-1].start()
        for c in copies:
            c.wait()

    shape = jax.ShapeDtypeStruct((len(rounds), rows, LANES), F32)
    return pl.pallas_call(
        kernel, out_shape=[shape] * len(messages), in_specs=[SMEM, HBM], out_specs=[HBM] * len(messages),
        scratch_shapes=[pltpu.VMEM((end - start, rows, LANES), F32), pltpu.SemaphoreType.DMA((end - start,)),
                        pltpu.SemaphoreType.DMA((len(messages) * len(rounds),))],
        compiler_params=params(), cost_estimate=cost(0, 2 * flow.size), name="pack_lines",
    )(me, flow)


def line_slopes(plan, rounds, groups, me, received, other, tables, share=0.01):
    n, rows = plan.chips, plan.rows
    length, half, count = plan.pens * rows, plan.pens * rows // 2, len(rounds)
    wide = count * LANES
    block = math.gcd(half, 256)

    def kernel(me_ref, high_ref, low_ref, *rest):
        ins, others = rest[:n], rest[n : 2 * n]
        outs = rest[2 * n : 2 * n + n * len(groups)]
        lines, result, x_high, x_low, in_sems, out_sems = rest[2 * n + n * len(groups) :]
        chip, core = me_ref[0] // CORES, me_ref[0] % CORES
        copies = []
        for refs, c in ((ins, core), (others, 1 - core)):
            for s in range(n):
                pen = plan.source(chip, s) * CORES + c
                at = pl.ds(pl.multiple_of(pen * rows, 8), rows)
                copies.append(pltpu.make_async_copy(refs[s], lines.at[:, at, :], in_sems.at[len(copies)]))
        run_copies(copies)

        @pl.loop(0, half // block)
        def _(b):
            upper = pl.ds(pl.multiple_of(b * block, block), block)
            lower = pl.ds(pl.multiple_of(b * block + half, block), block)
            for k in range(count):
                to = pl.ds(k * LANES, LANES)
                first, second = lines[k, upper, :], lines[k, lower, :]
                for part, value in enumerate((first + second, first - second)):
                    h, l = two_terms(value)
                    x_high[part, upper, to] = h
                    x_low[part, upper, to] = l

        for home in range(n // 2):
            at = pl.ds(pl.multiple_of((home * CORES + core) * rows, 16), rows)
            parts = []
            for part in range(2):
                t_high, t_low = high_ref[part, at, :], low_ref[part, at, :]
                h, l = x_high[part], x_low[part]
                parts.append(dot(t_high, h) + (dot(t_high, l) + dot(t_low, h)))
            top, bottom = parts[0] + parts[1], parts[0] - parts[1]
            for k in range(count):
                result[home, k] = top[:, k * LANES : (k + 1) * LANES]
                result[home + n // 2, k] = bottom[:, k * LANES : (k + 1) * LANES]

        copies = []
        for g, group in enumerate(groups):
            at_k = pl.ds(rounds.index(group[0]), len(group))
            for s in range(n):
                home = plan.to(chip, s)
                copies.append(pltpu.make_async_copy(result.at[home, at_k], outs[g * n + s], out_sems.at[len(copies)]))
        run_copies(copies)

    shapes = [jax.ShapeDtypeStruct((len(g), rows, LANES), F32) for g in groups for _ in range(n)]
    out = pl.pallas_call(
        kernel, out_shape=shapes,
        in_specs=[SMEM, VMEM, VMEM] + [HBM] * (2 * n), out_specs=[ANY] * len(shapes),
        scratch_shapes=[
            pltpu.VMEM((count, length, LANES), F32), pltpu.VMEM((n, count, rows, LANES), F32),
            pltpu.VMEM((2, half, wide), BF), pltpu.VMEM((2, half, wide), BF),
            pltpu.SemaphoreType.DMA((2 * n,)), pltpu.SemaphoreType.DMA((len(shapes),)),
        ],
        compiler_params=params(),
        cost_estimate=cost(6 * half * half * wide, 6 * count * length * LANES + 8 * half * half, share),
        name="line_slopes",
    )(me, *tables, *received, *other)
    return [out[g * n : (g + 1) * n] for g in range(len(groups))]


def depth_terms(flow, tables):
    fields, _, rows, depth = flow.shape
    half = depth // 2
    step = math.gcd(rows, 48)

    def kernel(flow_ref, high_ref, low_ref, base_ref, slope_ref):
        value = flow_ref[:, 0].reshape(fields * step, depth)
        parts = []
        for part, x in enumerate((value[:, :half] + value[:, half:], value[:, :half] - value[:, half:])):
            h, l = two_terms(x)
            parts.append(dot(h, high_ref[part]) + (dot(l, high_ref[part]) + dot(h, low_ref[part])))
        minus = jnp.concatenate([parts[0] + parts[1], parts[0] - parts[1]], axis=1)
        rows_of = lambda f: minus[f * step : (f + 1) * step]
        speed = flow_ref[2, 0]
        for i in range(3):
            term = speed * rows_of(i)
            if i == 2:
                term = term + rows_of(3)
                slope_ref[...] = -rows_of(2)
            base_ref[i] = flow_ref[i, 0] + 0.1 * term

    whole = pl.BlockSpec((2, half, half), lambda r: (0, 0, 0), pipeline_mode=pl.Buffered(1))
    size = 4 * fields * rows * depth
    return pl.pallas_call(
        kernel, grid=(rows // step,),
        out_shape=[jax.ShapeDtypeStruct((3, rows, depth), F32), jax.ShapeDtypeStruct((rows, depth), F32)],
        in_specs=[pl.BlockSpec((fields, 1, step, depth), lambda r: (0, 0, r, 0)), whole, whole],
        out_specs=[pl.BlockSpec((3, step, depth), lambda r: (0, r, 0)), pl.BlockSpec((step, depth), lambda r: (r, 0))],
        compiler_params=params(), cost_estimate=cost(12 * fields * rows * half * half, 2 * size + 8 * half * half),
        name="depth_terms",
    )(flow, *tables)


def slab_terms(coefficients, planes):
    n, fields, rows, width = planes.shape
    step = math.gcd(rows, 48)

    def kernel(in_ref, out_ref, slope_ref):
        for i in range(n):
            for f in range(fields):
                slope = sum(float(coefficients[i, j]) * in_ref[j, f] for j in range(n))
                if f == 0:
                    slope_ref[i] = slope
                if f < 3:
                    out_ref[i, f] = in_ref[i, 0] * slope
                else:
                    out_ref[i, 0] += slope

    size = 4 * n * fields * rows * width
    block = lambda *lead: pl.BlockSpec((*lead, step, width), lambda r: (0,) * len(lead) + (r, 0))
    return pl.pallas_call(
        kernel, grid=(rows // step,),
        out_shape=[jax.ShapeDtypeStruct((n, 3, rows, width), F32), jax.ShapeDtypeStruct((n, rows, width), F32)],
        in_specs=[block(n, fields)], out_specs=[block(n, 3), block(n)],
        compiler_params=params(), cost_estimate=cost(n * size, 2 * size), name="slab_terms",
    )(planes)


def marker_order(cells, weights, rows, depth):
    markers, stencil = weights.shape
    tiles, entries = depth // LANES, markers * stencil
    chunks = entries // CHUNK
    marker = lax.iota(jnp.int32, entries) // stencil
    flat = cells.reshape(-1)
    row, z = flat // depth, flat % depth
    place = (z // LANES * rows + row) * LANES + z % LANES
    weight = weights.reshape(-1)
    if rows * depth * markers < 2**31:
        key, weight = lax.sort((place * markers + marker, weight), num_keys=1)
        place, marker = key // markers, key % markers
    else:
        place, marker, weight = lax.sort((place, marker, weight), num_keys=1)
    shape = (chunks, 1, CHUNK)
    tile_row, lane = place // LANES, place % LANES
    tile = (tile_row // rows).reshape(chunks, CHUNK)
    first, last = tile[:, 0], tile[:, -1]
    end = jnp.cumsum(last - first + 1)
    start = end - (last - first + 1)
    pairs = chunks + tiles
    index = lax.iota(jnp.int32, pairs)
    chunk = jnp.minimum(jnp.sum((end[None, :] <= index[:, None]).astype(jnp.int32), axis=1), chunks - 1)
    pick = chunk[:, None] == lax.iota(jnp.int32, chunks)[None, :]
    at = jnp.sum(jnp.where(pick, (first - start)[None, :], 0), axis=1) + index
    at = jnp.where(index < end[-1], at, tiles)
    return chunk, at, tile_row.reshape(shape), lane.reshape(shape), marker.reshape(shape), weight.reshape(shape)


def home_slopes(plan, slot, groups):
    n, tiles = plan.chips, plan.tiles
    low, high = slot * tiles // n, ((slot + 1) * tiles - 1) // n
    wanted, buffers = [], []
    for group, blocks in groups:
        if any(low <= r <= high for r in group):
            wanted += [(len(buffers) + s, k, r, s) for k, r in enumerate(group) if low <= r <= high for s in range(n)]
            buffers += blocks

    def copies(me, refs, slopes, sems, first):
        return [(r, pltpu.make_async_copy(
            refs[b].at[k], slopes.at[(r - low) * n + plan.source(me // CORES, s)], sems.at[first + i]))
            for i, (b, k, r, s) in enumerate(wanted)]

    skip = slot * tiles - low * n
    spans = [(r, max(0, (r - low) * n - skip), min(tiles, (r - low + 1) * n - skip)) for r in range(low, high + 1)]
    return buffers, (high - low + 1) * n, len(wanted), skip, copies, spans


def home_divergence(plan, parts, me, slope_z, groups):
    rows, depth, tiles = plan.rows, plan.depth, plan.tiles
    buffers, span, count, skip, copies_of, _ = home_slopes(plan, FIELD_ORDER.index(1), groups)

    def kernel(me_ref, slope_ref, *rest):
        refs, (out_ref, slopes, third, sems) = rest[: len(buffers)], rest[len(buffers) :]
        copies = [c for _, c in copies_of(me_ref[0], refs, slopes, sems, 1)]
        run_copies([pltpu.make_async_copy(slope_ref, third, sems.at[0])] + copies)
        for t in range(tiles):
            z = slice(t * LANES, (t + 1) * LANES)
            third[:, z] = third[:, z] + slopes[skip + t]
        width = depth // parts
        for g in range(parts):
            out_ref[g] = third[:, g * width : (g + 1) * width]

    return pl.pallas_call(
        kernel, out_shape=jax.ShapeDtypeStruct((parts, rows, depth // parts), F32),
        in_specs=[SMEM] + [HBM] * (1 + len(buffers)), out_specs=VMEM,
        scratch_shapes=[pltpu.VMEM((span, rows, LANES), F32), pltpu.VMEM((rows, depth), F32),
                        pltpu.SemaphoreType.DMA((1 + count,))],
        compiler_params=params(), cost_estimate=cost(0, 12 * rows * depth), name="home_divergence",
    )(me, slope_z, *buffers)


def home_step(plan, component, me, flow, base, groups, order, solid, out, share=0.01):
    rows, depth, tiles = plan.rows, plan.depth, plan.tiles
    wanted = (1, 3) if component == 1 else (component,)
    sources = [home_slopes(plan, FIELD_ORDER.index(f), groups) for f in wanted]
    buffers = [b for source in sources for b in source[0]]
    total = len(buffers)
    chunk_of, tile_of, *entries = order
    pairs = chunk_of.shape[0]
    chunks = entries[0].shape[0]
    marker_rows = plan.marker_rows
    assert rows <= 256

    spans = sources[0][5]

    def kernel(me_ref, chunk_ref, tile_ref, flow_ref, base_ref, *rest):
        early, bufs, rest = rest[:5], rest[5 : 5 + total], rest[5 + total :]
        if out is not None:
            rest = rest[1:]
        out_ref, speed, value, prov, terms, found, row_ref, lane_ref, marker_ref, weight_ref, solid_ref, sems, *slopes = rest
        first = {span[0]: [] for span in spans}
        for r, start, end in spans:
            z = pl.ds(start * LANES, (end - start) * LANES)
            for src, dst in ((flow_ref.at[1, 0], speed), (base_ref.at[component], value)):
                at = sum(len(cs) for cs in first.values())
                first[r].append(pltpu.make_async_copy(src.at[:, z], dst.at[:, z], sems.at[at]))
        at, used = 2 * len(spans), 0
        for source, ref in zip(sources, slopes):
            for r, c in source[4](me_ref[0], bufs[used : used + len(source[0])], ref, sems, at):
                first[r if source is sources[0] else spans[0][0]].append(c)
            at += source[2]
            used += len(source[0])
        later = [pltpu.make_async_copy(src, dst, sems.at[at + i]) for i, (src, dst) in enumerate(zip(
            early, (row_ref, lane_ref, marker_ref, weight_ref, solid_ref)))]
        for c in [c for cs in first.values() for c in cs] + later:
            c.start()
        for r, start, end in spans:
            for c in first[r]:
                c.wait()
            for t in range(start, end):
                z = slice(t * LANES, (t + 1) * LANES)
                term = speed[:, z] * slopes[0][sources[0][3] + t]
                if component == 1:
                    term = term + slopes[1][sources[1][3] + t]
                result = value[:, z] - 0.1 * term
                prov[t] = result
                h, l = two_terms(result)
                terms[t, :, :LANES] = h
                terms[t, :, LANES:] = l
        for c in later:
            c.wait()

        row_at = lax.broadcasted_iota(jnp.int32, (rows, CHUNK), 0)
        marker_at = lax.broadcasted_iota(jnp.int32, (marker_rows, CHUNK), 0)
        row_key = row_at.astype(BF)
        lane_key = lax.broadcasted_iota(jnp.int32, (LANES, CHUNK), 0).astype(BF)
        one, zero = jnp.ones((), BF), jnp.zeros((), BF)

        def key(value):
            return value.astype(F32).astype(BF)

        def pair(i):
            c, t = chunk_ref[i], tile_ref[i]
            return c, jnp.minimum(t, tiles - 1), row_ref[c] - t * rows, lane_key == key(lane_ref[c])

        found[...] = jnp.zeros_like(found)

        def gather(i, carry):
            c, t, row, lanes_hit = pair(i)
            lanes = jnp.where(lanes_hit, one, zero)
            both = dot(terms[t], jnp.concatenate([lanes, lanes], axis=0))
            found[c] += jnp.sum(jnp.where(row_at == row, both, 0.0), axis=0, keepdims=True)
            return carry

        lax.fori_loop(0, pairs, gather, 0, unroll=UNROLL)

        def add_up(c, total):
            m = marker_ref[c]
            share = jnp.where(marker_at == m // LANES, found[c] * weight_ref[c], 0.0)
            low_part = jnp.where(lane_key == key(m % LANES), one, zero)
            return total + dot_t(jnp.concatenate(two_terms(share), axis=0), low_part)

        sampled = lax.fori_loop(0, chunks, add_up, jnp.zeros((2 * marker_rows, LANES), F32), unroll=16)
        sampled = jnp.concatenate(two_terms(sampled[:marker_rows] + sampled[marker_rows:]), axis=0)

        def spread(c, carry):
            m = marker_ref[c]
            both = dot(sampled, jnp.where(lane_key == key(m % LANES), one, zero))
            both = jnp.where(marker_at == m // LANES, both[:marker_rows] + both[marker_rows:], 0.0)
            found[c] = jnp.sum(both, axis=0, keepdims=True) * weight_ref[c]
            return carry

        lax.fori_loop(0, chunks, spread, 0, unroll=16)

        def scatter(i, carry):
            c, t, row, lanes_hit = pair(i)
            value = [jnp.where(lanes_hit, x, zero) for x in two_terms(found[c])]
            both = dot_t(jnp.where(row_key == key(row), one, zero), jnp.concatenate(value, axis=0))
            prov[t] -= both[:, :LANES] + both[:, LANES:]
            return carry

        lax.fori_loop(0, pairs, scatter, 0, unroll=UNROLL)
        fluid = 1.0 - solid_ref[...].astype(F32)
        last = []
        for i, (_, start, end) in enumerate(spans):
            for t in range(start, end):
                b = t * LANES // (depth // solid.shape[1])
                value[:, t * LANES : (t + 1) * LANES] = fluid[:, b : b + 1] * prov[t]
            z = pl.ds(start * LANES, (end - start) * LANES)
            last.append(pltpu.make_async_copy(value.at[:, z], out_ref.at[component, 0, :, z], sems.at[i]))
            last[-1].start()
        for c in last:
            c.wait()

    operands = [me, chunk_of, tile_of, flow, base, *entries, solid, *buffers]
    specs = [SMEM] * 3 + [HBM] * (2 + len(entries) + 1 + total)
    aliases = {}
    if out is not None:
        aliases = {len(operands): 0}
        operands.append(out)
        specs.append(HBM)
    block = pltpu.VMEM((rows, depth), F32)
    return pl.pallas_call(
        kernel, out_shape=jax.ShapeDtypeStruct((3, 1, rows, depth), F32), in_specs=specs, out_specs=HBM,
        input_output_aliases=aliases,
        scratch_shapes=[
            block, block, pltpu.VMEM((tiles, rows, LANES), F32), pltpu.VMEM((tiles, rows, 2 * LANES), BF),
            pltpu.VMEM((chunks, 1, CHUNK), F32),
            *[pltpu.VMEM(x.shape, x.dtype) for x in (*entries, solid)],
            pltpu.SemaphoreType.DMA((2 * len(spans) + sum(source[2] for source in sources) + 5,)),
            *[pltpu.VMEM((source[1], rows, LANES), F32) for source in sources],
        ],
        compiler_params=params(),
        cost_estimate=cost(pairs * 16 * rows * CHUNK * LANES, 20 * rows * depth, share), name="home_step",
    )(*operands)


def body(flow, marker_cells, marker_weights, solid_blocks, *, pens, grps):
    _, planes, rows, depth = flow.shape
    assert planes == 1 and depth % LANES == 0 and rows % 8 == 0
    width = depth // grps
    plan = Plan(pens, rows, depth)
    plan.marker_rows = -(-marker_weights.shape[2] // LANES // 8) * 8
    pen_at = jnp.full((1,), lax.axis_index("pen"), jnp.int32)
    tables = [jnp.asarray(t) for t in split_table(pens * rows)]
    tables_z = tables if depth == pens * rows else [jnp.asarray(t) for t in split_table(depth)]

    def after(value, *others):
        return lax.optimization_barrier((value, others))[0]

    chips = plan.chips
    shifts = [2, 3, 1] if chips == 4 else list(range(1, chips))

    def send_lines(blocks):
        got = {0: blocks[0]}
        for s in shifts:
            got[s] = lax.ppermute(blocks[s], "pen", [(i, plan.to(i // CORES, s) * CORES + i % CORES) for i in range(pens)])
        return [got[s] for s in range(chips)]

    def other(value):
        return lax.ppermute(value, "pen", [(i, i ^ 1) for i in range(pens)])

    def swap(blocks):
        joined = other(jnp.concatenate(blocks[1:], axis=0))
        return [other(blocks[0])] + jnp.split(joined, chips - 1, axis=0)

    def cut_depth(value):
        return jnp.moveaxis(value.reshape(*value.shape[:-1], grps, width), -2, 0)

    def exchange(value):
        return lax.all_to_all(value, "grp", 0, 0, tiled=True)

    def slopes_of(rounds, cut, lines, swapped, share=0.01):
        return line_slopes(plan, rounds, cut, pen_at, lines, swapped, tables, share)

    first, second = plan.stages
    middle = -(-len(second) // 2)
    cut = [second[:middle], second[middle:]] if len(second) > 1 else [second]
    def together(values):
        turn = lambda v, back: [v[0]] + [v[1 + (shifts.index(s) if back else shifts[s - 1] - 1)] for s in range(1, chips)]
        is_lines = lambda v: isinstance(v, list) and len(v) == chips and all(hasattr(x, "shape") for x in v)
        turned = [turn(v, False) if is_lines(v) else v for v in values]
        out = lax.optimization_barrier(tuple(turned))
        return [turn(o, True) if is_lines(v) else o for v, o in zip(values, out)]

    heavy, everything = shifts[0], list(range(chips))
    light = [s for s in everything if s != heavy]
    (packed_heavy,) = pack_lines(plan, first, pen_at, flow, [heavy])
    packed = list(pack_lines(plan, first, pen_at, after(flow, packed_heavy), light))
    packed.insert(heavy, packed_heavy)
    lines = send_lines(packed)
    lines_x = exchange(cut_depth(after(flow, packed)[:, 0]))
    order = marker_order(*after((marker_cells[0, 0], marker_weights[0, 0]), packed), rows, depth)
    packed = pack_lines(plan, second, pen_at, after(flow, order), everything)
    lines, order, packed = together((lines, order, packed))
    lines_2 = send_lines(packed)
    (slopes,) = slopes_of(first, [first], lines, swap(lines))
    own = other(after(packed[0], slopes))
    terms_x, slopes_x = slab_terms(compact_matrix(grps), after(lines_x, slopes))
    across = exchange(terms_x)
    lines_2, slopes, slopes_x, own = together((lines_2, slopes, slopes_x, own))
    back = send_lines(slopes)
    slopes = slopes_of(second, cut, lines_2, [own] + [other(x) for x in lines_2[1:]], 6.5)
    base, slope_z = depth_terms(after(flow, slopes), tables_z)
    base = base - 0.1 * jnp.moveaxis(after(across, base), 0, 2).reshape(3, rows, depth)
    back, slopes, base, slope_z = together((back, slopes, base, slope_z))
    groups = [(first, back)]
    step = functools.partial(home_step, plan, me=pen_at, flow=flow, base=base, order=order, solid=solid_blocks[0])
    back = send_lines(slopes[0])
    out = step(1, groups=groups, out=None)
    back, slopes, out = together((back, slopes, out))
    groups = groups + [(cut[0], back)]
    if len(cut) > 1:
        back = send_lines(slopes[1])
    out = step(0, groups=groups, out=out)
    divergence = home_divergence(plan, grps, pen_at, after(slope_z, out), groups)
    poisson = exchange(divergence)
    if len(cut) > 1:
        back, out = together((back, out))
        groups = groups + [(cut[1], back)]
    out = step(2, groups=groups, out=out, share=10.0)
    return out, poisson + slopes_x


def solution(mesh):
    return jax.shard_map(
        functools.partial(body, pens=mesh.shape["pen"], grps=mesh.shape["grp"]),
        mesh=mesh,
        in_specs=(
            P(None, "grp", "pen", None),
            P("grp", "pen", None, None),
            P("grp", "pen", None, None),
            P("grp", "pen", None),
        ),
        out_specs=(P(None, "grp", "pen", None), P(None, "pen", "grp")),
        check_vma=False,
    )
```
